32 devices in a mesh: dp: 4 (over y, core), row: 2 (over x), col: 4 (over z).
Axes of the slice: x: 2, y: 2, z: 4, core: 2. Of those that a mesh axis runs over, the one named last changes fastest.
Arguments:
- tokens: bfloat16 [8192, 1536], P(('dp', 'row', 'col')), may hold values from -6 to 6
- cotangent: bfloat16 [8192, 1536], P(('dp', 'row', 'col')), may hold values from -6 to 6
- seq_lengths: int32 [8, 4], P('dp'), may hold values from 1 to 682, 1024 in all within a row
- token_order: int32 [8192], replicated, may hold values from 0 to 8191, as said below
- norm_in: bfloat16 [1536], replicated, may hold values from 0.5 to 1.5
- w_gate: bfloat16 [1536, 3072], P('dp', ('row', 'col')), may hold values from -0.15625 to 0.15625
- w_value: bfloat16 [1536, 3072], P('dp', ('row', 'col')), may hold values from -0.15625 to 0.15625
- w_pair: bfloat16 [1536, 256], P('dp', ('row', 'col')), may hold values from -0.15625 to 0.15625
- w_step: bfloat16 [1536, 48], P('dp', ('row', 'col')), may hold values from -0.15625 to 0.15625
- conv_value: float32 [4, 3072], P(None, ('row', 'col')), may hold values from -3 to 3
- bias_value: float32 [3072], P(('row', 'col')), may hold values from -3 to 3
- conv_pair: float32 [4, 256], P(None, ('row', 'col')), may hold values from -3 to 3
- bias_pair: float32 [256], P(('row', 'col')), may hold values from -3 to 3
- step_bias: float32 [48], P(('row', 'col')), may hold values from -4 to -1
- decay_log: float32 [48], P(('row', 'col')), may hold values from 0 to 2.5
- skip_gain: float32 [48], P(('row', 'col')), may hold values from 0.5 to 1.5
- norm_gate: float32 [3072], P(('row', 'col')), may hold values from 0.5 to 1.5
- w_out: bfloat16 [3072, 1536], P(('row', 'col'), 'dp'), may hold values from -0.109375 to 0.109375
Outputs:
- block_out: bfloat16 [8192, 1536], P(('dp', 'row', 'col'))
- grad_tokens: bfloat16 [8192, 1536], P(('dp', 'row', 'col'))
- grad_norm_in: float32 [1536], replicated
- grad_w_gate: float32 [1536, 3072], P('dp', ('row', 'col'))
- grad_w_value: float32 [1536, 3072], P('dp', ('row', 'col'))
- grad_w_pair: float32 [1536, 256], P('dp', ('row', 'col'))
- grad_w_step: float32 [1536, 48], P('dp', ('row', 'col'))
- grad_conv_value: float32 [4, 3072], P(None, ('row', 'col'))
- grad_bias_value: float32 [3072], P(('row', 'col'))
- grad_conv_pair: float32 [4, 256], P(None, ('row', 'col'))
- grad_bias_pair: float32 [256], P(('row', 'col'))
- grad_step_bias: float32 [48], P(('row', 'col'))
- grad_decay_log: float32 [48], P(('row', 'col'))
- grad_skip_gain: float32 [48], P(('row', 'col'))
- grad_norm_gate: float32 [3072], P(('row', 'col'))
- grad_w_out: float32 [3072, 1536], P(('row', 'col'), 'dp')
The draws below stay inside these ranges and needn't reach their ends.
Inputs may be any that keep to these rules, and one draw needn't show every extreme that they name: token_order is a permutation. Cut the natural positions into 32 blocks of 256 in order, block index g * 2 * 4 + r. Let the dealt set (g, r) be the dealt positions g * 2048 + b * 1024 + r * 128 + u, for b < 2 and u < 128. Every natural block (g, r) sends exactly 64 tokens into each dealt set (g2, r), for every g2. `seq_lengths`: row b holds micro-batch b of token group b // 2; each row sums to 1024, its largest entry is 682, and its last entry counts padding tokens.
All inputs are finite; a program needn't handle non-finite values.
Results may differ from the reference program's by a relative error of at most 0.018.
Values may be sent and summed in bfloat16 or wider, within the bound.
No kernel may reach another device: no remote copies, remote signals or barrier semaphores. Data moves between devices by JAX's collectives and lax.ppermute only.
A program may use at most 192 MiB of HBM per device.

```python
import math
import jax
import jax.numpy as jnp
import numpy as np
from jax import lax

D = 1536
HEADS = 48
INNER = 3072
STATE = 128
CONV = 4
SPAN = 256
MBT = 1024
MB = 2
SEQS = 4
SEQ_MOST = 682
TOK_DP = 2048
TOKENS = 8192
N_DP = 4
N_ROW = 2
N_COL = 4


def draw_token_order(key, part):
    key = jax.random.fold_in(key, 11)
    group_count = TOKENS // TOK_DP
    team_count = N_ROW * N_COL
    share_len = TOK_DP // team_count
    piece_len = MBT // team_count
    quota_len = share_len // group_count
    unit_count = group_count * team_count
    source_key, target_key = jax.random.split(key)
    source_perm = jax.vmap(lambda item: jax.random.permutation(item, share_len))(jax.random.split(source_key, unit_count))
    target_perm = jax.vmap(lambda item: jax.random.permutation(item, share_len))(jax.random.split(target_key, unit_count))
    places = jnp.arange(TOKENS, dtype=jnp.int32)
    unit = places // share_len
    within = places % share_len
    source = unit // team_count
    member = unit % team_count
    picked = source_perm[unit, within].astype(jnp.int32)
    target = picked // quota_len
    column = source * quota_len + picked % quota_len
    listed = target_perm[target * team_count + member, column].astype(jnp.int32)
    dealt_at = target * TOK_DP + listed // piece_len * MBT + member * piece_len + listed % piece_len
    return jnp.zeros((TOKENS,), jnp.int32).at[dealt_at].set(places)


def level_of(stream_key, extent, pieces, low, largest):
    level = 1.0
    for position, blocks in pieces:
        steps = jax.random.uniform(jax.random.fold_in(jax.random.fold_in(stream_key, 6), position), (blocks,), jnp.float32, low / len(pieces), largest / len(pieces))
        level = level * jnp.repeat(jnp.exp(steps), extent[position] // blocks).reshape((-1,) + (1,) * (len(extent) - 1 - position))
    return level


def length_profile(number_of, total, limit, lean):
    loads = [(1 << 20) // math.isqrt(rank ** lean) + 1 for rank in range(2, number_of + 1)]
    surplus, counts = total - limit - (number_of - 1), [1] * (number_of - 1)
    while surplus > 0:
        movable = [i for i in range(number_of - 1) if counts[i] < limit]
        pool, remaining = sum([loads[i] for i in movable]), surplus
        for i in movable:
            extra = min(limit - counts[i], max(1, remaining * loads[i] // pool), surplus)
            counts[i] = counts[i] + extra
            surplus = surplus - extra
    return np.array([limit] + counts)


def uneven_parts(key, number_of, total, bound, lean):
    if number_of == 2:
        one = jax.random.randint(key, (), max(1, total - bound), min(bound, total - 1) + 1)
        return jnp.stack([one, total - one])
    tallies = jnp.asarray(length_profile(number_of, total, bound, lean), jnp.int32)
    twos = (number_of - 1) // 2
    giver, taker = tallies[1:1 + 2 * twos:2], tallies[2:2 + 2 * twos:2]
    margin = jnp.minimum(giver - 1, bound - taker)
    moved = jax.random.randint(jax.random.fold_in(key, 1), (twos,), 0, 1 << 20) % (margin + 1)
    tallies = tallies.at[1:1 + 2 * twos:2].set(giver - moved).at[2:2 + 2 * twos:2].set(taker + moved)
    return tallies[jax.random.permutation(jax.random.fold_in(key, 2), number_of)]


def gaussian(own_key, shape, scale, bound, pieces=(), held_as=jnp.bfloat16):
    entries = jax.random.normal(own_key, shape, jnp.float32) * scale
    if len(pieces) > 0:
        entries = level_of(own_key, shape, pieces, -0.22, 0.18) * entries
    return jnp.clip(entries, min=-bound, max=bound).astype(held_as)


def setup_inputs(seed: int = 0) -> dict:
    key_list = jax.random.split(jax.random.key(seed), 19)
    tokens = gaussian(key_list[0], (TOKENS, D), 1.0, 6.0, ((0, 32),))
    cotangent = gaussian(key_list[1], (TOKENS, D), 1.0, 6.0, ((0, 32),))
    seq_lengths = jax.vmap(lambda own: uneven_parts(own, SEQS, MBT, SEQ_MOST, 2))(jax.random.split(key_list[2], (N_DP * MB))).reshape((N_DP * MB, SEQS)).astype(jnp.int32)
    token_order = draw_token_order(jax.random.fold_in(key_list[18], 71), 0)
    norm_in = jnp.clip(1.0 + 0.1 * jax.random.normal(key_list[4], (D,), jnp.float32), 0.5, 1.5).astype(jnp.bfloat16)
    w_gate = gaussian(key_list[5], (D, INNER), D ** -0.5, 0.15625, ((0, 4), (1, 8)))
    w_value = gaussian(key_list[6], (D, INNER), D ** -0.5, 0.15625, ((0, 4), (1, 8)))
    w_pair = gaussian(key_list[7], (D, 2 * STATE), D ** -0.5, 0.15625, ((0, 4), (1, 8)))
    w_step = gaussian(key_list[8], (D, HEADS), D ** -0.5, 0.15625, ((0, 4), (1, 8)))
    conv_value = gaussian(key_list[9], (CONV, INNER), CONV ** -0.5, 3.0, ((1, 8),), jnp.float32)
    bias_value = gaussian(key_list[10], (INNER,), 0.5, 3.0, ((0, 8),), jnp.float32)
    conv_pair = gaussian(key_list[11], (CONV, 2 * STATE), CONV ** -0.5, 3.0, ((1, 8),), jnp.float32)
    bias_pair = gaussian(key_list[12], (2 * STATE,), 0.5, 3.0, ((0, 8),), jnp.float32)
    step_bias = jnp.clip(-4.0 + 3.0 * jax.random.uniform(key_list[13], (HEADS,), jnp.float32) ** level_of(key_list[13], (HEADS,), ((0, 8),), -0.2, 0.2), -4.0, -1.0)
    decay_log = jnp.clip(2.5 * jax.random.uniform(key_list[14], (HEADS,), jnp.float32) ** level_of(key_list[14], (HEADS,), ((0, 8),), -0.2, 0.2), 0.0, 2.5)
    skip_gain = jnp.clip(0.5 + 1.0 * jax.random.uniform(key_list[15], (HEADS,), jnp.float32) ** level_of(key_list[15], (HEADS,), ((0, 8),), -0.2, 0.2), 0.5, 1.5)
    norm_gate = jnp.clip(1.0 + 0.1 * jax.random.normal(key_list[16], (INNER,), jnp.float32), 0.5, 1.5)
    w_out = gaussian(key_list[17], (INNER, D), INNER ** -0.5, 0.109375, ((0, 8), (1, 4)))
    return {"tokens": tokens, "cotangent": cotangent, "seq_lengths": seq_lengths, "token_order": token_order, "norm_in": norm_in, "w_gate": w_gate, "w_value": w_value, "w_pair": w_pair, "w_step": w_step, "conv_value": conv_value, "bias_value": bias_value, "conv_pair": conv_pair, "bias_pair": bias_pair, "step_bias": step_bias, "decay_log": decay_log, "skip_gain": skip_gain, "norm_gate": norm_gate, "w_out": w_out}


EPS = 1e-05
PRECISE = lax.Precision.HIGHEST

@jax.custom_vjp
def low(v):
    return lax.optimization_barrier(v.astype(jnp.bfloat16)).astype(jnp.float32)

@jax.custom_vjp
def low_back(v):
    return v

def low_keep(v):
    return (low(v), None)

def low_pass(kept, grad):
    return (grad,)

def back_keep(v):
    return (v, None)

def back_low(kept, grad):
    return (low(grad),)
low.defvjp(low_keep, low_pass)
low_back.defvjp(back_keep, back_low)

def segment_ids(lengths_row, count):
    bounds = jnp.cumsum(lengths_row).astype(jnp.int32)
    places = jnp.arange(count, dtype=jnp.int32)
    return lax.optimization_barrier(jnp.sum((places[:, None] >= bounds[None, :]).astype(jnp.int32), axis=1)).astype(jnp.int32)

def causal_conv(values, kernel, offset, segment):
    tap_count = kernel.shape[0]
    length = values.shape[0]
    padded = jnp.concatenate([jnp.zeros((tap_count - 1, values.shape[1]), jnp.float32), values], axis=0)
    seg_pad = jnp.concatenate([jnp.full((tap_count - 1,), -1, jnp.int32), segment.astype(jnp.int32)])
    result = jnp.zeros_like(values) + offset[None, :]
    for tap_index in range(tap_count):
        same_seg = (seg_pad[tap_index:tap_index + length] == segment).astype(jnp.float32)
        result = result + padded[tap_index:tap_index + length] * kernel[tap_index][None, :] * same_seg[:, None]
    return result

def conv_silu(values, kernel, offset, segment):
    return jax.nn.silu(causal_conv(values, kernel, offset, segment))

def softplus_shift(step_proj, step_bias):
    return jax.nn.softplus(step_proj + step_bias[None, :])

def ssd_scan(values, steps_in, decay_rates, keys_in, reads_in, segment, span_len):
    length, head_count, head_width = values.shape
    block_count = length // span_len
    blocks = (values.reshape(block_count, span_len, head_count, head_width), steps_in.reshape(block_count, span_len, head_count), keys_in.reshape(block_count, span_len, keys_in.shape[1]), reads_in.reshape(block_count, span_len, reads_in.shape[1]), segment.reshape(block_count, span_len))
    places = jnp.arange(span_len, dtype=jnp.int32)
    causal = places[:, None] >= places[None, :]

    def one_block(carry, block):
        carry_state, last_seg = carry
        block_values, block_steps, block_keys, block_reads, block_seg = block
        log_decay = jnp.cumsum(block_steps * decay_rates[None, :], axis=0)
        allowed = (causal & (block_seg[:, None] == block_seg[None, :])).astype(jnp.float32)
        gap_logs = log_decay[:, None, :] - log_decay[None, :, :]
        decay_grid = jnp.exp(jnp.where(allowed[:, :, None] > 0.5, gap_logs, 0.0)) * allowed[:, :, None]
        scores = jnp.dot(block_reads, block_keys.T, precision=PRECISE)
        mix_grid = scores[:, :, None] * decay_grid * block_steps[None, :, :]
        inside = jnp.einsum('tsh,shp->thp', mix_grid, block_values, precision=PRECISE)
        carried = (block_seg == last_seg).astype(jnp.float32)
        reach_now = jnp.exp(log_decay) * carried[:, None]
        outside = jnp.einsum('tn,hpn->thp', block_reads, carry_state, precision=PRECISE) * reach_now[:, :, None]
        end_same = (block_seg == block_seg[-1]).astype(jnp.float32)
        tail_weight = jnp.exp(log_decay[-1][None, :] - log_decay) * block_steps * end_same[:, None]
        fresh_state = jnp.einsum('sh,shp,sn->hpn', tail_weight, block_values, block_keys, precision=PRECISE)
        kept_state = carry_state * (jnp.exp(log_decay[-1]) * carried[-1])[:, None, None] + fresh_state
        return ((kept_state, block_seg[-1]), inside + outside)
    start_carry = (jnp.zeros((head_count, head_width, keys_in.shape[1]), jnp.float32), jnp.int32(-1))
    final_carry, outputs = lax.scan(jax.checkpoint(one_block), start_carry, blocks)
    return outputs.reshape(length, head_count, head_width)

def mixer_local(mixed_in, steps_in, decay_log, shared, skip_gain, segment, head_count):
    length = mixed_in.shape[0]
    shaped = mixed_in.reshape(length, head_count, mixed_in.shape[1] // head_count)
    half_width = shared.shape[1] // 2
    scanned = ssd_scan(shaped, steps_in, -jnp.exp(decay_log), shared[:, :half_width], shared[:, half_width:], segment, SPAN)
    return (scanned + skip_gain[None, :, None] * shaped).reshape(length, mixed_in.shape[1])

def group_forward(weights, row_block, lengths_row):
    norm_in, w_gate, w_value, w_pair, w_step, conv_value, bias_value, conv_pair, bias_pair, step_bias, decay_log, skip_gain, norm_gate, w_out = weights
    length = row_block.shape[0]
    segment = segment_ids(lengths_row, length)
    live_mask = (segment < lengths_row.shape[0] - 1).astype(jnp.float32)
    rms_scale = lax.rsqrt(lax.optimization_barrier(jnp.mean(row_block * row_block, axis=1, keepdims=True)) + EPS)
    normed = low(row_block * rms_scale * norm_in[None, :])
    gate_proj = low_back(jnp.dot(normed, w_gate, precision=PRECISE))
    value_proj = low_back(jnp.dot(normed, w_value, precision=PRECISE))
    pair_proj = low_back(jnp.dot(normed, w_pair, precision=PRECISE))
    step_proj = low_back(jnp.dot(normed, w_step, precision=PRECISE))
    mixed_in = conv_silu(value_proj, conv_value, bias_value, segment)
    shared = low(conv_silu(pair_proj, conv_pair, bias_pair, segment))
    steps = softplus_shift(step_proj, step_bias)
    scanned = mixer_local(mixed_in, steps, decay_log, shared, skip_gain, segment, HEADS)
    gated = scanned * jax.nn.silu(gate_proj)
    spread = lax.rsqrt(lax.optimization_barrier(jnp.mean(gated * gated, axis=1, keepdims=True)) + EPS)
    normed_out = low(gated * spread * norm_gate[None, :])
    branch = jnp.dot(normed_out, w_out, precision=PRECISE)
    return row_block + live_mask[:, None] * branch

def reference(tokens, cotangent, seq_lengths, token_order, norm_in, w_gate, w_value, w_pair, w_step, conv_value, bias_value, conv_pair, bias_pair, step_bias, decay_log, skip_gain, norm_gate, w_out):
    params = tuple((item.astype(jnp.float32) for item in (norm_in, w_gate, w_value, w_pair, w_step, conv_value, bias_value, conv_pair, bias_pair, step_bias, decay_log, skip_gain, norm_gate, w_out)))
    width = tokens.shape[1]
    dealt = tokens.astype(jnp.float32)[token_order]
    dealt_back = cotangent.astype(jnp.float32)[token_order]
    group_count = seq_lengths.shape[0]
    blocks = dealt.reshape(group_count, -1, width)

    def forward(weights, row_blocks):

        def single(pair_in):
            return group_forward(weights, pair_in[0], pair_in[1])
        return lax.map(jax.checkpoint(single), (row_blocks, seq_lengths))
    outputs, pullback = jax.vjp(forward, params, blocks)
    grads, grad_blocks = pullback(dealt_back.reshape(blocks.shape))
    block_out = jnp.zeros_like(dealt).at[token_order].set(outputs.reshape(-1, width))
    grad_tokens = jnp.zeros_like(dealt).at[token_order].set(grad_blocks.reshape(-1, width))
    return (block_out.astype(jnp.bfloat16), grad_tokens.astype(jnp.bfloat16), grads[0], grads[1], grads[2], grads[3], grads[4], grads[5], grads[6], grads[7], grads[8], grads[9], grads[10], grads[11], grads[12], grads[13])
```

```python
from functools import partial

import jax
import jax.numpy as jnp
import numpy as np
from jax import lax
from jax.experimental import pallas as pl
from jax.experimental.pallas import tpu as pltpu
from jax.sharding import PartitionSpec as P

EPS = 1e-05
EXACT = lax.Precision.HIGHEST
F32 = jnp.float32
BF16 = jnp.bfloat16
SUB = 128
ROWS = 256
LANES = 128
VMEM_BYTES = 56 * 1024 * 1024


def dot_nn(a, b):
    return jnp.dot(a, b, preferred_element_type=F32)


def dot_nt(a, b):
    return lax.dot_general(a, b, (((1,), (1,)), ((), ())), preferred_element_type=F32)


def dot_tn(a, b):
    return lax.dot_general(a, b, (((0,), (0,)), ((), ())), preferred_element_type=F32)


def sigmoid(v):
    return 1.0 / (1.0 + jnp.exp(-v))


def softplus(v):
    return jnp.maximum(v, 0.0) + jnp.log1p(jnp.exp(-jnp.abs(v)))


def split_two(v):
    high = v.astype(BF16)
    return high, (v - high.astype(F32)).astype(BF16)


def read_bounds(bounds_ref, micro):
    return [bounds_ref[micro, k] for k in range(bounds_ref.shape[1])]


def segment_of(places, bounds):
    total = (places >= bounds[0]).astype(jnp.int32)
    for bound in bounds[1:]:
        total = total + (places >= bound).astype(jnp.int32)
    return total


def segment_scalar(place, bounds):
    total = jnp.int32(0)
    for bound in bounds:
        total = total + jnp.where(place >= bound, 1, 0)
    return total


def iota(shape, axis):
    return lax.broadcasted_iota(jnp.int32, shape, axis)


def same_masks(places, bounds, count):
    own = segment_of(places, bounds)
    return [
        (segment_of(places - shift, bounds) == own) & (places >= shift) & (places < count)
        for shift in range(1, 4)
    ]


def expand_heads(parts, spread_ref):
    stacked = jnp.concatenate(parts, axis=0)
    high, low = split_two(stacked)
    lane = iota(stacked.shape, 1)
    joined = jnp.where(lane < 8, high.astype(F32), pltpu.roll(low.astype(F32), 8, 1))
    wide = dot_nn(joined.astype(BF16), spread_ref[...])
    sizes = np.cumsum([0] + [part.shape[0] for part in parts])
    return [wide[sizes[k] : sizes[k + 1]] for k in range(len(parts))]


def reduce_heads(v, gather_ref):
    high, low = split_two(v)
    return dot_nn(high, gather_ref[...]) + dot_nn(low, gather_ref[...])


def scan_frame(base, bounds, steps, rate, lower_ref):
    start_place = base
    col = start_place + iota((SUB, LANES), 0)
    row = start_place + iota((SUB, SUB), 1)
    seg_col = segment_of(col, bounds)
    seg_row = segment_of(row, bounds)
    allowed = (seg_col == seg_row) & (col >= row)
    last_seg = jnp.where(start_place > 0, segment_scalar(start_place - 1, bounds), -1)
    end_seg = segment_scalar(start_place + SUB - 1, bounds)
    log_decay = jnp.dot(
        lower_ref[...], steps * rate, preferred_element_type=F32, precision=EXACT
    )
    reach = jnp.where(seg_col == last_seg, jnp.exp(log_decay), 0.0)
    tail = jnp.where(
        seg_col == end_seg, jnp.exp(log_decay[SUB - 1 : SUB, :] - log_decay), 0.0
    )
    return allowed, log_decay, reach, tail


def decay_grid(log_decay, log_rows, head):
    gap = log_decay[:, head : head + 1] - log_rows[head : head + 1, :]
    return jnp.exp(jnp.minimum(gap, 0.0))


def forward_kernel(
    pair_count,
    bounds_ref,
    x_ref,
    norm_in_ref,
    w_value_ref,
    w_gate_ref,
    w_small_ref,
    taps_value_ref,
    taps_pair_ref,
    heads_ref,
    skip_ref,
    norm_gate_ref,
    w_out_ref,
    spread_ref,
    lower_ref,
    normed_ref,
    gate_ref,
    value_ref,
    conv_value_ref,
    pair_ref,
    conv_pair_ref,
    step_ref,
    scanned_ref,
    states_ref,
    partial_ref,
    square_ref,
    halo_value,
    halo_pair,
    state,
):
    micro = pl.program_id(0)
    block = pl.program_id(1)
    count = pl.num_programs(1) * ROWS
    bounds = read_bounds(bounds_ref, micro)
    base = block * ROWS

    @pl.when(block == 0)
    def _():
        halo_value[...] = jnp.zeros_like(halo_value)
        halo_pair[...] = jnp.zeros_like(halo_pair)
        state[...] = jnp.zeros_like(state)

    x = x_ref[...].reshape(ROWS, x_ref.shape[-1]).astype(F32)
    rms = lax.rsqrt(jnp.mean(x * x, axis=1, keepdims=True) + EPS)
    normed = (x * rms * norm_in_ref[...].astype(F32)).astype(BF16)
    normed_ref[...] = normed
    value = dot_nn(normed, w_value_ref[...])
    gate = dot_nn(normed, w_gate_ref[...])
    small = dot_nt(normed, w_small_ref[...])
    pair_width = conv_pair_ref.shape[-1]
    pair = small[:, :pair_width]
    step = small[:, pair_width : pair_width + LANES]
    value_ref[...] = value
    gate_ref[...] = gate
    pair_ref[...] = pair
    step_ref[...] = step

    places = base + iota((ROWS, LANES), 0)
    masks = same_masks(places, bounds, count)

    def convolve(v, halo, taps):
        longer = jnp.concatenate([halo, v], axis=0)
        width = v.shape[1]
        out = taps[4:5, :] + taps[3:4, :] * v
        for shift in range(1, 4):
            moved = pltpu.roll(longer, shift, 0)[8:, :]
            mask = jnp.concatenate([masks[shift - 1]] * (width // LANES), axis=1)
            out = out + jnp.where(mask, moved * taps[3 - shift : 4 - shift, :], 0.0)
        return out

    conv_value = convolve(value, halo_value[...], taps_value_ref[...])
    conv_pair = convolve(pair, halo_pair[...], taps_pair_ref[...])
    halo_value[...] = value[ROWS - 8 :, :]
    halo_pair[...] = pair[ROWS - 8 :, :]
    conv_value_ref[...] = conv_value
    conv_pair_ref[...] = conv_pair
    mixed = conv_value * sigmoid(conv_value)
    shared = (conv_pair * sigmoid(conv_pair)).astype(BF16)
    steps = softplus(step + heads_ref[0:1, :])
    rate = heads_ref[1:2, :]
    lane = iota((SUB, LANES), 1)
    left = lane < 64

    scanned_parts = []
    for sub in range(ROWS // SUB):
        rows = slice(sub * SUB, (sub + 1) * SUB)
        sub_steps = steps[rows]
        allowed, log_decay, reach, tail = scan_frame(
            base + sub * SUB, bounds, sub_steps, rate, lower_ref
        )
        steps_wide, reach_wide, tail_wide = expand_heads(
            [sub_steps, reach, tail], spread_ref
        )
        log_rows = log_decay.T
        keys = shared[rows, :LANES]
        reads = shared[rows, LANES:]
        scores = jnp.where(allowed, dot_nt(reads, keys), 0.0)
        stepped = mixed[rows] * steps_wide
        stepped_low = stepped.astype(BF16)
        held = state[...]
        states_ref[sub] = held
        outside = dot_nn(reads, held.astype(BF16)) * reach_wide
        inside = []
        for p in range(pair_count):
            cols = slice(p * LANES, (p + 1) * LANES)
            grids = [
                (scores * decay_grid(log_decay, log_rows, 2 * p + k)).astype(BF16)
                for k in range(2)
            ]
            both = stepped_low[:, cols]
            zero = jnp.zeros_like(both)
            inside.append(
                dot_nn(
                    jnp.concatenate(grids, axis=1),
                    jnp.concatenate(
                        [jnp.where(left, both, zero), jnp.where(left, zero, both)], axis=0
                    ),
                )
            )
        scanned_parts.append(
            jnp.concatenate(inside, axis=1) + outside + mixed[rows] * skip_ref[...]
        )
        state[...] = held * reach_wide[SUB - 1 : SUB, :] + dot_tn(
            keys, (stepped * tail_wide).astype(BF16)
        )
    scanned = jnp.concatenate(scanned_parts, axis=0)
    scanned_ref[...] = scanned
    gated = scanned * (gate * sigmoid(gate))
    high, low = split_two(gated * gated)
    ones = jnp.ones((8, gated.shape[1]), BF16)
    square_ref[...] = dot_nt(ones, high) + dot_nt(ones, low)
    scaled = (gated * norm_gate_ref[...]).astype(BF16)
    partial_ref[...] = (
        dot_nn(scaled, w_out_ref[...]).astype(BF16).reshape(partial_ref.shape)
    )


def back_kernel(
    live_ids,
    bounds_ref,
    back_ref,
    w_out_ref,
    norm_gate_ref,
    scanned_ref,
    gate_ref,
    square_ref,
    grad_normed_ref,
    stats_ref,
):
    micro = pl.program_id(0)
    bounds = read_bounds(bounds_ref, micro)
    base = pl.program_id(1) * ROWS
    places = base + iota((ROWS, LANES), 0)
    live = segment_of(places, bounds) < live_ids
    grad = dot_nt(back_ref[...].reshape(ROWS, back_ref.shape[-1]), w_out_ref[...])
    live_wide = jnp.concatenate([live] * (grad.shape[1] // LANES), axis=1)
    grad = jnp.where(live_wide, grad, 0.0)
    grad_normed_ref[...] = grad
    gate = gate_ref[...]
    gated = scanned_ref[...] * (gate * sigmoid(gate))
    high, low = split_two(grad * norm_gate_ref[...] * gated)
    ones = jnp.ones((8, gated.shape[1]), BF16)
    cross = dot_nt(ones, high) + dot_nt(ones, low)
    stats_ref[...] = jnp.where(iota(cross.shape, 0) == 0, square_ref[...], cross)


def backward_kernel(
    pair_count,
    live_ids,
    inner_full,
    bounds_ref,
    stats_ref,
    grad_normed_ref,
    normed_ref,
    gate_ref,
    value_ref,
    conv_value_ref,
    pair_ref,
    conv_pair_ref,
    step_ref,
    scanned_ref,
    states_ref,
    w_value_ref,
    w_gate_ref,
    w_small_ref,
    taps_value_ref,
    taps_pair_ref,
    heads_ref,
    skip_ref,
    norm_gate_ref,
    spread_ref,
    gather_ref,
    lower_ref,
    upper_ref,
    low_gate_ref,
    low_value_ref,
    low_small_ref,
    normed_out_ref,
    grad_in_ref,
    sums_ref,
    sums_in_ref,
    halo_value,
    halo_pair,
    state,
):
    micro = pl.program_id(0)
    turn = pl.program_id(1)
    block_count = pl.num_programs(1)
    block = block_count - 1 - turn
    count = block_count * ROWS
    bounds = read_bounds(bounds_ref, micro)
    base = block * ROWS

    @pl.when((micro == 0) & (turn == 0))
    def _():
        sums_ref[...] = jnp.zeros_like(sums_ref)
        sums_in_ref[...] = jnp.zeros_like(sums_in_ref)

    @pl.when(turn == 0)
    def _():
        halo_value[...] = jnp.zeros_like(halo_value)
        halo_pair[...] = jnp.zeros_like(halo_pair)
        state[...] = jnp.zeros_like(state)

    width = gate_ref.shape[1]
    tiles = width // LANES
    places = base + iota((ROWS, LANES), 0)
    live = segment_of(places, bounds) < live_ids

    gate = gate_ref[...]
    scanned = scanned_ref[...]
    grad_normed = grad_normed_ref[...]
    norm_gate = norm_gate_ref[...]
    spread = lax.rsqrt(stats_ref[:, 0:1] / inner_full + EPS)
    cross = stats_ref[:, 1:2] / inner_full
    sg = sigmoid(gate)
    act = gate * sg
    gated = scanned * act
    normed_gated = gated * spread
    live_wide = jnp.concatenate([live] * tiles, axis=1)
    normed_out_ref[...] = jnp.where(live_wide, normed_gated * norm_gate, 0.0).astype(BF16)
    grad_gated = spread * (grad_normed * norm_gate - normed_gated * (spread * cross))
    grad_scanned = grad_gated * act
    low_gate = (grad_gated * scanned * (sg * (1.0 + gate * (1.0 - sg)))).astype(BF16)
    low_gate_ref[...] = low_gate

    conv_value = conv_value_ref[...]
    sig_value = sigmoid(conv_value)
    mixed = conv_value * sig_value
    conv_pair = conv_pair_ref[...]
    sig_pair = sigmoid(conv_pair)
    shared = (conv_pair * sig_pair).astype(BF16)
    step_in = step_ref[...] + heads_ref[0:1, :]
    steps = softplus(step_in)
    rate = heads_ref[1:2, :]
    skip = skip_ref[...]
    lane = iota((SUB, LANES), 1)
    left = lane < 64

    grad_mixed_parts = []
    grad_shared_parts = []
    grad_step_parts = []
    decay_sum = jnp.zeros((1, LANES), F32)
    for sub in reversed(range(ROWS // SUB)):
        rows = slice(sub * SUB, (sub + 1) * SUB)
        sub_steps = steps[rows]
        allowed, log_decay, reach, tail = scan_frame(
            base + sub * SUB, bounds, sub_steps, rate, lower_ref
        )
        steps_wide, reach_wide, tail_wide = expand_heads(
            [sub_steps, reach, tail], spread_ref
        )
        log_rows = log_decay.T
        keys = shared[rows, :LANES]
        reads = shared[rows, LANES:]
        scores = jnp.where(allowed, dot_nt(reads, keys), 0.0)
        sub_mixed = mixed[rows]
        stepped = sub_mixed * steps_wide
        stepped_low = stepped.astype(BF16)
        grad_y = grad_scanned[rows]
        grad_low = grad_y.astype(BF16)
        held = states_ref[sub]
        later = state[...]
        later_low = later.astype(BF16)
        grad_scores = jnp.zeros((SUB, SUB), F32)
        inner = []
        for p in range(pair_count):
            cols = slice(p * LANES, (p + 1) * LANES)
            both_x = stepped_low[:, cols]
            both_y = grad_low[:, cols]
            zero = jnp.zeros_like(both_y)
            halves = [jnp.where(left, both_y, zero), jnp.where(left, zero, both_y)]
            grids = []
            for k in range(2):
                fade = decay_grid(log_decay, log_rows, 2 * p + k)
                grids.append((scores * fade).astype(BF16))
                grad_scores = grad_scores + dot_nt(halves[k], both_x) * fade
            inner.append(
                dot_tn(jnp.concatenate(grids, axis=0), jnp.concatenate(halves, axis=0))
            )
        grad_scores = jnp.where(allowed, grad_scores, 0.0).astype(BF16)
        tail_part = tail_wide * dot_nn(keys, later_low)
        grad_stepped = jnp.concatenate(inner, axis=1) + tail_part
        reached = (grad_y * reach_wide).astype(BF16)
        tailed = (stepped * tail_wide).astype(BF16)
        grad_reads = dot_nn(grad_scores, keys) + dot_nt(reached, held.astype(BF16))
        grad_keys = dot_tn(grad_scores, reads) + dot_nt(tailed, later_low)
        stepped_back = stepped_low.astype(F32)
        per_log = reduce_heads(
            grad_low.astype(F32) * (scanned[rows] - skip * sub_mixed)
            - stepped_back * grad_stepped,
            gather_ref,
        )
        kept_wide = reach_wide[SUB - 1 : SUB, :]
        at_end = jnp.sum(stepped_back * tail_part, axis=0, keepdims=True) + kept_wide * jnp.sum(
            later * held, axis=0, keepdims=True
        )
        at_end = reduce_heads(jnp.broadcast_to(at_end, (8, width)), gather_ref)[0:1, :]
        grad_log = (
            jnp.dot(upper_ref[...], per_log, preferred_element_type=F32, precision=EXACT)
            + at_end
        )
        decay_sum = decay_sum + jnp.sum(grad_log * sub_steps, axis=0, keepdims=True) * rate
        grad_steps = reduce_heads(grad_stepped * sub_mixed, gather_ref) + rate * grad_log
        grad_step_parts.insert(0, grad_steps)
        grad_shared_parts.insert(0, jnp.concatenate([grad_keys, grad_reads], axis=1))
        grad_mixed_parts.insert(0, grad_stepped * steps_wide + skip * grad_y)
        state[...] = later * kept_wide + dot_tn(reads, reached)
    grad_mixed = jnp.concatenate(grad_mixed_parts, axis=0)
    grad_shared = jnp.concatenate(grad_shared_parts, axis=0)
    grad_step = jnp.concatenate(grad_step_parts, axis=0) * sigmoid(step_in)

    longer_places = base + iota((ROWS + 8, LANES), 0)
    masks = same_masks(longer_places, bounds, count)

    def convolve_back(q, halo, v, taps):
        longer = jnp.concatenate([q, halo], axis=0)
        grad = taps[3:4, :] * q
        tap_sums = [jnp.sum(v * q, axis=0, keepdims=True)]
        for shift in range(1, 4):
            mask = jnp.concatenate([masks[shift - 1]] * (q.shape[1] // LANES), axis=1)
            kept = jnp.where(mask, longer, 0.0)
            moved = pltpu.roll(kept, ROWS + 8 - shift, 0)[:ROWS, :]
            grad = grad + taps[3 - shift : 4 - shift, :] * moved
            tap_sums.insert(0, jnp.sum(v * moved, axis=0, keepdims=True))
        return grad, tap_sums + [jnp.sum(q, axis=0, keepdims=True)]

    q_value = grad_mixed * (sig_value * (1.0 + conv_value * (1.0 - sig_value)))
    q_pair = grad_shared * (sig_pair * (1.0 + conv_pair * (1.0 - sig_pair)))
    grad_value, value_sums = convolve_back(
        q_value, halo_value[...], value_ref[...], taps_value_ref[...]
    )
    grad_pair, pair_sums = convolve_back(
        q_pair, halo_pair[...], pair_ref[...], taps_pair_ref[...]
    )
    halo_value[...] = q_value[:8, :]
    halo_pair[...] = q_pair[:8, :]
    low_value = grad_value.astype(BF16)
    low_small = jnp.concatenate([grad_pair, grad_step], axis=1).astype(BF16)
    low_value_ref[...] = low_value
    low_small_ref[...] = low_small
    grad_in = (
        dot_nt(low_gate, w_gate_ref[...])
        + dot_nt(low_value, w_value_ref[...])
        + dot_nn(low_small, w_small_ref[...])
    )
    grad_in_ref[...] = grad_in.astype(BF16).reshape(grad_in_ref.shape)
    sums_in_ref[0:1, :] += jnp.sum(grad_in * normed_ref[...].astype(F32), axis=0, keepdims=True)
    gate_sum = jnp.sum(grad_normed * normed_gated, axis=0, keepdims=True)
    skip_sum = jnp.sum(grad_scanned * mixed, axis=0, keepdims=True)
    step_sum = jnp.sum(grad_step, axis=0, keepdims=True)
    for k in range(5):
        sums_ref[k : k + 1, :] += value_sums[k]
    sums_ref[5:6, :] += gate_sum
    sums_ref[6:7, :] += skip_sum
    sums_ref[7:8, :LANES] += step_sum
    sums_ref[7:8, LANES : 2 * LANES] += decay_sum
    for k in range(5):
        sums_ref[8 + k : 9 + k, : pair_sums[k].shape[1]] += pair_sums[k]


def whole_spec(shape):
    return pl.BlockSpec(shape, lambda *_: (0,) * len(shape))


def smem_spec():
    return pl.BlockSpec(memory_space=pltpu.SMEM)


def kernel_params():
    return pltpu.CompilerParams(vmem_limit_bytes=VMEM_BYTES)


def head_constants(head_count, head_width):
    width = head_count * head_width
    spread = np.zeros((LANES, width), np.float32)
    for h in range(head_count):
        spread[h, h * head_width : (h + 1) * head_width] = 1.0
        spread[h + 8, h * head_width : (h + 1) * head_width] = 1.0
    gather = np.zeros((width, LANES), np.float32)
    for h in range(head_count):
        gather[h * head_width : (h + 1) * head_width, h] = 1.0
    lower = np.tril(np.ones((SUB, SUB), np.float32))
    return (
        jnp.asarray(spread, BF16),
        jnp.asarray(gather, BF16),
        jnp.asarray(lower),
        jnp.asarray(lower.T),
    )


def run_forward(bounds, rows, weights, consts):
    micro_count, block_len = rows.shape[1], rows.shape[0] * rows.shape[2]
    blocks = block_len // ROWS
    per_block = ROWS // rows.shape[2]
    norm_in, w_value, w_gate, w_small, taps_value, taps_pair, heads, skip, norm_gate, w_out = weights
    spread, _, lower, _ = consts
    full = rows.shape[3]
    width = w_value.shape[1]
    pair_width = taps_pair.shape[1]
    length = micro_count * block_len
    subs = ROWS // SUB

    def by_rows(cols):
        return pl.BlockSpec((ROWS, cols), lambda b, i: (b * blocks + i, 0))

    row_block = pl.BlockSpec((per_block, None, rows.shape[2], full), lambda b, i: (i, b, 0, 0))
    wholes = [norm_in, w_value, w_gate, w_small, taps_value, taps_pair, heads, skip, norm_gate, w_out, spread, lower]
    widths = [width, width, width, pair_width, pair_width, LANES, width]
    return pl.pallas_call(
        partial(forward_kernel, width // LANES),
        grid=(micro_count, blocks),
        in_specs=[smem_spec(), row_block] + [whole_spec(item.shape) for item in wholes],
        out_specs=[by_rows(full)]
        + [by_rows(cols) for cols in widths]
        + [
            pl.BlockSpec((subs, LANES, width), lambda b, i: (b * blocks + i, 0, 0)),
            row_block,
            pl.BlockSpec((8, ROWS), lambda b, i: (0, b * blocks + i)),
        ],
        out_shape=[jax.ShapeDtypeStruct((length, full), BF16)]
        + [jax.ShapeDtypeStruct((length, cols), F32) for cols in widths]
        + [
            jax.ShapeDtypeStruct((length // SUB, LANES, width), F32),
            jax.ShapeDtypeStruct(rows.shape, BF16),
            jax.ShapeDtypeStruct((8, length), F32),
        ],
        scratch_shapes=[
            pltpu.VMEM((8, width), F32),
            pltpu.VMEM((8, pair_width), F32),
            pltpu.VMEM((LANES, width), F32),
        ],
        compiler_params=kernel_params(),
        name="forward",
    )(bounds, rows, *wholes)


def run_back(bounds, back, w_out, norm_gate, scanned, gate, square, live_ids):
    micro_count, block_len = back.shape[1], back.shape[0] * back.shape[2]
    blocks = block_len // ROWS
    per_block = ROWS // back.shape[2]
    width = gate.shape[1]
    length = micro_count * block_len
    by_rows = pl.BlockSpec((ROWS, width), lambda b, i: (b * blocks + i, 0))
    by_cols = pl.BlockSpec((8, ROWS), lambda b, i: (0, b * blocks + i))
    row_block = pl.BlockSpec((per_block, None, back.shape[2], back.shape[3]), lambda b, i: (i, b, 0, 0))
    return pl.pallas_call(
        partial(back_kernel, live_ids),
        grid=(micro_count, blocks),
        in_specs=[
            smem_spec(),
            row_block,
            whole_spec(w_out.shape),
            whole_spec(norm_gate.shape),
            by_rows,
            by_rows,
            by_cols,
        ],
        out_specs=[by_rows, by_cols],
        out_shape=[
            jax.ShapeDtypeStruct((length, width), F32),
            jax.ShapeDtypeStruct((8, length), F32),
        ],
        compiler_params=kernel_params(),
        name="back",
    )(bounds, back, w_out, norm_gate, scanned, gate, square)


def run_backward(bounds, stats, grad_normed, kept, weights, consts, rows_shape, live_ids, inner_full):
    micro_count, block_len = rows_shape[1], rows_shape[0] * rows_shape[2]
    blocks = block_len // ROWS
    per_block = ROWS // rows_shape[2]
    normed, gate, value, conv_value, pair, conv_pair, step, scanned, states = kept
    _, w_value, w_gate, w_small, taps_value, taps_pair, heads, skip, norm_gate, _ = weights
    spread, gather, lower, upper = consts
    full = rows_shape[3]
    width = gate.shape[1]
    pair_width = pair.shape[1]
    length = micro_count * block_len
    subs = ROWS // SUB

    def place(b, i):
        return b * blocks + blocks - 1 - i

    def by_rows(item):
        return pl.BlockSpec((ROWS, item.shape[1]), lambda b, i: (place(b, i), 0))

    row_block = pl.BlockSpec(
        (per_block, None, rows_shape[2], full), lambda b, i: (blocks - 1 - i, b, 0, 0)
    )
    rowwise = [stats, grad_normed, normed, gate, value, conv_value, pair, conv_pair, step, scanned]
    wholes = [w_value, w_gate, w_small, taps_value, taps_pair, heads, skip, norm_gate, spread, gather, lower, upper]
    outs = [
        jax.ShapeDtypeStruct((length, width), BF16),
        jax.ShapeDtypeStruct((length, width), BF16),
        jax.ShapeDtypeStruct((length, w_small.shape[0]), BF16),
        jax.ShapeDtypeStruct((length, width), BF16),
        jax.ShapeDtypeStruct(rows_shape, BF16),
        jax.ShapeDtypeStruct((16, width), F32),
        jax.ShapeDtypeStruct((8, full), F32),
    ]
    return pl.pallas_call(
        partial(backward_kernel, width // LANES, live_ids, inner_full),
        grid=(micro_count, blocks),
        in_specs=[smem_spec()]
        + [by_rows(item) for item in rowwise]
        + [pl.BlockSpec((subs, LANES, width), lambda b, i: (place(b, i), 0, 0))]
        + [whole_spec(item.shape) for item in wholes],
        out_specs=[by_rows(item) for item in outs[:4]]
        + [row_block, whole_spec(outs[5].shape), whole_spec(outs[6].shape)],
        out_shape=outs,
        scratch_shapes=[
            pltpu.VMEM((8, width), F32),
            pltpu.VMEM((8, pair_width), F32),
            pltpu.VMEM((LANES, width), F32),
        ],
        compiler_params=kernel_params(),
        name="backward",
    )(bounds, *rowwise, states, *wholes)


def deal_kernel(
    group_shift,
    place_ref,
    listed_ref,
    listed_cols_ref,
    own_ref,
    own_col_ref,
    tokens_ref,
    cotangent_ref,
    send_tokens_ref,
    send_cotangent_ref,
    send_map_ref,
    take_map_ref,
):
    start, group, target = place_ref[0], place_ref[1], place_ref[2]
    share = tokens_ref.shape[0]
    group_count = listed_cols_ref.shape[1]
    quota = share // group_count
    natural = start + iota((share, share), 1)
    found = []
    for g in range(group_count):
        hits = (listed_cols_ref[:, g : g + 1] == natural).astype(F32)
        found.append(jnp.sum(hits, axis=0, keepdims=True))
    pad = -group_count % 8
    found = jnp.concatenate(found + [jnp.zeros((pad, share), F32)] * (pad > 0), axis=0)
    before = (iota((share, share), 0) < iota((share, share), 1)).astype(BF16)
    rank = dot_nn(found.astype(BF16), before)
    slot = (iota(found.shape, 0) ^ group) * quota
    place = jnp.sum(found * (rank + slot.astype(F32)), axis=0, keepdims=True)
    send_map = (iota((share, share), 0).astype(F32) == place).astype(BF16)
    send_map_ref[...] = send_map
    own_row = jnp.broadcast_to(own_ref[...], (share, share))
    own_col = jnp.broadcast_to(own_col_ref[...], (share, share))
    src_row = lax.shift_right_logical(own_row, group_shift)
    src_col = lax.shift_right_logical(own_col, group_shift)
    ahead = ((src_row == src_col) & (own_row < own_col)).astype(F32)
    order = jnp.sum(ahead, axis=1, keepdims=True)
    wanted = ((src_col ^ target) * quota).astype(F32) + order
    take_map_ref[...] = (iota((share, share), 1).astype(F32) == wanted).astype(BF16)
    send_tokens_ref[...] = dot_nn(send_map, tokens_ref[...]).astype(BF16)
    send_cotangent_ref[...] = dot_nn(send_map, cotangent_ref[...]).astype(BF16)


def run_deal(place, listed, own, tokens, cotangent, group_len):
    share, width = tokens.shape
    vmem = pl.BlockSpec(memory_space=pltpu.VMEM)
    return pl.pallas_call(
        partial(deal_kernel, group_len.bit_length() - 1),
        in_specs=[smem_spec()] + [vmem] * 6,
        out_specs=[vmem] * 4,
        out_shape=[jax.ShapeDtypeStruct((share, width), BF16)] * 2
        + [jax.ShapeDtypeStruct((share, share), BF16)] * 2,
        compiler_params=kernel_params(),
        name="deal",
    )(place, listed, listed.T, own[None, :], own[:, None], tokens, cotangent)


def pick_kernel(transposed, map_ref, rows_ref, out_ref):
    dot = dot_tn if transposed else dot_nn
    out_ref[...] = dot(map_ref[...], rows_ref[...]).astype(BF16)


def run_pick(take_map, rows, transposed):
    vmem = pl.BlockSpec(memory_space=pltpu.VMEM)
    return pl.pallas_call(
        partial(pick_kernel, transposed),
        in_specs=[vmem] * 2,
        out_specs=vmem,
        out_shape=jax.ShapeDtypeStruct((take_map.shape[0], rows.shape[1]), BF16),
        compiler_params=kernel_params(),
        name="pick",
    )(take_map, rows)


def close_out_kernel(map_ref, dealt_ref, branch_ref, weight_ref, out_ref):
    shape = dealt_ref.shape
    out = dealt_ref[...].astype(F32) + weight_ref[...] * branch_ref[...].reshape(shape).astype(F32)
    out_ref[...] = dot_tn(map_ref[...], out.astype(BF16)).astype(BF16)


def close_back_kernel(map_ref, dealt_ref, back_ref, grad_ref, norm_in_ref, out_ref):
    shape = dealt_ref.shape
    x = dealt_ref[...].astype(F32)
    rms = lax.rsqrt(jnp.mean(x * x, axis=1, keepdims=True) + EPS)
    xhat = x * rms
    win = grad_ref[...].reshape(shape).astype(F32) * norm_in_ref[...].astype(F32)
    cross = jnp.mean(win * xhat, axis=1, keepdims=True)
    out = back_ref[...].astype(F32) + rms * (win - xhat * cross)
    out_ref[...] = dot_tn(map_ref[...], out.astype(BF16)).astype(BF16)


def run_close(body, take_map, *items):
    vmem = pl.BlockSpec(memory_space=pltpu.VMEM)
    return pl.pallas_call(
        body,
        in_specs=[vmem] * (1 + len(items)),
        out_specs=vmem,
        out_shape=jax.ShapeDtypeStruct(items[0].shape, BF16),
        compiler_params=kernel_params(),
        name="close",
    )(take_map, *items)


ALL = ("pair", "core", "row", "half", "near")
TEAM = ("row", "core", "near")


def make_perm(sizes, move):
    ranks = np.arange(int(np.prod(sizes))).reshape(sizes)
    return [
        (int(ranks[where]), int(ranks[move(*where)])) for where in np.ndindex(*sizes)
    ]


def turned(perm):
    return [(target, source) for source, target in perm]


def swap(v, perm):
    return lax.ppermute(v, ALL, perm)


def choose(bit, first, second, axis):
    return jnp.where(
        bit == 0,
        jnp.concatenate([first, second], axis=axis),
        jnp.concatenate([second, first], axis=axis),
    )


def per_device(
    sizes,
    tokens,
    cotangent,
    seq_lengths,
    token_order,
    norm_in,
    w_gate,
    w_value,
    w_pair,
    w_step,
    conv_value,
    bias_value,
    conv_pair,
    bias_pair,
    step_bias,
    decay_log,
    skip_gain,
    norm_gate,
    w_out,
):
    pair_count = sizes[0]
    group_count = sizes[0] * sizes[1]
    team_size = sizes[2] * sizes[3] * sizes[4]
    my_pair, my_core, my_row, my_half, my_near = [lax.axis_index(name) for name in ALL]
    group = my_pair * 2 + my_core
    target = my_pair * 2 + my_half
    member = my_row * (sizes[3] * sizes[4]) + my_half * sizes[4] + my_near
    seat = my_row * (sizes[3] * sizes[4]) + my_core * sizes[4] + my_near

    share_len, width_full = tokens.shape
    quota_len = share_len // group_count
    micro_count = seq_lengths.shape[0]
    piece_len = share_len // micro_count
    block_len = piece_len * team_size
    group_len = share_len * team_size
    width = w_gate.shape[1]
    inner_full = width * team_size
    head_count = step_bias.shape[0]
    head_width = width // head_count
    pair_part = w_pair.shape[1]
    pair_width = pair_part * team_size
    small_width = pair_width + LANES

    deal_perms = [
        make_perm(
            sizes,
            lambda p, c, r, h, n, e=e: (p ^ (e // 2), h, r, c ^ (e % 2), n),
        )
        for e in range(group_count)
    ]
    cross_perms = [
        make_perm(sizes, lambda p, c, r, h, n, f=f: (p, h, r, c ^ f, n)) for f in range(2)
    ]
    pair_bits = [k for k in range(pair_count.bit_length() - 1)]
    pair_perms = [
        make_perm(sizes, lambda p, c, r, h, n, k=k: (p ^ (1 << k), c, r, h, n))
        for k in pair_bits
    ]

    def gather_groups(block, axis):
        first = swap(block, cross_perms[0])
        second = swap(block, cross_perms[1])
        current = choose(my_half, first, second, axis)
        for k in pair_bits:
            other = swap(current, pair_perms[k])
            current = choose((my_pair >> k) & 1, current, other, axis)
        return current

    def scatter_groups(total, axis):
        current = total
        for k in reversed(pair_bits):
            half = current.shape[axis] // 2
            bit = (my_pair >> k) & 1
            kept = lax.dynamic_slice_in_dim(current, bit * half, half, axis)
            sent = lax.dynamic_slice_in_dim(current, (1 - bit) * half, half, axis)
            arrived = swap(sent.astype(BF16), pair_perms[k])
            current = kept + arrived.astype(F32)
        half = current.shape[axis] // 2
        first = lax.dynamic_slice_in_dim(current, my_half * half, half, axis)
        second = lax.dynamic_slice_in_dim(current, (1 - my_half) * half, half, axis)
        first = swap(first.astype(BF16), turned(cross_perms[0]))
        second = swap(second.astype(BF16), turned(cross_perms[1]))
        return first.astype(F32) + second.astype(F32)

    listed = lax.dynamic_index_in_dim(
        token_order.reshape(group_count, micro_count, team_size, piece_len),
        member,
        2,
        keepdims=False,
    ).reshape(group_count, share_len)
    seat_listed = lax.dynamic_slice(
        token_order.reshape(group_count, micro_count, team_size, piece_len),
        (target, 0, seat, 0),
        (1, micro_count, 1, piece_len),
    ).reshape(share_len)
    start = (group * team_size + member) * share_len
    send_tokens, send_cotangent, send_map, take_map = run_deal(
        jnp.stack([start, group, target]).astype(jnp.int32),
        listed,
        seat_listed,
        tokens,
        cotangent,
        group_len,
    )

    def deal(rows):
        pieces = [
            swap(rows[e * quota_len : (e + 1) * quota_len], deal_perms[e])
            for e in range(group_count)
        ]
        return run_pick(take_map, jnp.concatenate(pieces, axis=0), False)

    def undeal(rows):
        pieces = [
            swap(rows[e * quota_len : (e + 1) * quota_len], turned(deal_perms[e]))
            for e in range(group_count)
        ]
        return run_pick(send_map, jnp.concatenate(pieces, axis=0), True)

    bounds = lax.ppermute(
        seq_lengths.astype(F32), ALL, cross_perms[0]
    ).astype(jnp.int32)
    bounds = jnp.cumsum(bounds, axis=1).astype(jnp.int32)
    live_ids = seq_lengths.shape[1] - 1

    def regroup(item):
        return swap(item, cross_perms[0])

    dealt_tokens = deal(send_tokens)
    full_rows = lax.all_gather(
        dealt_tokens.reshape(micro_count, piece_len, width_full), TEAM, axis=0
    )
    dealt_back = deal(send_cotangent)
    full_back = lax.all_gather(
        dealt_back.reshape(micro_count, piece_len, width_full), TEAM, axis=0
    )

    value_w = gather_groups(w_value, 0)
    gate_w = gather_groups(w_gate, 0)
    small_pad = -(pair_part + head_count) % 16
    small_own = jnp.concatenate(
        [w_pair.T, w_step.T, jnp.zeros((small_pad, w_pair.shape[0]), BF16)], axis=0
    )
    small_w = gather_groups(small_own, 1)
    pair_w = lax.all_gather(small_w[:pair_part], TEAM, axis=0, tiled=True)
    step_w = jnp.pad(
        small_w[pair_part : pair_part + head_count], ((0, LANES - head_count), (0, 0))
    )
    small_w = jnp.concatenate([pair_w, step_w], axis=0)
    out_w = gather_groups(w_out, 1)

    def pack_taps(taps, bias):
        return jnp.concatenate(
            [taps, bias[None, :], jnp.zeros((3, bias.shape[0]), F32)], axis=0
        )

    heads_own = jnp.pad(jnp.stack([step_bias, decay_log, skip_gain]), ((0, 5), (0, 0)))
    local_params = jnp.concatenate(
        [
            pack_taps(conv_value, bias_value),
            jnp.broadcast_to(norm_gate[None, :], (8, width)),
            jnp.pad(heads_own, ((0, 0), (0, width - head_count))),
            jnp.pad(pack_taps(conv_pair, bias_pair), ((0, 0), (0, width - pair_part))),
        ],
        axis=0,
    )
    local_params = regroup(local_params)
    taps_value = local_params[:8]
    norm_gate_row = local_params[8:9]
    heads_got = local_params[16:24, :head_count]
    skip_row = jnp.repeat(heads_got[2:3], head_width, axis=1)
    heads_row = jnp.pad(
        jnp.concatenate([heads_got[0:1], -jnp.exp(heads_got[1:2])], axis=0),
        ((0, 6), (0, LANES - head_count)),
    )
    taps_pair = lax.all_gather(local_params[24:32, :pair_part], TEAM, axis=1, tiled=True)

    consts = head_constants(head_count, head_width)
    weights = (
        norm_in[None, :],
        value_w,
        gate_w,
        small_w,
        taps_value,
        taps_pair,
        heads_row,
        skip_row,
        norm_gate_row,
        out_w,
    )
    outs = run_forward(bounds, full_rows, weights, consts)
    kept = outs[:9]
    partial_out, square = outs[9], outs[10]
    branch = lax.psum_scatter(partial_out, TEAM, scatter_dimension=0)
    normed, gate, scanned = kept[0], kept[1], kept[7]
    grad_normed, stats = run_back(
        bounds, full_back, out_w, norm_gate_row, scanned, gate, square, live_ids
    )
    stats = lax.psum(stats[:2], TEAM)
    stats_cols = jnp.pad(stats.T, ((0, 0), (0, 6)))
    low_gate, low_value, low_small, normed_out, grad_in, sums, sums_in = run_backward(
        bounds, stats_cols, grad_normed, kept, weights, consts, full_rows.shape, live_ids, inner_full
    )
    grad_in = lax.psum_scatter(grad_in, TEAM, scatter_dimension=0)

    flat_back = (
        jnp.swapaxes(full_back, 0, 1).reshape(micro_count * block_len, width_full)
    )
    g_out = scatter_groups(dot_tn(normed_out, flat_back), 1)
    g_gate = scatter_groups(dot_tn(normed, low_gate), 0)
    g_value = scatter_groups(dot_tn(normed, low_value), 0)
    g_small = dot_tn(low_small, normed)
    g_pair = lax.psum_scatter(
        g_small[:pair_width].astype(BF16), TEAM, scatter_dimension=0, tiled=True
    )
    g_small = jnp.concatenate(
        [
            g_pair.astype(F32),
            g_small[pair_width : pair_width + head_count],
            jnp.zeros((small_pad, width_full), F32),
        ],
        axis=0,
    )
    g_small = scatter_groups(g_small, 1)
    g_pair = g_small[:pair_part].T
    g_step = g_small[pair_part : pair_part + head_count].T

    sums_group = lax.psum(sums[:8], ("pair", "half"))
    sums_group = swap(sums_group, turned(cross_perms[0]))
    sums_team = lax.psum((sums[8:13, :pair_width], sums_in[0]), ALL)
    pair_sums = lax.dynamic_slice_in_dim(sums_team[0], member * pair_part, pair_part, 1)
    g_norm_in = sums_team[1] / norm_in.astype(F32)
    g_skip = jnp.sum(sums_group[6].reshape(head_count, head_width), axis=1)

    live_start = seat * piece_len
    local_stats = lax.dynamic_slice_in_dim(
        stats.reshape(2, micro_count, block_len)[0], live_start, piece_len, 1
    )
    local_places = live_start + jnp.arange(piece_len, dtype=jnp.int32)
    local_seg = jnp.sum(
        (local_places[None, :, None] >= bounds[:, None, :]).astype(jnp.int32), axis=2
    )
    weight = jnp.where(
        local_seg < live_ids, lax.rsqrt(local_stats / inner_full + EPS), 0.0
    ).reshape(share_len, 1)
    block_out = undeal(run_close(close_out_kernel, take_map, dealt_tokens, branch, weight))
    grad_tokens = undeal(
        run_close(
            close_back_kernel, take_map, dealt_tokens, dealt_back, grad_in, norm_in[None, :]
        )
    )
    return (
        block_out,
        grad_tokens,
        g_norm_in,
        g_gate,
        g_value,
        g_pair,
        g_step,
        sums_group[0:4],
        sums_group[4],
        pair_sums[0:4],
        pair_sums[4],
        sums_group[7, :head_count],
        sums_group[7, LANES : LANES + head_count],
        g_skip,
        sums_group[5],
        g_out,
    )


def solution(mesh):
    shape = mesh.devices.shape
    sizes = (shape[0] // 2, 2, shape[1], 2, shape[2] // 2)
    fine = jax.sharding.Mesh(mesh.devices.reshape(sizes), ALL)
    dp, team = ("pair", "core"), ("row", "half", "near")
    everything = ("pair", "core", "row", "half", "near")
    placed = (
        P(everything, None),
        P(everything, None),
        P(dp, None),
        P(),
        P(),
        P(dp, team),
        P(dp, team),
        P(dp, team),
        P(dp, team),
        P(None, team),
        P(team),
        P(None, team),
        P(team),
        P(team),
        P(team),
        P(team),
        P(team),
        P(team, dp),
    )
    return jax.shard_map(
        partial(per_device, sizes),
        mesh=fine,
        in_specs=placed,
        out_specs=(
            P(everything, None),
            P(everything, None),
            P(),
            P(dp, team),
            P(dp, team),
            P(dp, team),
            P(dp, team),
            P(None, team),
            P(team),
            P(None, team),
            P(team),
            P(team),
            P(team),
            P(team),
            P(team),
            P(team, dp),
        ),
        check_vma=False,
    )
```

```python
from functools import partial
from functools import reduce

import jax
import jax.numpy as jnp
import numpy as np
from jax import lax
from jax.experimental import pallas as pl
from jax.experimental.pallas import tpu as pltpu
from jax.sharding import PartitionSpec as P

EPS = 1e-05
EXACT = lax.Precision.HIGHEST
F32 = jnp.float32
BF16 = jnp.bfloat16
SUB = 128
ROWS = 256
LANES = 128
VMEM_BYTES = 56 * 1024 * 1024


def dot_nn(a, b):
    return jnp.dot(a, b, preferred_element_type=F32)


def dot_nt(a, b):
    return lax.dot_general(a, b, (((1,), (1,)), ((), ())), preferred_element_type=F32)


def dot_tn(a, b):
    return lax.dot_general(a, b, (((0,), (0,)), ((), ())), preferred_element_type=F32)


def sigmoid(v):
    return 1.0 / (1.0 + jnp.exp(-v))


def softplus(v):
    return jnp.maximum(v, 0.0) + jnp.log1p(jnp.exp(-jnp.abs(v)))


def split_two(v):
    high = v.astype(BF16)
    return high, (v - high.astype(F32)).astype(BF16)


def read_bounds(bounds_ref, micro):
    return [bounds_ref[micro, k] for k in range(bounds_ref.shape[1])]


def segment_of(places, bounds):
    total = (places >= bounds[0]).astype(jnp.int32)
    for bound in bounds[1:]:
        total = total + (places >= bound).astype(jnp.int32)
    return total


def segment_scalar(place, bounds):
    total = jnp.int32(0)
    for bound in bounds:
        total = total + jnp.where(place >= bound, 1, 0)
    return total


def iota(shape, axis):
    return lax.broadcasted_iota(jnp.int32, shape, axis)


def same_masks(places, bounds, count):
    own = segment_of(places, bounds)
    return [
        (segment_of(places - shift, bounds) == own) & (places >= shift) & (places < count)
        for shift in range(1, 4)
    ]


def expand_heads(parts, spread_ref):
    stacked = jnp.concatenate(parts, axis=0)
    high, low = split_two(stacked)
    lane = iota(stacked.shape, 1)
    joined = jnp.where(lane < 8, high.astype(F32), pltpu.roll(low.astype(F32), 8, 1))
    wide = dot_nn(joined.astype(BF16), spread_ref[...])
    sizes = np.cumsum([0] + [part.shape[0] for part in parts])
    return [wide[sizes[k] : sizes[k + 1]] for k in range(len(parts))]


def reduce_heads(v, gather_ref):
    high, low = split_two(v)
    return dot_nn(high, gather_ref[...]) + dot_nn(low, gather_ref[...])


def scan_frame(base, bounds, steps, rate, lower_ref):
    start_place = base
    col = start_place + iota((SUB, LANES), 0)
    row = start_place + iota((SUB, SUB), 1)
    seg_col = segment_of(col, bounds)
    seg_row = segment_of(row, bounds)
    allowed = (seg_col == seg_row) & (col >= row)
    last_seg = jnp.where(start_place > 0, segment_scalar(start_place - 1, bounds), -1)
    end_seg = segment_scalar(start_place + SUB - 1, bounds)
    log_decay = jnp.dot(
        lower_ref[...], steps * rate, preferred_element_type=F32, precision=EXACT
    )
    reach = jnp.where(seg_col == last_seg, jnp.exp(log_decay), 0.0)
    tail = jnp.where(
        seg_col == end_seg, jnp.exp(log_decay[SUB - 1 : SUB, :] - log_decay), 0.0
    )
    return allowed, log_decay, reach, tail


def decay_grid(log_decay, log_rows, head):
    gap = log_decay[:, head : head + 1] - log_rows[head : head + 1, :]
    return jnp.exp(jnp.minimum(gap, 0.0))


def forward_kernel(
    pair_count,
    bounds_ref,
    x_ref,
    norm_in_ref,
    w_value_ref,
    w_small_ref,
    taps_value_ref,
    taps_pair_ref,
    heads_ref,
    skip_ref,
    spread_ref,
    lower_ref,
    normed_ref,
    value_ref,
    conv_value_ref,
    pair_ref,
    conv_pair_ref,
    step_ref,
    scanned_ref,
    states_ref,
    halo_value,
    halo_pair,
    state,
):
    micro = pl.program_id(0)
    block = pl.program_id(1)
    count = pl.num_programs(1) * ROWS
    bounds = read_bounds(bounds_ref, micro)
    base = block * ROWS

    @pl.when(block == 0)
    def _():
        halo_value[...] = jnp.zeros_like(halo_value)
        halo_pair[...] = jnp.zeros_like(halo_pair)
        state[...] = jnp.zeros_like(state)

    x = x_ref[...].reshape(ROWS, x_ref.shape[-1]).astype(F32)
    rms = lax.rsqrt(jnp.mean(x * x, axis=1, keepdims=True) + EPS)
    normed = (x * rms * norm_in_ref[...].astype(F32)).astype(BF16)
    normed_ref[...] = normed
    value = dot_nn(normed, w_value_ref[...])
    small = dot_nt(normed, w_small_ref[...])
    pair_width = conv_pair_ref.shape[-1]
    pair = small[:, :pair_width]
    step = small[:, pair_width : pair_width + LANES]
    value_ref[...] = value
    pair_ref[...] = pair
    step_ref[...] = step

    places = base + iota((ROWS, LANES), 0)
    masks = same_masks(places, bounds, count)

    def convolve(v, halo, taps):
        longer = jnp.concatenate([halo, v], axis=0)
        width = v.shape[1]
        out = taps[4:5, :] + taps[3:4, :] * v
        for shift in range(1, 4):
            moved = pltpu.roll(longer, shift, 0)[8:, :]
            mask = jnp.concatenate([masks[shift - 1]] * (width // LANES), axis=1)
            out = out + jnp.where(mask, moved * taps[3 - shift : 4 - shift, :], 0.0)
        return out

    conv_value = convolve(value, halo_value[...], taps_value_ref[...])
    conv_pair = convolve(pair, halo_pair[...], taps_pair_ref[...])
    halo_value[...] = value[ROWS - 8 :, :]
    halo_pair[...] = pair[ROWS - 8 :, :]
    conv_value_ref[...] = conv_value
    conv_pair_ref[...] = conv_pair
    mixed = conv_value * sigmoid(conv_value)
    shared = (conv_pair * sigmoid(conv_pair)).astype(BF16)
    steps = softplus(step + heads_ref[0:1, :])
    rate = heads_ref[1:2, :]
    lane = iota((SUB, LANES), 1)
    left = lane < 64

    scanned_parts = []
    for sub in range(ROWS // SUB):
        rows = slice(sub * SUB, (sub + 1) * SUB)
        sub_steps = steps[rows]
        allowed, log_decay, reach, tail = scan_frame(
            base + sub * SUB, bounds, sub_steps, rate, lower_ref
        )
        steps_wide, reach_wide, tail_wide = expand_heads(
            [sub_steps, reach, tail], spread_ref
        )
        log_rows = log_decay.T
        keys = shared[rows, :LANES]
        reads = shared[rows, LANES:]
        scores = jnp.where(allowed, dot_nt(reads, keys), 0.0)
        stepped = mixed[rows] * steps_wide
        stepped_low = stepped.astype(BF16)
        held = state[...]
        states_ref[sub] = held
        outside = dot_nn(reads, held.astype(BF16)) * reach_wide
        inside = []
        for p in range(pair_count):
            cols = slice(p * LANES, (p + 1) * LANES)
            grids = [
                (scores * decay_grid(log_decay, log_rows, 2 * p + k)).astype(BF16)
                for k in range(2)
            ]
            both = stepped_low[:, cols]
            zero = jnp.zeros_like(both)
            inside.append(
                dot_nn(
                    jnp.concatenate(grids, axis=1),
                    jnp.concatenate(
                        [jnp.where(left, both, zero), jnp.where(left, zero, both)], axis=0
                    ),
                )
            )
        scanned_parts.append(
            jnp.concatenate(inside, axis=1) + outside + mixed[rows] * skip_ref[...]
        )
        state[...] = held * reach_wide[SUB - 1 : SUB, :] + dot_tn(
            keys, (stepped * tail_wide).astype(BF16)
        )
    scanned_ref[...] = jnp.concatenate(scanned_parts, axis=0)


def back_kernel(
    live_ids,
    bounds_ref,
    back_ref,
    normed_ref,
    w_gate_ref,
    w_out_ref,
    norm_gate_ref,
    scanned_ref,
    gate_ref,
    scaled_ref,
    grad_normed_ref,
    stats_ref,
):
    micro = pl.program_id(0)
    bounds = read_bounds(bounds_ref, micro)
    base = pl.program_id(1) * ROWS
    places = base + iota((ROWS, LANES), 0)
    live = segment_of(places, bounds) < live_ids
    gate = dot_nn(normed_ref[...], w_gate_ref[...])
    gate_ref[...] = gate
    gated = scanned_ref[...] * (gate * sigmoid(gate))
    normed_gated = gated * norm_gate_ref[...]
    scaled_ref[...] = normed_gated.astype(BF16).reshape(scaled_ref.shape)
    grad = dot_nn(back_ref[...].reshape(ROWS, back_ref.shape[-1]), w_out_ref[...])
    live_wide = jnp.concatenate([live] * (grad.shape[1] // LANES), axis=1)
    grad = jnp.where(live_wide, grad, 0.0)
    grad_normed_ref[...] = grad
    ones = jnp.ones((8, gated.shape[1]), BF16)
    high, low = split_two(gated * gated)
    square = dot_nt(ones, high) + dot_nt(ones, low)
    high, low = split_two(grad * normed_gated)
    cross = dot_nt(ones, high) + dot_nt(ones, low)
    stats_ref[...] = jnp.where(iota(cross.shape, 0) == 0, square, cross)


def gate_kernel(
    live_ids,
    inner_full,
    bounds_ref,
    stats_ref,
    grad_normed_ref,
    gate_ref,
    scanned_ref,
    norm_gate_ref,
    low_gate_ref,
    normed_out_ref,
    grad_scanned_ref,
    sums_ref,
):
    micro = pl.program_id(0)
    block = pl.program_id(1)
    bounds = read_bounds(bounds_ref, micro)

    @pl.when((micro == 0) & (block == 0))
    def _():
        sums_ref[...] = jnp.zeros_like(sums_ref)

    tiles = gate_ref.shape[1] // LANES
    live = segment_of(block * ROWS + iota((ROWS, LANES), 0), bounds) < live_ids
    gate = gate_ref[...]
    scanned = scanned_ref[...]
    grad_normed = grad_normed_ref[...]
    norm_gate = norm_gate_ref[...]
    stats = stats_ref[...].T / inner_full
    spread = lax.rsqrt(stats[:, 0:1] + EPS)
    cross = stats[:, 1:2]
    sg = sigmoid(gate)
    act = gate * sg
    gated = scanned * act
    normed_gated = gated * spread
    live_wide = jnp.concatenate([live] * tiles, axis=1)
    normed_out = jnp.where(live_wide, normed_gated * norm_gate, 0.0).astype(BF16)
    normed_out_ref[...] = normed_out.reshape(normed_out_ref.shape)
    grad_gated = spread * (grad_normed * norm_gate - normed_gated * (spread * cross))
    grad_scanned_ref[...] = grad_gated * act
    low_gate_ref[...] = (
        grad_gated * scanned * (sg * (1.0 + gate * (1.0 - sg)))
    ).astype(BF16)
    sums_ref[0:1, :] += jnp.sum(grad_normed * normed_gated, axis=0, keepdims=True)


def backward_kernel(
    pair_count,
    micro,
    first,
    apart,
    bounds_ref,
    grad_scanned_ref,
    low_gate_ref,
    normed_ref,
    value_ref,
    conv_value_ref,
    pair_ref,
    conv_pair_ref,
    step_ref,
    scanned_ref,
    states_ref,
    w_value_ref,
    w_gate_ref,
    w_small_ref,
    taps_value_ref,
    taps_pair_ref,
    heads_ref,
    skip_ref,
    spread_ref,
    gather_ref,
    lower_ref,
    upper_ref,
    *rest,
):
    if not first:
        rest = rest[2:]
    (
        low_value_ref,
        low_small_ref,
        *grad_in_refs,
        sums_ref,
        sums_in_ref,
        halo_value,
        halo_pair,
        state,
    ) = rest
    turn = pl.program_id(0)
    block_count = pl.num_programs(0)
    block = block_count - 1 - turn
    count = block_count * ROWS
    bounds = read_bounds(bounds_ref, micro)
    base = block * ROWS

    @pl.when(turn == 0)
    def _():
        sums_ref[...] = jnp.zeros_like(sums_ref)
        sums_in_ref[...] = jnp.zeros_like(sums_in_ref)
        halo_value[...] = jnp.zeros_like(halo_value)
        halo_pair[...] = jnp.zeros_like(halo_pair)
        state[...] = jnp.zeros_like(state)

    width = value_ref.shape[1]
    scanned = scanned_ref[...]
    grad_scanned = grad_scanned_ref[...]
    low_gate = low_gate_ref[...]

    conv_value = conv_value_ref[...]
    sig_value = sigmoid(conv_value)
    mixed = conv_value * sig_value
    conv_pair = conv_pair_ref[...]
    sig_pair = sigmoid(conv_pair)
    shared = (conv_pair * sig_pair).astype(BF16)
    step_in = step_ref[...] + heads_ref[0:1, :]
    steps = softplus(step_in)
    rate = heads_ref[1:2, :]
    skip = skip_ref[...]
    lane = iota((SUB, LANES), 1)
    left = lane < 64

    grad_mixed_parts = []
    grad_shared_parts = []
    grad_step_parts = []
    decay_sum = jnp.zeros((1, LANES), F32)
    for sub in reversed(range(ROWS // SUB)):
        rows = slice(sub * SUB, (sub + 1) * SUB)
        sub_steps = steps[rows]
        allowed, log_decay, reach, tail = scan_frame(
            base + sub * SUB, bounds, sub_steps, rate, lower_ref
        )
        steps_wide, reach_wide, tail_wide = expand_heads(
            [sub_steps, reach, tail], spread_ref
        )
        log_rows = log_decay.T
        keys = shared[rows, :LANES]
        reads = shared[rows, LANES:]
        scores = jnp.where(allowed, dot_nt(reads, keys), 0.0)
        sub_mixed = mixed[rows]
        stepped = sub_mixed * steps_wide
        stepped_low = stepped.astype(BF16)
        grad_y = grad_scanned[rows]
        grad_low = grad_y.astype(BF16)
        held = states_ref[sub]
        later = state[...]
        later_low = later.astype(BF16)
        grad_scores = jnp.zeros((SUB, SUB), F32)
        inner = []
        for p in range(pair_count):
            cols = slice(p * LANES, (p + 1) * LANES)
            both_x = stepped_low[:, cols]
            both_y = grad_low[:, cols]
            zero = jnp.zeros_like(both_y)
            halves = [jnp.where(left, both_y, zero), jnp.where(left, zero, both_y)]
            grids = []
            for k in range(2):
                fade = decay_grid(log_decay, log_rows, 2 * p + k)
                grids.append((scores * fade).astype(BF16))
                grad_scores = grad_scores + dot_nt(halves[k], both_x) * fade
            inner.append(
                dot_tn(jnp.concatenate(grids, axis=0), jnp.concatenate(halves, axis=0))
            )
        grad_scores = jnp.where(allowed, grad_scores, 0.0).astype(BF16)
        tail_part = tail_wide * dot_nn(keys, later_low)
        grad_stepped = jnp.concatenate(inner, axis=1) + tail_part
        reached = (grad_y * reach_wide).astype(BF16)
        tailed = (stepped * tail_wide).astype(BF16)
        grad_reads = dot_nn(grad_scores, keys) + dot_nt(reached, held.astype(BF16))
        grad_keys = dot_tn(grad_scores, reads) + dot_nt(tailed, later_low)
        stepped_back = stepped_low.astype(F32)
        per_log = reduce_heads(
            grad_low.astype(F32) * (scanned[rows] - skip * sub_mixed)
            - stepped_back * grad_stepped,
            gather_ref,
        )
        kept_wide = reach_wide[SUB - 1 : SUB, :]
        at_end = jnp.sum(stepped_back * tail_part, axis=0, keepdims=True) + kept_wide * jnp.sum(
            later * held, axis=0, keepdims=True
        )
        at_end = reduce_heads(jnp.broadcast_to(at_end, (8, width)), gather_ref)[0:1, :]
        grad_log = (
            jnp.dot(upper_ref[...], per_log, preferred_element_type=F32, precision=EXACT)
            + at_end
        )
        decay_sum = decay_sum + jnp.sum(grad_log * sub_steps, axis=0, keepdims=True) * rate
        grad_steps = reduce_heads(grad_stepped * sub_mixed, gather_ref) + rate * grad_log
        grad_step_parts.insert(0, grad_steps)
        grad_shared_parts.insert(0, jnp.concatenate([grad_keys, grad_reads], axis=1))
        grad_mixed_parts.insert(0, grad_stepped * steps_wide + skip * grad_y)
        state[...] = later * kept_wide + dot_tn(reads, reached)
    grad_mixed = jnp.concatenate(grad_mixed_parts, axis=0)
    grad_shared = jnp.concatenate(grad_shared_parts, axis=0)
    grad_step = jnp.concatenate(grad_step_parts, axis=0) * sigmoid(step_in)

    longer_places = base + iota((ROWS + 8, LANES), 0)
    masks = same_masks(longer_places, bounds, count)

    def convolve_back(q, halo, v, taps):
        longer = jnp.concatenate([q, halo], axis=0)
        grad = taps[3:4, :] * q
        tap_sums = [jnp.sum(v * q, axis=0, keepdims=True)]
        for shift in range(1, 4):
            mask = jnp.concatenate([masks[shift - 1]] * (q.shape[1] // LANES), axis=1)
            kept = jnp.where(mask, longer, 0.0)
            moved = pltpu.roll(kept, ROWS + 8 - shift, 0)[:ROWS, :]
            grad = grad + taps[3 - shift : 4 - shift, :] * moved
            tap_sums.insert(0, jnp.sum(v * moved, axis=0, keepdims=True))
        return grad, tap_sums + [jnp.sum(q, axis=0, keepdims=True)]

    q_value = grad_mixed * (sig_value * (1.0 + conv_value * (1.0 - sig_value)))
    q_pair = grad_shared * (sig_pair * (1.0 + conv_pair * (1.0 - sig_pair)))
    grad_value, value_sums = convolve_back(
        q_value, halo_value[...], value_ref[...], taps_value_ref[...]
    )
    grad_pair, pair_sums = convolve_back(
        q_pair, halo_pair[...], pair_ref[...], taps_pair_ref[...]
    )
    halo_value[...] = q_value[:8, :]
    halo_pair[...] = q_pair[:8, :]
    low_value = grad_value.astype(BF16)
    low_small = jnp.concatenate([grad_pair, grad_step], axis=1).astype(BF16)
    low_value_ref[...] = low_value
    low_small_ref[...] = low_small
    grad_in = (
        dot_nt(low_gate, w_gate_ref[...])
        + dot_nt(low_value, w_value_ref[...])
        + dot_nn(low_small, w_small_ref[...])
    )
    grad_in_low = grad_in.astype(BF16).reshape(grad_in_refs[0].shape)
    if apart:
        mine = block % 2 == bounds_ref[bounds_ref.shape[0] - 1, 0]

        @pl.when(mine)
        def _():
            grad_in_refs[0][...] = grad_in_low

        @pl.when(jnp.logical_not(mine))
        def _():
            grad_in_refs[1][...] = grad_in_low

    else:
        grad_in_refs[0][...] = grad_in_low
    sums_in_ref[0:1, :] += jnp.sum(grad_in * normed_ref[...].astype(F32), axis=0, keepdims=True)
    skip_sum = jnp.sum(grad_scanned * mixed, axis=0, keepdims=True)
    step_sum = jnp.sum(grad_step, axis=0, keepdims=True)
    for k in range(5):
        sums_ref[k : k + 1, :] += value_sums[k]
    sums_ref[6:7, :] += skip_sum
    sums_ref[7:8, :LANES] += step_sum
    sums_ref[7:8, LANES : 2 * LANES] += decay_sum
    for k in range(5):
        sums_ref[8 + k : 9 + k, : pair_sums[k].shape[1]] += pair_sums[k]


def whole_spec(shape):
    return pl.BlockSpec(shape, lambda *_: (0,) * len(shape))


def smem_spec():
    return pl.BlockSpec(memory_space=pltpu.SMEM)


def kernel_params():
    return pltpu.CompilerParams(vmem_limit_bytes=VMEM_BYTES)


def head_constants(head_count, head_width):
    width = head_count * head_width
    spread = np.zeros((LANES, width), np.float32)
    for h in range(head_count):
        spread[h, h * head_width : (h + 1) * head_width] = 1.0
        spread[h + 8, h * head_width : (h + 1) * head_width] = 1.0
    gather = np.zeros((width, LANES), np.float32)
    for h in range(head_count):
        gather[h * head_width : (h + 1) * head_width, h] = 1.0
    lower = np.tril(np.ones((SUB, SUB), np.float32))
    return (
        jnp.asarray(spread, BF16),
        jnp.asarray(gather, BF16),
        jnp.asarray(lower),
        jnp.asarray(lower.T),
    )


def seat_spec(piece, cols):
    return pl.BlockSpec((None, 2, None, piece, cols), lambda b, i: (i // 2, 0, i % 2, b, 0))


def seat_view(item):
    return item.reshape((item.shape[0] // 4, 2, 2) + item.shape[1:])


def cost(flops, count, moved):
    return pl.CostEstimate(flops=int(flops), transcendentals=int(count), bytes_accessed=int(moved))


def run_forward(bounds, rows, weights, consts, micro_count, piece):
    block_len = 8 * piece
    blocks = block_len // ROWS
    norm_in, w_value, _, w_small, taps_value, taps_pair, heads, skip = weights
    spread, _, lower, _ = consts
    full = rows.shape[4]
    width = w_value.shape[1]
    pair_width = taps_pair.shape[1]
    length = micro_count * block_len
    subs = ROWS // SUB

    def by_rows(cols):
        return pl.BlockSpec((ROWS, cols), lambda b, i: (b * blocks + i, 0))

    wholes = [norm_in, w_value, w_small, taps_value, taps_pair, heads, skip, spread, lower]
    widths = [width, width, pair_width, pair_width, LANES, width]
    return pl.pallas_call(
        partial(forward_kernel, width // LANES),
        grid=(micro_count, blocks),
        in_specs=[smem_spec(), seat_spec(piece, full)] + [whole_spec(item.shape) for item in wholes],
        out_specs=[by_rows(full)]
        + [by_rows(cols) for cols in widths]
        + [
            pl.BlockSpec((subs, LANES, width), lambda b, i: (b * blocks + i, 0, 0)),
        ],
        out_shape=[jax.ShapeDtypeStruct((length, full), BF16)]
        + [jax.ShapeDtypeStruct((length, cols), F32) for cols in widths]
        + [
            jax.ShapeDtypeStruct((length // SUB, LANES, width), F32),
        ],
        scratch_shapes=[
            pltpu.VMEM((8, width), F32),
            pltpu.VMEM((8, pair_width), F32),
            pltpu.VMEM((LANES, width), F32),
        ],
        compiler_params=kernel_params(),
        cost_estimate=cost(length * full * width * 12, length * width * 8, length * width * 40),
        name="forward",
    )(bounds, rows, *wholes)


def run_back(bounds, back, normed, w_gate, w_out, norm_gate, scanned, live_ids, micro_count, piece):
    block_len = 8 * piece
    blocks = block_len // ROWS
    length, width = scanned.shape
    full = normed.shape[1]

    def by_rows(cols):
        return pl.BlockSpec((ROWS, cols), lambda b, i: (b * blocks + i, 0))

    by_cols = pl.BlockSpec((8, ROWS), lambda b, i: (0, b * blocks + i))
    return pl.pallas_call(
        partial(back_kernel, live_ids),
        grid=(micro_count, blocks),
        in_specs=[
            smem_spec(),
            seat_spec(piece, full),
            by_rows(full),
            whole_spec(w_gate.shape),
            whole_spec(w_out.shape),
            whole_spec(norm_gate.shape),
            by_rows(width),
        ],
        out_specs=[by_rows(width), seat_spec(piece, width), by_rows(width), by_cols],
        out_shape=[
            jax.ShapeDtypeStruct((length, width), F32),
            jax.ShapeDtypeStruct(back.shape[:4] + (width,), BF16),
            jax.ShapeDtypeStruct((length, width), F32),
            jax.ShapeDtypeStruct((8, length), F32),
        ],
        compiler_params=kernel_params(),
        cost_estimate=cost(length * full * width * 4, length * width, length * width * 30),
        name="back",
    )(bounds, back, normed, w_gate, w_out, norm_gate, scanned)


def run_gate(bounds, stats, grad_normed, gate, scanned, norm_gate, live_ids, inner_full, micro_count, piece):
    block_len = 8 * piece
    blocks = block_len // ROWS
    length, width = gate.shape
    by_rows = pl.BlockSpec((ROWS, width), lambda b, i: (b * blocks + i, 0))
    return pl.pallas_call(
        partial(gate_kernel, live_ids, inner_full),
        grid=(micro_count, blocks),
        in_specs=[
            smem_spec(),
            pl.BlockSpec((8, ROWS), lambda b, i: (0, b * blocks + i)),
            by_rows,
            by_rows,
            by_rows,
            whole_spec(norm_gate.shape),
        ],
        out_specs=[
            by_rows,
            seat_spec(piece, width),
            by_rows,
            whole_spec((8, width)),
        ],
        out_shape=[
            jax.ShapeDtypeStruct((length, width), BF16),
            jax.ShapeDtypeStruct((blocks // 2, 2, 2, micro_count * piece, width), BF16),
            jax.ShapeDtypeStruct((length, width), F32),
            jax.ShapeDtypeStruct((8, width), F32),
        ],
        compiler_params=kernel_params(),
        cost_estimate=cost(length * width * 20, length * width, length * width * 20),
        name="gate",
    )(bounds, stats, grad_normed, gate, scanned, norm_gate)


def run_backward(bounds, grad_scanned, low_gate, kept, weights, consts, micro, piece, earlier, apart):
    block_len = 8 * piece
    blocks = block_len // ROWS
    normed, value, conv_value, pair, conv_pair, step, scanned, states = kept
    _, w_value, w_gate, w_small, taps_value, taps_pair, heads, skip = weights
    spread, gather, lower, upper = consts
    full = normed.shape[1]
    length, width = value.shape
    pair_width = pair.shape[1]
    subs = ROWS // SUB

    def place(i):
        return micro * blocks + blocks - 1 - i

    def by_rows(item):
        return pl.BlockSpec((ROWS, item.shape[1]), lambda i: (place(i), 0))

    if apart:
        row_blocks = [
            pl.BlockSpec((None, 2, piece, full), lambda i: ((blocks - 1 - i) // 2, 0, 0, 0))
        ] * 2
        row_shapes = [jax.ShapeDtypeStruct((blocks // 2, 2, piece, full), BF16)] * 2
    else:
        row_blocks = [
            pl.BlockSpec(
                (None, 2, None, piece, full),
                lambda i: ((blocks - 1 - i) // 2, 0, (blocks - 1 - i) % 2, 0, 0),
            )
        ]
        row_shapes = [jax.ShapeDtypeStruct((blocks // 2, 2, 2, piece, full), BF16)]
    rowwise = [grad_scanned, low_gate, normed, value, conv_value, pair, conv_pair, step, scanned]
    wholes = [w_value, w_gate, w_small, taps_value, taps_pair, heads, skip, spread, gather, lower, upper]
    outs = [
        jax.ShapeDtypeStruct((length, width), BF16),
        jax.ShapeDtypeStruct((length, w_small.shape[0]), BF16),
        *row_shapes,
        jax.ShapeDtypeStruct((16, width), F32),
        jax.ShapeDtypeStruct((8, full), F32),
    ]
    ins = [bounds] + rowwise + [states] + wholes
    return pl.pallas_call(
        partial(backward_kernel, width // LANES, micro, earlier is None, apart),
        grid=(blocks,),
        in_specs=[smem_spec()]
        + [by_rows(item) for item in rowwise]
        + [pl.BlockSpec((subs, LANES, width), lambda i: (place(i), 0, 0))]
        + [whole_spec(item.shape) for item in wholes]
        + ([] if earlier is None else [pl.BlockSpec(memory_space=pl.ANY)] * 2),
        out_specs=[by_rows(item) for item in outs[:2]]
        + row_blocks
        + [whole_spec(item.shape) for item in outs[-2:]],
        out_shape=outs,
        input_output_aliases={} if earlier is None else {len(ins): 0, len(ins) + 1: 1},
        scratch_shapes=[
            pltpu.VMEM((8, width), F32),
            pltpu.VMEM((8, pair_width), F32),
            pltpu.VMEM((LANES, width), F32),
        ],
        compiler_params=kernel_params(),
        cost_estimate=cost(block_len * full * width * 14, block_len * width * 16, block_len * width * 40),
        name="backward",
    )(*ins, *([] if earlier is None else earlier))


def deal_kernel(
    group_shift,
    place_ref,
    listed_ref,
    listed_cols_ref,
    own_ref,
    own_col_ref,
    tokens_ref,
    cotangent_ref,
    send_tokens_ref,
    send_cotangent_ref,
    send_map_ref,
    take_map_ref,
):
    start, group, target = place_ref[0], place_ref[1], place_ref[2]
    share = tokens_ref.shape[0]
    group_count = listed_cols_ref.shape[1]
    quota = share // group_count
    natural = start + iota((share, share), 1)
    found = []
    for g in range(group_count):
        hits = (listed_cols_ref[:, g : g + 1] == natural).astype(F32)
        found.append(jnp.sum(hits, axis=0, keepdims=True))
    pad = -group_count % 8
    found = jnp.concatenate(found + [jnp.zeros((pad, share), F32)] * (pad > 0), axis=0)
    before = (iota((share, share), 0) < iota((share, share), 1)).astype(BF16)
    rank = dot_nn(found.astype(BF16), before)
    slot = (iota(found.shape, 0) ^ group) * quota
    place = jnp.sum(found * (rank + slot.astype(F32)), axis=0, keepdims=True)
    send_map = (iota((share, share), 0).astype(F32) == place).astype(BF16)
    send_map_ref[...] = send_map
    own_row = jnp.broadcast_to(own_ref[...], (share, share))
    own_col = jnp.broadcast_to(own_col_ref[...], (share, share))
    src_row = lax.shift_right_logical(own_row, group_shift)
    src_col = lax.shift_right_logical(own_col, group_shift)
    ahead = ((src_row == src_col) & (own_row < own_col)).astype(F32)
    order = jnp.sum(ahead, axis=1, keepdims=True)
    wanted = ((src_col ^ target) * quota).astype(F32) + order
    take_map_ref[...] = (iota((share, share), 1).astype(F32) == wanted).astype(BF16)
    send_tokens_ref[...] = dot_nn(send_map, tokens_ref[...]).astype(BF16)
    send_cotangent_ref[...] = dot_nn(send_map, cotangent_ref[...]).astype(BF16)


def run_deal(place, listed, own, tokens, cotangent, group_len):
    share, width = tokens.shape
    vmem = pl.BlockSpec(memory_space=pltpu.VMEM)
    return pl.pallas_call(
        partial(deal_kernel, group_len.bit_length() - 1),
        in_specs=[smem_spec()] + [vmem] * 6,
        out_specs=[vmem] * 4,
        out_shape=[jax.ShapeDtypeStruct((share, width), BF16)] * 2
        + [jax.ShapeDtypeStruct((share, share), BF16)] * 2,
        compiler_params=kernel_params(),
        name="deal",
    )(place, listed, listed.T, own[None, :], own[:, None], tokens, cotangent)


def pick_kernel(transposed, map_ref, rows_ref, out_ref):
    dot = dot_tn if transposed else dot_nn
    out_ref[...] = dot(map_ref[...], rows_ref[...]).astype(BF16)


def run_pick(take_map, rows, transposed):
    vmem = pl.BlockSpec(memory_space=pltpu.VMEM)
    return pl.pallas_call(
        partial(pick_kernel, transposed),
        in_specs=[vmem] * 2,
        out_specs=vmem,
        out_shape=jax.ShapeDtypeStruct((take_map.shape[0], rows.shape[1]), BF16),
        compiler_params=kernel_params(),
        name="pick",
    )(take_map, rows)


def close_out_kernel(map_ref, dealt_ref, branch_ref, weight_ref, out_ref):
    shape = dealt_ref.shape
    out = dealt_ref[...].astype(F32) + weight_ref[...] * branch_ref[...].reshape(shape).astype(F32)
    out_ref[...] = dot_tn(map_ref[...], out.astype(BF16)).astype(BF16)


def close_back_kernel(map_ref, dealt_ref, back_ref, norm_in_ref, *refs):
    grad_refs, out_ref = refs[:-1], refs[-1]
    x = dealt_ref[...].astype(F32)
    rms = lax.rsqrt(jnp.mean(x * x, axis=1, keepdims=True) + EPS)
    xhat = x * rms
    grad = jnp.concatenate([item[...].astype(F32) for item in grad_refs], axis=0)
    win = grad * norm_in_ref[...].astype(F32)
    cross = jnp.mean(win * xhat, axis=1, keepdims=True)
    out = back_ref[...].astype(F32) + rms * (win - xhat * cross)
    out_ref[...] = dot_tn(map_ref[...], out.astype(BF16)).astype(BF16)


def run_close(body, take_map, *items):
    vmem = pl.BlockSpec(memory_space=pltpu.VMEM)
    return pl.pallas_call(
        body,
        in_specs=[vmem] * (1 + len(items)),
        out_specs=vmem,
        out_shape=jax.ShapeDtypeStruct(items[0].shape, BF16),
        compiler_params=kernel_params(),
        name="close",
    )(take_map, *items)


ALL = ("pair", "core", "row", "half", "near")
TEAM = ("row", "near", "core")


def make_perm(sizes, move):
    ranks = np.arange(int(np.prod(sizes))).reshape(sizes)
    return [
        (int(ranks[where]), int(ranks[move(*where)])) for where in np.ndindex(*sizes)
    ]


def turned(perm):
    return [(target, source) for source, target in perm]


def swap(v, perm):
    return lax.ppermute(v, ALL, perm)


def choose(bit, first, second, axis):
    return jnp.where(
        bit == 0,
        jnp.concatenate([first, second], axis=axis),
        jnp.concatenate([second, first], axis=axis),
    )


def per_device(
    sizes,
    tokens,
    cotangent,
    seq_lengths,
    token_order,
    norm_in,
    w_gate,
    w_value,
    w_pair,
    w_step,
    conv_value,
    bias_value,
    conv_pair,
    bias_pair,
    step_bias,
    decay_log,
    skip_gain,
    norm_gate,
    w_out,
):
    pair_count = sizes[0]
    group_count = sizes[0] * sizes[1]
    team_size = sizes[2] * sizes[3] * sizes[4]
    my_pair, my_core, my_row, my_half, my_near = [lax.axis_index(name) for name in ALL]
    group = my_pair * 2 + my_core
    target = my_pair * 2 + my_half
    member = my_row * (sizes[3] * sizes[4]) + my_half * sizes[4] + my_near
    seat = my_row * (sizes[3] * sizes[4]) + my_core * sizes[4] + my_near

    share_len, width_full = tokens.shape
    quota_len = share_len // group_count
    micro_count = seq_lengths.shape[0]
    piece_len = share_len // micro_count
    block_len = piece_len * team_size
    group_len = share_len * team_size
    width = w_gate.shape[1]
    inner_full = width * team_size
    head_count = step_bias.shape[0]
    head_width = width // head_count
    pair_part = w_pair.shape[1]
    pair_width = pair_part * team_size
    small_width = pair_width + LANES

    deal_perms = [
        make_perm(
            sizes,
            lambda p, c, r, h, n, e=e: (p ^ (e // 2), h, r, c ^ (e % 2), n),
        )
        for e in range(group_count)
    ]
    cross_perms = [
        make_perm(sizes, lambda p, c, r, h, n, f=f: (p, h, r, c ^ f, n)) for f in range(2)
    ]
    pair_bits = [k for k in range(pair_count.bit_length() - 1)]
    pair_perms = [
        make_perm(sizes, lambda p, c, r, h, n, k=k: (p ^ (1 << k), c, r, h, n))
        for k in pair_bits
    ]

    team_perms = {
        "core": make_perm(sizes, lambda p, c, r, h, n: (p, 1 - c, r, h, n)),
        "near": make_perm(sizes, lambda p, c, r, h, n: (p, c, r, h, 1 - n)),
        "row": make_perm(sizes, lambda p, c, r, h, n: (p, c, 1 - r, h, n)),
    }

    def after(v, *others):
        return lax.optimization_barrier((v,) + others)[0]

    def cross_groups(block):
        return swap(block, cross_perms[0]), swap(block, cross_perms[1])

    def gather_groups(crossed, axis):
        first, second = crossed
        current = choose(my_half, first, second, axis)
        for k in pair_bits:
            other = swap(current, pair_perms[k])
            current = choose((my_pair >> k) & 1, current, other, axis)
        return current

    def scatter_groups(current, sums=None, split=None, join=None, waits=(), ends=()):
        def pack(v):
            v = v.astype(BF16)
            if sums is None:
                return v
            rows = split(sums)
            rows = jnp.broadcast_to(rows, v.shape[:-2] + rows.shape)
            return jnp.concatenate([v, rows], axis=-2)

        length = current.shape[-2]

        def unpack(v, total):
            if total is None:
                return v.astype(F32), None
            first = v if v.ndim == 2 else v[0]
            return v[..., :length, :].astype(F32), total + join(
                first[length:], total.shape[0]
            )

        for k in reversed(pair_bits):
            half = current.shape[0] // 2
            bit = (my_pair >> k) & 1
            kept = lax.dynamic_slice_in_dim(current, bit * half, half, 0)
            sent = lax.dynamic_slice_in_dim(current, (1 - bit) * half, half, 0)
            arrived = after(swap(pack(sent), pair_perms[k]), *waits)
            arrived, sums = unpack(arrived, sums)
            current = kept + arrived
        first = lax.dynamic_index_in_dim(current, my_half, 0, keepdims=False)
        second = lax.dynamic_index_in_dim(current, 1 - my_half, 0, keepdims=False)
        first = after(swap(pack(first), turned(cross_perms[0])), *ends)
        second = after(swap(pack(second), turned(cross_perms[1])), *ends)
        if sums is None:
            return first.astype(F32) + second.astype(F32)
        zero = jnp.zeros_like(sums)
        first, sums_first = unpack(first, zero)
        second, sums_second = unpack(second, zero)
        return first + second, sums_first + sums_second

    listed = lax.dynamic_index_in_dim(
        token_order.reshape(group_count, micro_count, team_size, piece_len),
        member,
        2,
        keepdims=False,
    ).reshape(group_count, share_len)
    seat_listed = lax.dynamic_slice(
        token_order.reshape(group_count, micro_count, team_size, piece_len),
        (target, 0, seat, 0),
        (1, micro_count, 1, piece_len),
    ).reshape(share_len)
    start = (group * team_size + member) * share_len
    send_tokens, send_cotangent, send_map, take_map = run_deal(
        jnp.stack([start, group, target]).astype(jnp.int32),
        listed,
        seat_listed,
        tokens,
        cotangent,
        group_len,
    )

    def deal_pieces(rows):
        return [
            swap(rows[e * quota_len : (e + 1) * quota_len], deal_perms[e])
            for e in range(group_count)
        ]

    def undeal(rows, *waits):
        pieces = [
            swap(rows[e * quota_len : (e + 1) * quota_len], turned(deal_perms[e]))
            for e in range(group_count)
        ]
        pieces = [after(piece, *waits) for piece in pieces]
        return run_pick(send_map, jnp.concatenate(pieces, axis=0), True)

    def exchange(v, axis_name):
        return swap(v, team_perms[axis_name])

    def sum_over(v, names):
        for name in names:
            v = v + exchange(v, name)
        return v

    def pack_taps(taps, bias):
        return jnp.concatenate(
            [taps, bias[None, :], jnp.zeros((3, bias.shape[0]), F32)], axis=0
        )

    heads_own = jnp.pad(jnp.stack([step_bias, decay_log, skip_gain]), ((0, 5), (0, 0)))
    lengths_own = jnp.pad(
        seq_lengths.astype(F32),
        ((0, 8 - micro_count), (0, width - seq_lengths.shape[1])),
    )
    local_params = jnp.concatenate(
        [
            pack_taps(conv_value, bias_value),
            jnp.broadcast_to(norm_gate[None, :], (8, width)),
            jnp.pad(heads_own, ((0, 0), (0, width - head_count))),
            jnp.pad(pack_taps(conv_pair, bias_pair), ((0, 0), (0, width - pair_part))),
            lengths_own,
        ],
        axis=0,
    )
    local_params = swap(after(local_params, send_tokens), cross_perms[0])
    taps_value = local_params[:8]
    norm_gate_row = local_params[8:9]
    heads_got = local_params[16:24, :head_count]
    own_taps = local_params[24:32, :pair_part]
    live_ids = seq_lengths.shape[1] - 1
    bounds = jnp.cumsum(
        local_params[32 : 32 + micro_count, : live_ids + 1].astype(jnp.int32), axis=1
    )
    skip_row = jnp.repeat(heads_got[2:3], head_width, axis=1)
    heads_row = jnp.pad(
        jnp.concatenate([heads_got[0:1], -jnp.exp(heads_got[1:2])], axis=0),
        ((0, 6), (0, LANES - head_count)),
    )
    tap_high = lax.reduce_precision(own_taps, 8, 7)
    tap_mid = lax.reduce_precision(own_taps - tap_high, 8, 7)
    tap_low = own_taps - tap_high - tap_mid
    tap_row = jnp.stack([tap_high, tap_mid, tap_low]).astype(BF16).reshape(1, -1)
    tap_count = tap_row.shape[1]

    small_pad = -(pair_part + head_count) % 16
    small_own = jnp.concatenate(
        [w_pair.T, w_step.T, jnp.zeros((small_pad, w_pair.shape[0]), BF16)], axis=0
    )
    small_w = gather_groups(cross_groups(after(small_own, send_tokens)), 1)

    pieces = deal_pieces(send_tokens)
    dealt_tokens = run_pick(take_map, jnp.concatenate(pieces, axis=0), False)
    full_rows = seat_view(
        lax.all_gather(
            jnp.concatenate(
                [
                    dealt_tokens,
                    small_w[:pair_part],
                    jnp.pad(tap_row, ((0, 15), (0, width_full - tap_count))),
                ],
                axis=0,
            ),
            TEAM,
            axis=0,
        )
    )
    value_w = cross_groups(after(w_value, *pieces))
    pieces = deal_pieces(after(send_cotangent, *value_w))
    value_w = gather_groups(value_w, 0)
    dealt_back = run_pick(take_map, jnp.concatenate(pieces, axis=0), False)
    full_back = seat_view(lax.all_gather(dealt_back, TEAM, axis=0))
    later_w = cross_groups(after(jnp.stack([w_gate, w_out.T]), *pieces))
    full_rows, *later_w = lax.optimization_barrier((full_rows, *later_w))
    later_w = gather_groups(later_w, 1)
    gate_w, out_w = later_w[0], later_w[1]

    extra = full_rows[:, :, :, share_len:]
    pair_w = extra[:, :, :, :pair_part].reshape(pair_width, width_full)
    taps_got = extra[:, :, :, pair_part, :tap_count].astype(F32)
    taps_got = taps_got.reshape(team_size, 3, 8, pair_part)
    taps_got = taps_got[:, 0] + (taps_got[:, 1] + taps_got[:, 2])
    taps_pair = jnp.swapaxes(taps_got, 0, 1).reshape(8, pair_width)
    step_w = jnp.pad(
        small_w[pair_part : pair_part + head_count], ((0, LANES - head_count), (0, 0))
    )
    small_w = jnp.concatenate([pair_w, step_w], axis=0)

    consts = head_constants(head_count, head_width)
    weights = (
        norm_in[None, :],
        value_w,
        gate_w,
        small_w,
        taps_value,
        taps_pair,
        heads_row,
        skip_row,
    )
    outs = run_forward(bounds, full_rows, weights, consts, micro_count, piece_len)
    normed, value, conv_v, pair, conv_p, step, scanned, states = outs
    flat = micro_count * block_len
    gate, scaled, grad_normed, stats = run_back(
        bounds, full_back, normed, gate_w, out_w, norm_gate_row, scanned, live_ids, micro_count, piece_len
    )
    partial_out = dot_nt(scaled.reshape(flat, width), out_w).astype(BF16)
    partial_out, stats = lax.optimization_barrier((partial_out, stats))
    branch = lax.psum_scatter(partial_out, TEAM, scatter_dimension=0, tiled=True)
    stats = sum_over(stats, ("core", "near", "row"))
    low_gate, normed_out, grad_scanned, gate_sums = run_gate(
        bounds, stats, grad_normed, gate, scanned, norm_gate_row, live_ids, inner_full, micro_count, piece_len
    )
    kept = (normed, value, conv_v, pair, conv_p, step, scanned, states)
    g_out = dot_tn(full_back.reshape(flat, width_full), normed_out.reshape(flat, width))
    g_gate = dot_tn(normed, low_gate)
    g_out, g_gate, grad_scanned = lax.optimization_barrier(
        (g_out.astype(BF16), g_gate.astype(BF16), grad_scanned)
    )
    flagged = jnp.concatenate(
        [bounds, jnp.full((1, bounds.shape[1]), my_core, jnp.int32)], axis=0
    )
    totals = []
    all_sums = []
    earlier = None
    for micro in range(micro_count):
        low_value, low_small, keep, send, sums, sums_in = run_backward(
            flagged, grad_scanned, low_gate, kept, weights, consts, micro, piece_len, earlier, True
        )
        earlier = (low_value, low_small)
        totals.append(keep.astype(F32) + exchange(send, "core").astype(F32))
        all_sums.append((sums, sums_in))
    low_value, low_small, branch, g_out, g_gate, *totals = lax.optimization_barrier(
        (low_value, low_small, branch, g_out, g_gate, *totals)
    )
    early = [
        lax.psum_scatter(item, ("pair", "half"), scatter_dimension=0, tiled=True)
        for item in (g_out, g_gate)
    ]
    sides = {"near": (my_near, 1), "row": (my_row, 0)}

    def halve(total, name, other):
        bit, axis = sides[name]
        axis = min(axis, total.ndim - 3)
        keep = lax.dynamic_index_in_dim(total, bit, axis, keepdims=False)
        send = lax.dynamic_index_in_dim(total, 1 - bit, axis, keepdims=False)
        return keep + exchange(send.astype(BF16), name).astype(F32)

    orders = [("near", "row") if micro % 2 == 0 else ("row", "near") for micro in range(micro_count)]
    totals = [halve(total, order[0], order[1]) for total, order in zip(totals, orders)]
    branch, *totals = lax.optimization_barrier((branch, *totals))
    middle = totals
    totals = [halve(total, order[1], order[0]) for total, order in zip(totals, orders)]
    grad_ins = totals

    g_out, g_gate = [
        swap(after(item, *grad_ins), turned(cross_perms[0])).astype(F32) for item in early
    ]
    g_out = g_out.T
    g_value = dot_tn(normed, low_value)
    g_small = dot_tn(low_small, normed)
    sums = reduce(jnp.add, [item[0] for item in all_sums])
    sums_in = reduce(jnp.add, [item[1] for item in all_sums])[0:1]
    pair_sums = sums[8:13, :pair_width].reshape(1, -1)
    pair_sums = jnp.pad(pair_sums, ((0, 0), (0, -pair_sums.shape[1] % width_full)))
    team_rows = jnp.concatenate(
        [sums_in, pair_sums.reshape(-1, width_full)], axis=0
    )

    def split_rows(v, axis=0):
        high = lax.reduce_precision(v, 8, 7)
        both = jnp.concatenate([high, v - high], axis=0).astype(BF16)
        return jnp.pad(both, ((0, -both.shape[0] % 16), (0, 0)))

    def join_rows(v, count):
        return v[:count].astype(F32) + v[count : 2 * count].astype(F32)

    g_pair = g_small[:pair_width].reshape(sizes[2], sizes[4], 2, pair_part, width_full)
    for name, bit, axis in (("core", my_core, 2), ("near", my_near, 1), ("row", my_row, 0)):
        keep = lax.dynamic_index_in_dim(g_pair, bit, axis, keepdims=False)
        send = lax.dynamic_index_in_dim(g_pair, 1 - bit, axis, keepdims=False)
        count = send.size // width_full
        packed = jnp.concatenate(
            [send.astype(BF16).reshape(count, width_full), split_rows(team_rows)], axis=0
        )
        packed = exchange(packed, name)
        if name != "core":
            packed = after(packed, *middle)
        g_pair = keep + packed[:count].reshape(keep.shape).astype(F32)
        team_rows = team_rows + join_rows(packed[count:], team_rows.shape[0])
    g_small = jnp.concatenate(
        [
            g_pair,
            g_small[pair_width : pair_width + head_count],
            jnp.zeros((small_pad, width_full), F32),
        ],
        axis=0,
    )
    sums = jnp.concatenate(
        [sums[:5], gate_sums[0:1], sums[6:8], team_rows.reshape(-1, width)], axis=0
    )
    small_rows = g_small.shape[0]
    value_rows = width_full // group_count
    late = jnp.swapaxes(g_small.reshape(small_rows, group_count, -1), 0, 1)
    if value_rows != width:
        late = jnp.pad(late, ((0, 0), (0, 0), (0, width - value_rows)))
    send_back = run_close(
        close_back_kernel, take_map, dealt_tokens, dealt_back, norm_in[None, :], *grad_ins
    )
    late, sums = scatter_groups(
        late, sums, split_rows, join_rows, grad_ins, [send_back]
    )
    g_value = g_value.reshape(group_count, -1, width)
    g_value = scatter_groups(g_value, waits=middle, ends=[send_back])
    g_small = late[:, :value_rows]
    g_pair = g_small[:pair_part].T
    g_step = g_small[pair_part : pair_part + head_count].T
    pair_sums = sums[8 + width_full // width :].reshape(-1)[: 5 * pair_width]
    pair_sums = pair_sums.reshape(5, pair_width)
    in_sums = sums[8 : 8 + width_full // width]
    own_place = (my_row * sizes[4] + my_near) * sizes[3] + my_half
    pair_sums = lax.dynamic_slice_in_dim(pair_sums, own_place * pair_part, pair_part, 1)
    g_norm_in = in_sums.reshape(-1) / norm_in.astype(F32)
    g_skip = jnp.sum(sums[6].reshape(head_count, head_width), axis=1)

    live_start = seat * piece_len
    local_stats = lax.dynamic_slice_in_dim(
        stats[0].reshape(micro_count, block_len), live_start, piece_len, 1
    )
    local_places = live_start + jnp.arange(piece_len, dtype=jnp.int32)
    local_seg = jnp.sum(
        (local_places[None, :, None] >= bounds[:, None, :]).astype(jnp.int32), axis=2
    )
    weight = jnp.where(
        local_seg < live_ids, lax.rsqrt(local_stats / inner_full + EPS), 0.0
    ).reshape(share_len, 1)
    block_out = undeal(run_close(close_out_kernel, take_map, dealt_tokens, branch, weight), send_back)
    grad_tokens = undeal(send_back)
    return (
        block_out,
        grad_tokens,
        g_norm_in,
        g_gate,
        g_value,
        g_pair,
        g_step,
        sums[0:4],
        sums[4],
        pair_sums[0:4],
        pair_sums[4],
        sums[7, :head_count],
        sums[7, LANES : LANES + head_count],
        g_skip,
        sums[5],
        g_out,
    )


def solution(mesh):
    shape = mesh.devices.shape
    sizes = (shape[0] // 2, 2, shape[1], 2, shape[2] // 2)
    fine = jax.sharding.Mesh(mesh.devices.reshape(sizes), ALL)
    dp, team = ("pair", "core"), ("row", "half", "near")
    everything = ("pair", "core", "row", "half", "near")
    placed = (
        P(everything, None),
        P(everything, None),
        P(dp, None),
        P(),
        P(),
        P(dp, team),
        P(dp, team),
        P(dp, team),
        P(dp, team),
        P(None, team),
        P(team),
        P(None, team),
        P(team),
        P(team),
        P(team),
        P(team),
        P(team),
        P(team, dp),
    )
    return jax.shard_map(
        partial(per_device, sizes),
        mesh=fine,
        in_specs=placed,
        out_specs=(
            P(everything, None),
            P(everything, None),
            P(),
            P(dp, team),
            P(dp, team),
            P(dp, team),
            P(dp, team),
            P(None, team),
            P(team),
            P(None, team),
            P(team),
            P(team),
            P(team),
            P(team),
            P(team),
            P(team, dp),
        ),
        check_vma=False,
    )
```

```python
from functools import partial
from functools import reduce

import jax
import jax.numpy as jnp
import numpy as np
from jax import lax
from jax.experimental import pallas as pl
from jax.experimental.pallas import tpu as pltpu
from jax.sharding import PartitionSpec as P

EPS = 1e-05
EXACT = lax.Precision.HIGHEST
F32 = jnp.float32
BF16 = jnp.bfloat16
SUB = 128
ROWS = 256
LANES = 128
MIB = 1024 * 1024


def dot_nn(a, b):
    return jnp.dot(a, b, preferred_element_type=F32)


def dot_nt(a, b):
    return lax.dot_general(a, b, (((1,), (1,)), ((), ())), preferred_element_type=F32)


def dot_tn(a, b):
    return lax.dot_general(a, b, (((0,), (0,)), ((), ())), preferred_element_type=F32)


def sigmoid(v):
    return 1.0 / (1.0 + jnp.exp(-v))


def softplus(v):
    return jnp.maximum(v, 0.0) + jnp.log1p(jnp.exp(-jnp.abs(v)))


def split_two(v):
    high = v.astype(BF16)
    return high, (v - high.astype(F32)).astype(BF16)


def read_bounds(bounds_ref, micro):
    return [bounds_ref[micro, k] for k in range(bounds_ref.shape[1])]


def segment_of(places, bounds):
    total = (places >= bounds[0]).astype(jnp.int32)
    for bound in bounds[1:]:
        total = total + (places >= bound).astype(jnp.int32)
    return total


def segment_scalar(place, bounds):
    total = jnp.int32(0)
    for bound in bounds:
        total = total + jnp.where(place >= bound, 1, 0)
    return total


def iota(shape, axis):
    return lax.broadcasted_iota(jnp.int32, shape, axis)


def same_masks(places, bounds, count):
    own = segment_of(places, bounds)
    return [
        (segment_of(places - shift, bounds) == own) & (places >= shift) & (places < count)
        for shift in range(1, 4)
    ]


def expand_heads(parts, spread_ref):
    stacked = jnp.concatenate(parts, axis=0)
    high, low = split_two(stacked)
    lane = iota(stacked.shape, 1)
    joined = jnp.where(lane < 8, high.astype(F32), pltpu.roll(low.astype(F32), 8, 1))
    wide = dot_nn(joined.astype(BF16), spread_ref[...])
    sizes = np.cumsum([0] + [part.shape[0] for part in parts])
    return [wide[sizes[k] : sizes[k + 1]] for k in range(len(parts))]


def reduce_heads(v, gather_ref):
    high, low = split_two(v)
    return dot_nn(high, gather_ref[...]) + dot_nn(low, gather_ref[...])


def scan_frame(base, bounds, steps, rate, lower_ref):
    start_place = base
    col = start_place + iota((SUB, LANES), 0)
    row = start_place + iota((SUB, SUB), 1)
    seg_col = segment_of(col, bounds)
    seg_row = segment_of(row, bounds)
    allowed = (seg_col == seg_row) & (col >= row)
    last_seg = jnp.where(start_place > 0, segment_scalar(start_place - 1, bounds), -1)
    end_seg = segment_scalar(start_place + SUB - 1, bounds)
    log_decay = jnp.dot(
        lower_ref[...], steps * rate, preferred_element_type=F32, precision=EXACT
    )
    reach = jnp.where(seg_col == last_seg, jnp.exp(log_decay), 0.0)
    tail = jnp.where(
        seg_col == end_seg, jnp.exp(log_decay[SUB - 1 : SUB, :] - log_decay), 0.0
    )
    return allowed, log_decay, reach, tail


def decay_grid(log_decay, log_rows, head):
    gap = log_decay[:, head : head + 1] - log_rows[head : head + 1, :]
    return jnp.exp(jnp.minimum(gap, 0.0))


def forward_kernel(
    pair_count,
    bounds_ref,
    x_ref,
    norm_in_ref,
    w_value_ref,
    w_small_ref,
    taps_value_ref,
    taps_pair_ref,
    heads_ref,
    skip_ref,
    spread_ref,
    lower_ref,
    normed_ref,
    value_ref,
    conv_value_ref,
    pair_ref,
    conv_pair_ref,
    step_ref,
    scanned_ref,
    states_ref,
    halo_value,
    halo_pair,
    state,
):
    micro = pl.program_id(0)
    block = pl.program_id(1)
    count = pl.num_programs(1) * ROWS
    bounds = read_bounds(bounds_ref, micro)
    base = block * ROWS

    @pl.when(block == 0)
    def _():
        halo_value[...] = jnp.zeros_like(halo_value)
        halo_pair[...] = jnp.zeros_like(halo_pair)
        state[...] = jnp.zeros_like(state)

    x = x_ref[...].reshape(ROWS, x_ref.shape[-1]).astype(F32)
    rms = lax.rsqrt(jnp.mean(x * x, axis=1, keepdims=True) + EPS)
    normed = (x * rms * norm_in_ref[...].astype(F32)).astype(BF16)
    normed_ref[...] = normed
    value = dot_nn(normed, w_value_ref[...])
    small = dot_nt(normed, w_small_ref[...])
    pair_width = conv_pair_ref.shape[-1]
    pair = small[:, :pair_width]
    step = small[:, pair_width : pair_width + LANES]
    value_ref[...] = value.astype(BF16)
    pair_ref[...] = pair.astype(BF16)
    step_ref[...] = step

    places = base + iota((ROWS, LANES), 0)
    masks = same_masks(places, bounds, count)

    def convolve(v, halo, taps):
        longer = jnp.concatenate([halo, v], axis=0)
        width = v.shape[1]
        out = taps[4:5, :] + taps[3:4, :] * v
        for shift in range(1, 4):
            moved = pltpu.roll(longer, shift, 0)[8:, :]
            mask = jnp.concatenate([masks[shift - 1]] * (width // LANES), axis=1)
            out = out + jnp.where(mask, moved * taps[3 - shift : 4 - shift, :], 0.0)
        return out

    conv_value = convolve(value, halo_value[...], taps_value_ref[...])
    conv_pair = convolve(pair, halo_pair[...], taps_pair_ref[...])
    halo_value[...] = value[ROWS - 8 :, :]
    halo_pair[...] = pair[ROWS - 8 :, :]
    conv_value_ref[...] = conv_value
    conv_pair_ref[...] = conv_pair
    mixed = conv_value * sigmoid(conv_value)
    shared = (conv_pair * sigmoid(conv_pair)).astype(BF16)
    steps = softplus(step + heads_ref[0:1, :])
    rate = heads_ref[1:2, :]
    lane = iota((SUB, LANES), 1)
    left = lane < 64

    scanned_parts = []
    for sub in range(ROWS // SUB):
        rows = slice(sub * SUB, (sub + 1) * SUB)
        sub_steps = steps[rows]
        allowed, log_decay, reach, tail = scan_frame(
            base + sub * SUB, bounds, sub_steps, rate, lower_ref
        )
        steps_wide, reach_wide, tail_wide = expand_heads(
            [sub_steps, reach, tail], spread_ref
        )
        log_rows = log_decay.T
        keys = shared[rows, :LANES]
        reads = shared[rows, LANES:]
        scores = jnp.where(allowed, dot_nt(reads, keys), 0.0)
        stepped = mixed[rows] * steps_wide
        stepped_low = stepped.astype(BF16)
        held = state[...]
        held_low = held.astype(BF16)
        states_ref[sub] = held_low
        outside = dot_nn(reads, held_low) * reach_wide
        inside = []
        for p in range(pair_count):
            cols = slice(p * LANES, (p + 1) * LANES)
            grids = [
                (scores * decay_grid(log_decay, log_rows, 2 * p + k)).astype(BF16)
                for k in range(2)
            ]
            both = stepped_low[:, cols]
            zero = jnp.zeros_like(both)
            inside.append(
                dot_nn(
                    jnp.concatenate(grids, axis=1),
                    jnp.concatenate(
                        [jnp.where(left, both, zero), jnp.where(left, zero, both)], axis=0
                    ),
                )
            )
        scanned_parts.append(
            jnp.concatenate(inside, axis=1) + outside + mixed[rows] * skip_ref[...]
        )
        state[...] = held * reach_wide[SUB - 1 : SUB, :] + dot_tn(
            keys, (stepped * tail_wide).astype(BF16)
        )
    scanned_ref[...] = jnp.concatenate(scanned_parts, axis=0)


def back_kernel(
    live_ids,
    bounds_ref,
    back_ref,
    normed_ref,
    w_gate_ref,
    w_out_ref,
    norm_gate_ref,
    scanned_ref,
    gate_ref,
    scaled_ref,
    grad_normed_ref,
    stats_ref,
):
    micro = pl.program_id(0)
    bounds = read_bounds(bounds_ref, micro)
    base = pl.program_id(1) * ROWS
    places = base + iota((ROWS, LANES), 0)
    live = segment_of(places, bounds) < live_ids
    gate = dot_nn(normed_ref[...], w_gate_ref[...])
    gate_ref[...] = gate
    gated = scanned_ref[...] * (gate * sigmoid(gate))
    normed_gated = gated * norm_gate_ref[...]
    scaled_ref[...] = normed_gated.astype(BF16).reshape(scaled_ref.shape)
    grad = dot_nn(back_ref[...].reshape(ROWS, back_ref.shape[-1]), w_out_ref[...])
    live_wide = jnp.concatenate([live] * (grad.shape[1] // LANES), axis=1)
    grad = jnp.where(live_wide, grad, 0.0)
    grad_normed_ref[...] = grad.astype(BF16)
    ones = jnp.ones((8, gated.shape[1]), BF16)
    high, low = split_two(gated * gated)
    square = dot_nt(ones, high) + dot_nt(ones, low)
    high, low = split_two(grad * normed_gated)
    cross = dot_nt(ones, high) + dot_nt(ones, low)
    stats_ref[...] = jnp.where(iota(cross.shape, 0) == 0, square, cross)


def gate_kernel(
    live_ids,
    inner_full,
    bounds_ref,
    stats_ref,
    grad_normed_ref,
    gate_ref,
    scanned_ref,
    norm_gate_ref,
    low_gate_ref,
    normed_out_ref,
    grad_scanned_ref,
    sums_ref,
):
    micro = pl.program_id(0)
    block = pl.program_id(1)
    bounds = read_bounds(bounds_ref, micro)

    @pl.when((micro == 0) & (block == 0))
    def _():
        sums_ref[...] = jnp.zeros_like(sums_ref)

    tiles = gate_ref.shape[1] // LANES
    live = segment_of(block * ROWS + iota((ROWS, LANES), 0), bounds) < live_ids
    gate = gate_ref[...]
    scanned = scanned_ref[...]
    grad_normed = grad_normed_ref[...].astype(F32)
    norm_gate = norm_gate_ref[...]
    stats = stats_ref[...].T / inner_full
    spread = lax.rsqrt(stats[:, 0:1] + EPS)
    cross = stats[:, 1:2]
    sg = sigmoid(gate)
    act = gate * sg
    gated = scanned * act
    normed_gated = gated * spread
    live_wide = jnp.concatenate([live] * tiles, axis=1)
    normed_out = jnp.where(live_wide, normed_gated * norm_gate, 0.0).astype(BF16)
    normed_out_ref[...] = normed_out.reshape(normed_out_ref.shape)
    grad_gated = spread * (grad_normed * norm_gate - normed_gated * (spread * cross))
    grad_scanned_ref[...] = (grad_gated * act).astype(BF16)
    low_gate_ref[...] = (
        grad_gated * scanned * (sg * (1.0 + gate * (1.0 - sg)))
    ).astype(BF16)
    sums_ref[0:1, :] += jnp.sum(grad_normed * normed_gated, axis=0, keepdims=True)


def backward_kernel(
    pair_count,
    micro,
    first,
    apart,
    bounds_ref,
    grad_scanned_ref,
    low_gate_ref,
    normed_ref,
    value_ref,
    conv_value_ref,
    pair_ref,
    conv_pair_ref,
    step_ref,
    scanned_ref,
    states_ref,
    w_value_ref,
    w_gate_ref,
    w_small_ref,
    taps_value_ref,
    taps_pair_ref,
    heads_ref,
    skip_ref,
    spread_ref,
    gather_ref,
    lower_ref,
    upper_ref,
    *rest,
):
    if not first:
        rest = rest[2:]
    (
        low_value_ref,
        low_small_ref,
        *grad_in_refs,
        sums_ref,
        sums_in_ref,
        halo_value,
        halo_pair,
        state,
    ) = rest
    turn = pl.program_id(0)
    block_count = pl.num_programs(0)
    block = block_count - 1 - turn
    count = block_count * ROWS
    bounds = read_bounds(bounds_ref, micro)
    base = block * ROWS

    @pl.when(turn == 0)
    def _():
        sums_ref[...] = jnp.zeros_like(sums_ref)
        sums_in_ref[...] = jnp.zeros_like(sums_in_ref)
        halo_value[...] = jnp.zeros_like(halo_value)
        halo_pair[...] = jnp.zeros_like(halo_pair)
        state[...] = jnp.zeros_like(state)

    width = value_ref.shape[1]
    scanned = scanned_ref[...]
    grad_low_all = grad_scanned_ref[...]
    grad_scanned = grad_low_all.astype(F32)
    low_gate = low_gate_ref[...]

    conv_value = conv_value_ref[...]
    sig_value = sigmoid(conv_value)
    mixed = conv_value * sig_value
    conv_pair = conv_pair_ref[...]
    sig_pair = sigmoid(conv_pair)
    shared = (conv_pair * sig_pair).astype(BF16)
    step_in = step_ref[...] + heads_ref[0:1, :]
    steps = softplus(step_in)
    rate = heads_ref[1:2, :]
    skip = skip_ref[...]
    lane = iota((SUB, LANES), 1)
    left = lane < 64

    grad_mixed_parts = []
    grad_shared_parts = []
    grad_step_parts = []
    decay_sum = jnp.zeros((1, LANES), F32)
    for sub in reversed(range(ROWS // SUB)):
        rows = slice(sub * SUB, (sub + 1) * SUB)
        sub_steps = steps[rows]
        allowed, log_decay, reach, tail = scan_frame(
            base + sub * SUB, bounds, sub_steps, rate, lower_ref
        )
        steps_wide, reach_wide, tail_wide = expand_heads(
            [sub_steps, reach, tail], spread_ref
        )
        log_rows = log_decay.T
        keys = shared[rows, :LANES]
        reads = shared[rows, LANES:]
        scores = jnp.where(allowed, dot_nt(reads, keys), 0.0)
        sub_mixed = mixed[rows]
        stepped = sub_mixed * steps_wide
        stepped_low = stepped.astype(BF16)
        grad_y = grad_scanned[rows]
        grad_low = grad_low_all[rows]
        held_low = states_ref[sub]
        later = state[...]
        later_low = later.astype(BF16)
        grad_scores = jnp.zeros((SUB, SUB), F32)
        inner = []
        for p in range(pair_count):
            cols = slice(p * LANES, (p + 1) * LANES)
            both_x = stepped_low[:, cols]
            both_y = grad_low[:, cols]
            zero = jnp.zeros_like(both_y)
            halves = [jnp.where(left, both_y, zero), jnp.where(left, zero, both_y)]
            grids = []
            for k in range(2):
                fade = decay_grid(log_decay, log_rows, 2 * p + k)
                grids.append((scores * fade).astype(BF16))
                grad_scores = grad_scores + dot_nt(halves[k], both_x) * fade
            inner.append(
                dot_tn(jnp.concatenate(grids, axis=0), jnp.concatenate(halves, axis=0))
            )
        grad_scores = jnp.where(allowed, grad_scores, 0.0).astype(BF16)
        tail_part = tail_wide * dot_nn(keys, later_low)
        grad_stepped = jnp.concatenate(inner, axis=1) + tail_part
        reached = (grad_y * reach_wide).astype(BF16)
        tailed = (stepped * tail_wide).astype(BF16)
        grad_reads = dot_nn(grad_scores, keys) + dot_nt(reached, held_low)
        grad_keys = dot_tn(grad_scores, reads) + dot_nt(tailed, later_low)
        stepped_back = stepped_low.astype(F32)
        per_log = reduce_heads(
            grad_y * (scanned[rows] - skip * sub_mixed)
            - stepped_back * grad_stepped,
            gather_ref,
        )
        kept_wide = reach_wide[SUB - 1 : SUB, :]
        at_end = jnp.sum(stepped_back * tail_part, axis=0, keepdims=True) + kept_wide * jnp.sum(
            later * held_low.astype(F32), axis=0, keepdims=True
        )
        at_end = reduce_heads(jnp.broadcast_to(at_end, (8, width)), gather_ref)[0:1, :]
        grad_log = (
            jnp.dot(upper_ref[...], per_log, preferred_element_type=F32, precision=EXACT)
            + at_end
        )
        decay_sum = decay_sum + jnp.sum(grad_log * sub_steps, axis=0, keepdims=True) * rate
        grad_steps = reduce_heads(grad_stepped * sub_mixed, gather_ref) + rate * grad_log
        grad_step_parts.insert(0, grad_steps)
        grad_shared_parts.insert(0, jnp.concatenate([grad_keys, grad_reads], axis=1))
        grad_mixed_parts.insert(0, grad_stepped * steps_wide + skip * grad_y)
        state[...] = later * kept_wide + dot_tn(reads, reached)
    grad_mixed = jnp.concatenate(grad_mixed_parts, axis=0)
    grad_shared = jnp.concatenate(grad_shared_parts, axis=0)
    grad_step = jnp.concatenate(grad_step_parts, axis=0) * sigmoid(step_in)

    longer_places = base + iota((ROWS + 8, LANES), 0)
    masks = same_masks(longer_places, bounds, count)

    def convolve_back(q, halo, v, taps):
        longer = jnp.concatenate([q, halo], axis=0)
        grad = taps[3:4, :] * q
        tap_sums = [jnp.sum(v * q, axis=0, keepdims=True)]
        for shift in range(1, 4):
            mask = jnp.concatenate([masks[shift - 1]] * (q.shape[1] // LANES), axis=1)
            kept = jnp.where(mask, longer, 0.0)
            moved = pltpu.roll(kept, ROWS + 8 - shift, 0)[:ROWS, :]
            grad = grad + taps[3 - shift : 4 - shift, :] * moved
            tap_sums.insert(0, jnp.sum(v * moved, axis=0, keepdims=True))
        return grad, tap_sums + [jnp.sum(q, axis=0, keepdims=True)]

    q_value = grad_mixed * (sig_value * (1.0 + conv_value * (1.0 - sig_value)))
    q_pair = grad_shared * (sig_pair * (1.0 + conv_pair * (1.0 - sig_pair)))
    grad_value, value_sums = convolve_back(
        q_value, halo_value[...], value_ref[...].astype(F32), taps_value_ref[...]
    )
    grad_pair, pair_sums = convolve_back(
        q_pair, halo_pair[...], pair_ref[...].astype(F32), taps_pair_ref[...]
    )
    halo_value[...] = q_value[:8, :]
    halo_pair[...] = q_pair[:8, :]
    low_value = grad_value.astype(BF16)
    low_small = jnp.concatenate([grad_pair, grad_step], axis=1).astype(BF16)
    low_value_ref[...] = low_value
    low_small_ref[...] = low_small
    grad_in = (
        dot_nt(low_gate, w_gate_ref[...])
        + dot_nt(low_value, w_value_ref[...])
        + dot_nn(low_small, w_small_ref[...])
    )
    grad_in_low = grad_in.astype(BF16).reshape(grad_in_refs[0].shape)
    if apart:
        mine = block % 2 == bounds_ref[bounds_ref.shape[0] - 1, 0]

        @pl.when(mine)
        def _():
            grad_in_refs[0][...] = grad_in_low

        @pl.when(jnp.logical_not(mine))
        def _():
            grad_in_refs[1][...] = grad_in_low

    else:
        grad_in_refs[0][...] = grad_in_low
    sums_in_ref[0:1, :] += jnp.sum(grad_in * normed_ref[...].astype(F32), axis=0, keepdims=True)
    skip_sum = jnp.sum(grad_scanned * mixed, axis=0, keepdims=True)
    step_sum = jnp.sum(grad_step, axis=0, keepdims=True)
    for k in range(5):
        sums_ref[k : k + 1, :] += value_sums[k]
    sums_ref[6:7, :] += skip_sum
    sums_ref[7:8, :LANES] += step_sum
    sums_ref[7:8, LANES : 2 * LANES] += decay_sum
    for k in range(5):
        sums_ref[8 + k : 9 + k, : pair_sums[k].shape[1]] += pair_sums[k]


def whole_spec(shape):
    return pl.BlockSpec(shape, lambda *_: (0,) * len(shape))


def smem_spec():
    return pl.BlockSpec(memory_space=pltpu.SMEM)


def kernel_params(size):
    return pltpu.CompilerParams(vmem_limit_bytes=size * MIB)


def head_constants(head_count, head_width):
    width = head_count * head_width
    spread = np.zeros((LANES, width), np.float32)
    for h in range(head_count):
        spread[h, h * head_width : (h + 1) * head_width] = 1.0
        spread[h + 8, h * head_width : (h + 1) * head_width] = 1.0
    gather = np.zeros((width, LANES), np.float32)
    for h in range(head_count):
        gather[h * head_width : (h + 1) * head_width, h] = 1.0
    lower = np.tril(np.ones((SUB, SUB), np.float32))
    return (
        jnp.asarray(spread, BF16),
        jnp.asarray(gather, BF16),
        jnp.asarray(lower),
        jnp.asarray(lower.T),
    )


def seat_spec(piece, cols):
    return pl.BlockSpec((None, 2, None, piece, cols), lambda b, i: (i // 2, 0, i % 2, b, 0))


def seat_view(item):
    return item.reshape((item.shape[0] // 4, 2, 2) + item.shape[1:])


def cost(flops, count, moved):
    return pl.CostEstimate(flops=int(flops), transcendentals=int(count), bytes_accessed=int(moved))


def run_forward(bounds, rows, weights, consts, micro_count, piece):
    block_len = 8 * piece
    blocks = block_len // ROWS
    norm_in, w_value, _, w_small, taps_value, taps_pair, heads, skip = weights
    spread, _, lower, _ = consts
    full = rows.shape[4]
    width = w_value.shape[1]
    pair_width = taps_pair.shape[1]
    length = micro_count * block_len
    subs = ROWS // SUB

    def by_rows(cols):
        return pl.BlockSpec((ROWS, cols), lambda b, i: (b * blocks + i, 0))

    wholes = [norm_in, w_value, w_small, taps_value, taps_pair, heads, skip, spread, lower]
    widths = [width, width, pair_width, pair_width, LANES, width]
    types = [BF16, F32, BF16, F32, F32, F32]
    return pl.pallas_call(
        partial(forward_kernel, width // LANES),
        grid=(micro_count, blocks),
        in_specs=[smem_spec(), seat_spec(piece, full)] + [whole_spec(item.shape) for item in wholes],
        out_specs=[by_rows(full)]
        + [by_rows(cols) for cols in widths]
        + [
            pl.BlockSpec((subs, LANES, width), lambda b, i: (b * blocks + i, 0, 0)),
        ],
        out_shape=[jax.ShapeDtypeStruct((length, full), BF16)]
        + [jax.ShapeDtypeStruct((length, cols), kind) for cols, kind in zip(widths, types)]
        + [
            jax.ShapeDtypeStruct((length // SUB, LANES, width), BF16),
        ],
        scratch_shapes=[
            pltpu.VMEM((8, width), F32),
            pltpu.VMEM((8, pair_width), F32),
            pltpu.VMEM((LANES, width), F32),
        ],
        compiler_params=kernel_params(56),
        cost_estimate=cost(length * full * width * 12, length * width * 8, length * width * 40),
        name="forward",
    )(bounds, rows, *wholes)


def run_back(bounds, back, normed, w_gate, w_out, norm_gate, scanned, live_ids, micro_count, piece):
    block_len = 8 * piece
    blocks = block_len // ROWS
    length, width = scanned.shape
    full = normed.shape[1]

    def by_rows(cols):
        return pl.BlockSpec((ROWS, cols), lambda b, i: (b * blocks + i, 0))

    by_cols = pl.BlockSpec((8, ROWS), lambda b, i: (0, b * blocks + i))
    return pl.pallas_call(
        partial(back_kernel, live_ids),
        grid=(micro_count, blocks),
        in_specs=[
            smem_spec(),
            seat_spec(piece, full),
            by_rows(full),
            whole_spec(w_gate.shape),
            whole_spec(w_out.shape),
            whole_spec(norm_gate.shape),
            by_rows(width),
        ],
        out_specs=[by_rows(width), seat_spec(piece, width), by_rows(width), by_cols],
        out_shape=[
            jax.ShapeDtypeStruct((length, width), F32),
            jax.ShapeDtypeStruct(back.shape[:4] + (width,), BF16),
            jax.ShapeDtypeStruct((length, width), BF16),
            jax.ShapeDtypeStruct((8, length), F32),
        ],
        compiler_params=kernel_params(56),
        cost_estimate=cost(length * full * width * 4, length * width, length * width * 30),
        name="back",
    )(bounds, back, normed, w_gate, w_out, norm_gate, scanned)


def run_gate(bounds, stats, grad_normed, gate, scanned, norm_gate, live_ids, inner_full, micro_count, piece):
    block_len = 8 * piece
    blocks = block_len // ROWS
    length, width = gate.shape
    by_rows = pl.BlockSpec((ROWS, width), lambda b, i: (b * blocks + i, 0))
    return pl.pallas_call(
        partial(gate_kernel, live_ids, inner_full),
        grid=(micro_count, blocks),
        in_specs=[
            smem_spec(),
            pl.BlockSpec((8, ROWS), lambda b, i: (0, b * blocks + i)),
            by_rows,
            by_rows,
            by_rows,
            whole_spec(norm_gate.shape),
        ],
        out_specs=[
            by_rows,
            seat_spec(piece, width),
            by_rows,
            whole_spec((8, width)),
        ],
        out_shape=[
            jax.ShapeDtypeStruct((length, width), BF16),
            jax.ShapeDtypeStruct((blocks // 2, 2, 2, micro_count * piece, width), BF16),
            jax.ShapeDtypeStruct((length, width), BF16),
            jax.ShapeDtypeStruct((8, width), F32),
        ],
        compiler_params=kernel_params(56),
        cost_estimate=cost(length * width * 20, length * width, length * width * 20),
        name="gate",
    )(bounds, stats, grad_normed, gate, scanned, norm_gate)


def run_backward(bounds, grad_scanned, low_gate, kept, weights, consts, micro, piece, earlier, apart):
    block_len = 8 * piece
    blocks = block_len // ROWS
    normed, value, conv_value, pair, conv_pair, step, scanned, states = kept
    _, w_value, w_gate, w_small, taps_value, taps_pair, heads, skip = weights
    spread, gather, lower, upper = consts
    full = normed.shape[1]
    length, width = value.shape
    pair_width = pair.shape[1]
    subs = ROWS // SUB

    def place(i):
        return micro * blocks + blocks - 1 - i

    def by_rows(item):
        return pl.BlockSpec((ROWS, item.shape[1]), lambda i: (place(i), 0))

    if apart:
        row_blocks = [
            pl.BlockSpec((None, 2, piece, full), lambda i: ((blocks - 1 - i) // 2, 0, 0, 0))
        ] * 2
        row_shapes = [jax.ShapeDtypeStruct((blocks // 2, 2, piece, full), BF16)] * 2
    else:
        row_blocks = [
            pl.BlockSpec(
                (None, 2, None, piece, full),
                lambda i: ((blocks - 1 - i) // 2, 0, (blocks - 1 - i) % 2, 0, 0),
            )
        ]
        row_shapes = [jax.ShapeDtypeStruct((blocks // 2, 2, 2, piece, full), BF16)]
    rowwise = [grad_scanned, low_gate, normed, value, conv_value, pair, conv_pair, step, scanned]
    wholes = [w_value, w_gate, w_small, taps_value, taps_pair, heads, skip, spread, gather, lower, upper]
    outs = [
        jax.ShapeDtypeStruct((length, width), BF16),
        jax.ShapeDtypeStruct((length, w_small.shape[0]), BF16),
        *row_shapes,
        jax.ShapeDtypeStruct((16, width), F32),
        jax.ShapeDtypeStruct((8, full), F32),
    ]
    ins = [bounds] + rowwise + [states] + wholes
    return pl.pallas_call(
        partial(backward_kernel, width // LANES, micro, earlier is None, apart),
        grid=(blocks,),
        in_specs=[smem_spec()]
        + [by_rows(item) for item in rowwise]
        + [pl.BlockSpec((subs, LANES, width), lambda i: (place(i), 0, 0))]
        + [whole_spec(item.shape) for item in wholes]
        + ([] if earlier is None else [pl.BlockSpec(memory_space=pl.ANY)] * 2),
        out_specs=[by_rows(item) for item in outs[:2]]
        + row_blocks
        + [whole_spec(item.shape) for item in outs[-2:]],
        out_shape=outs,
        input_output_aliases={} if earlier is None else {len(ins): 0, len(ins) + 1: 1},
        scratch_shapes=[
            pltpu.VMEM((8, width), F32),
            pltpu.VMEM((8, pair_width), F32),
            pltpu.VMEM((LANES, width), F32),
        ],
        compiler_params=kernel_params(56),
        cost_estimate=cost(block_len * full * width * 14, block_len * width * 16, block_len * width * 40),
        name="backward",
    )(*ins, *([] if earlier is None else earlier))


def deal_kernel(
    group_shift,
    place_ref,
    listed_ref,
    listed_cols_ref,
    own_ref,
    own_col_ref,
    tokens_ref,
    cotangent_ref,
    send_map_ref,
    take_map_ref,
    *piece_refs,
):
    start, group, target = place_ref[0], place_ref[1], place_ref[2]
    share = tokens_ref.shape[0]
    group_count = listed_cols_ref.shape[1]
    quota = share // group_count
    natural = start + iota((share, share), 1)
    found = []
    for g in range(group_count):
        hits = (listed_cols_ref[:, g : g + 1] == natural).astype(F32)
        found.append(jnp.sum(hits, axis=0, keepdims=True))
    pad = -group_count % 8
    found = jnp.concatenate(found + [jnp.zeros((pad, share), F32)] * (pad > 0), axis=0)
    before = (iota((share, share), 0) < iota((share, share), 1)).astype(BF16)
    rank = dot_nn(found.astype(BF16), before)
    slot = (iota(found.shape, 0) ^ group) * quota
    place = jnp.sum(found * (rank + slot.astype(F32)), axis=0, keepdims=True)
    send_map = (iota((share, share), 0).astype(F32) == place).astype(BF16)
    send_map_ref[...] = send_map
    own_row = jnp.broadcast_to(own_ref[...], (share, share))
    own_col = jnp.broadcast_to(own_col_ref[...], (share, share))
    src_row = lax.shift_right_logical(own_row, group_shift)
    src_col = lax.shift_right_logical(own_col, group_shift)
    ahead = ((src_row == src_col) & (own_row < own_col)).astype(F32)
    order = jnp.sum(ahead, axis=1, keepdims=True)
    wanted = ((src_col ^ target) * quota).astype(F32) + order
    take_map_ref[...] = (iota((share, share), 1).astype(F32) == wanted).astype(BF16)
    write_pieces(piece_refs[:group_count], dot_nn(send_map, tokens_ref[...]))
    write_pieces(piece_refs[group_count:], dot_nn(send_map, cotangent_ref[...]))


def write_pieces(piece_refs, rows):
    size = rows.shape[0] // len(piece_refs)
    for k, piece_ref in enumerate(piece_refs):
        piece_ref[...] = rows[k * size : (k + 1) * size].astype(BF16)


def join_pieces(piece_refs):
    if piece_refs[0].shape[0] % 16 == 0:
        return jnp.concatenate([piece_ref[...] for piece_ref in piece_refs], axis=0)
    wide = [piece_ref[...].astype(F32) for piece_ref in piece_refs]
    return jnp.concatenate(wide, axis=0).astype(BF16)


def run_deal(place, listed, own, tokens, cotangent, group_len):
    share, width = tokens.shape
    group_count = listed.shape[0]
    vmem = pl.BlockSpec(memory_space=pltpu.VMEM)
    piece = jax.ShapeDtypeStruct((share // group_count, width), BF16)
    outs = pl.pallas_call(
        partial(deal_kernel, group_len.bit_length() - 1),
        in_specs=[smem_spec()] + [vmem] * 6,
        out_specs=[vmem] * (2 + 2 * group_count),
        out_shape=[jax.ShapeDtypeStruct((share, share), BF16)] * 2
        + [piece] * (2 * group_count),
        compiler_params=kernel_params(16),
        name="deal",
    )(place, listed, listed.T, own[None, :], own[:, None], tokens, cotangent)
    return outs[2 : 2 + group_count], outs[2 + group_count :], outs[0], outs[1]


def pick_kernel(transposed, extra_rows, map_ref, *refs):
    out_ref = refs[-1]
    pieces = refs[:-1]
    if extra_rows:
        share = out_ref.shape[0] - extra_rows
        out_ref[share:, :] = pieces[-1][...]
        pieces = pieces[:-1]
    dot = dot_tn if transposed else dot_nn
    rows = dot(map_ref[...], join_pieces(pieces)).astype(BF16)
    if extra_rows:
        out_ref[:share, :] = rows
    else:
        out_ref[...] = rows


def run_pick(take_map, pieces, transposed, extra=None):
    vmem = pl.BlockSpec(memory_space=pltpu.VMEM)
    extra_rows = 0 if extra is None else extra.shape[0]
    items = list(pieces) + ([] if extra is None else [extra])
    return pl.pallas_call(
        partial(pick_kernel, transposed, extra_rows),
        in_specs=[vmem] * (1 + len(items)),
        out_specs=vmem,
        out_shape=jax.ShapeDtypeStruct(
            (take_map.shape[0] + extra_rows, pieces[0].shape[1]), BF16
        ),
        compiler_params=kernel_params(16),
        name="pick",
    )(take_map, *items)


def close_out_kernel(map_ref, dealt_ref, branch_ref, weight_ref, *piece_refs):
    shape = dealt_ref.shape
    out = dealt_ref[...].astype(F32) + weight_ref[...] * branch_ref[...].reshape(shape).astype(F32)
    write_pieces(piece_refs, dot_tn(map_ref[...], out.astype(BF16)))


def close_back_kernel(
    grad_count, map_ref, dealt_ref, back_ref, norm_in_ref, *refs
):
    grad_refs, piece_refs = refs[: 2 * grad_count], refs[2 * grad_count :]
    x = dealt_ref[...].astype(F32)
    rms = lax.rsqrt(jnp.mean(x * x, axis=1, keepdims=True) + EPS)
    xhat = x * rms
    grad = jnp.concatenate(
        [
            grad_refs[2 * k][...] + grad_refs[2 * k + 1][...].astype(F32)
            for k in range(grad_count)
        ],
        axis=0,
    )
    win = grad * norm_in_ref[...].astype(F32)
    cross = jnp.mean(win * xhat, axis=1, keepdims=True)
    out = back_ref[...].astype(F32) + rms * (win - xhat * cross)
    write_pieces(piece_refs, dot_tn(map_ref[...], out.astype(BF16)))


def run_close(body, group_count, take_map, dealt, *items):
    share, width = take_map.shape[0], dealt.shape[1]
    whole = [whole_spec(item.shape) for item in items]
    return pl.pallas_call(
        body,
        grid=(1,),
        in_specs=[whole_spec(take_map.shape), whole_spec((share, width))] + whole,
        out_specs=[whole_spec((share // group_count, width))] * group_count,
        out_shape=[jax.ShapeDtypeStruct((share // group_count, width), BF16)] * group_count,
        compiler_params=kernel_params(16),
        name="close",
    )(take_map, dealt, *items)


def halves_kernel(axes, bits_ref, *refs):
    count = len(axes)
    for k, (axis, bit_index) in enumerate(axes):
        held_ref, arrived_ref = refs[2 * k], refs[2 * k + 1]
        keep_ref, send_ref = refs[2 * (count + k)], refs[2 * (count + k) + 1]
        bit = bits_ref[bit_index]

        def total(where):
            return held_ref[where].astype(F32) + arrived_ref[where].astype(F32)

        if len(held_ref.shape) == 3:
            keep_ref[...] = total(bit)
            send_ref[...] = total(1 - bit).astype(BF16)
            continue
        for other in range(2):
            here = (other, bit) if axis == 1 else (bit, other)
            there = (other, 1 - bit) if axis == 1 else (1 - bit, other)
            keep_ref[other] = total(here)
            send_ref[other] = total(there).astype(BF16)


def run_halves(axes, bits, *items):
    vmem = pl.BlockSpec(memory_space=pltpu.VMEM)
    outs = []
    for item in items[::2]:
        outs.append(jax.ShapeDtypeStruct(item.shape[1:], F32))
        outs.append(jax.ShapeDtypeStruct(item.shape[1:], BF16))
    return pl.pallas_call(
        partial(halves_kernel, axes),
        in_specs=[smem_spec()] + [vmem] * len(items),
        out_specs=[vmem] * len(outs),
        out_shape=outs,
        compiler_params=kernel_params(56),
        name="halves",
    )(bits, *items)


ALL = ("pair", "core", "row", "half", "near")
TEAM = ("row", "near", "core")


def make_perm(sizes, move):
    ranks = np.arange(int(np.prod(sizes))).reshape(sizes)
    return [
        (int(ranks[where]), int(ranks[move(*where)])) for where in np.ndindex(*sizes)
    ]


def turned(perm):
    return [(target, source) for source, target in perm]


def swap(v, perm):
    return lax.ppermute(v, ALL, perm)


def choose(bit, first, second, axis):
    return jnp.where(
        bit == 0,
        jnp.concatenate([first, second], axis=axis),
        jnp.concatenate([second, first], axis=axis),
    )


def per_device(
    sizes,
    tokens,
    cotangent,
    seq_lengths,
    token_order,
    norm_in,
    w_gate,
    w_value,
    w_pair,
    w_step,
    conv_value,
    bias_value,
    conv_pair,
    bias_pair,
    step_bias,
    decay_log,
    skip_gain,
    norm_gate,
    w_out,
):
    pair_count = sizes[0]
    group_count = sizes[0] * sizes[1]
    team_size = sizes[2] * sizes[3] * sizes[4]
    my_pair, my_core, my_row, my_half, my_near = [lax.axis_index(name) for name in ALL]
    group = my_pair * 2 + my_core
    target = my_pair * 2 + my_half
    member = my_row * (sizes[3] * sizes[4]) + my_half * sizes[4] + my_near
    seat = my_row * (sizes[3] * sizes[4]) + my_core * sizes[4] + my_near

    share_len, width_full = tokens.shape
    quota_len = share_len // group_count
    micro_count = seq_lengths.shape[0]
    piece_len = share_len // micro_count
    block_len = piece_len * team_size
    group_len = share_len * team_size
    width = w_gate.shape[1]
    inner_full = width * team_size
    head_count = step_bias.shape[0]
    head_width = width // head_count
    pair_part = w_pair.shape[1]
    pair_width = pair_part * team_size
    small_width = pair_width + LANES

    deal_perms = [
        make_perm(
            sizes,
            lambda p, c, r, h, n, e=e: (p ^ (e // 2), h, r, c ^ (e % 2), n),
        )
        for e in range(group_count)
    ]
    cross_perms = [
        make_perm(sizes, lambda p, c, r, h, n, f=f: (p, h, r, c ^ f, n)) for f in range(2)
    ]
    pair_bits = [k for k in range(pair_count.bit_length() - 1)]
    pair_perms = [
        make_perm(sizes, lambda p, c, r, h, n, k=k: (p ^ (1 << k), c, r, h, n))
        for k in pair_bits
    ]

    team_perms = {
        "core": make_perm(sizes, lambda p, c, r, h, n: (p, 1 - c, r, h, n)),
        "near": make_perm(sizes, lambda p, c, r, h, n: (p, c, r, h, 1 - n)),
        "row": make_perm(sizes, lambda p, c, r, h, n: (p, c, 1 - r, h, n)),
    }

    def after(v, *others):
        return lax.optimization_barrier((v,) + others)[0]

    def cross_groups(block):
        return swap(block, cross_perms[0]), swap(block, cross_perms[1])

    def gather_groups(crossed, axis):
        first, second = crossed
        current = choose(my_half, first, second, axis)
        for k in pair_bits:
            other = swap(current, pair_perms[k])
            current = choose((my_pair >> k) & 1, current, other, axis)
        return current

    def open_scatter(part):
        half = part.shape[0] // 2
        bit = (my_pair >> pair_bits[-1]) & 1
        kept = lax.dynamic_slice_in_dim(part, bit * half, half, 0)
        sent = lax.dynamic_slice_in_dim(part, (1 - bit) * half, half, 0)
        return kept, sent.astype(BF16)

    def scatter_groups(
        parts, sums=None, split=None, join=None, waits=(), bound=(), opened=None
    ):
        def pack(items):
            items = [item.astype(BF16) for item in items]
            if sums is not None:
                rows = split(sums)
                items.append(jnp.broadcast_to(rows, items[0].shape[:-2] + rows.shape))
            return jnp.concatenate(items, axis=-2)

        if opened is not None:
            parts = [opened[0]]
        marks = np.cumsum([0] + [part.shape[-2] for part in parts])

        def unpack(v, total):
            items = [
                v[..., int(marks[k]) : int(marks[k + 1]), :].astype(F32)
                for k in range(len(parts))
            ]
            if total is None:
                return items, None
            first = v if v.ndim == 2 else v[0]
            return items, total + join(first[int(marks[-1]) :], total.shape[0])

        for k in reversed(pair_bits):
            if opened is not None:
                arrived = after(swap(opened[1], pair_perms[k]), *waits)
                parts = [opened[0].astype(F32) + arrived.astype(F32)]
                opened = None
                continue
            half = parts[0].shape[0] // 2
            bit = (my_pair >> k) & 1
            kept = [lax.dynamic_slice_in_dim(part, bit * half, half, 0) for part in parts]
            sent = [lax.dynamic_slice_in_dim(part, (1 - bit) * half, half, 0) for part in parts]
            arrived = after(swap(pack(sent), pair_perms[k]), *waits)
            arrived, sums = unpack(arrived, sums)
            parts = [mine.astype(F32) + other for mine, other in zip(kept, arrived)]
        first = [lax.dynamic_index_in_dim(part, my_half, 0, keepdims=False) for part in parts]
        second = [
            lax.dynamic_index_in_dim(part, 1 - my_half, 0, keepdims=False) for part in parts
        ]
        first, second, *bound = lax.optimization_barrier((pack(first), pack(second), *bound))
        first = swap(first, turned(cross_perms[0]))
        second = swap(second, turned(cross_perms[1]))

        def finish(first, second):
            zero = None if sums is None else jnp.zeros_like(sums)
            first, sums_first = unpack(first, zero)
            second, sums_second = unpack(second, zero)
            total = [mine + other for mine, other in zip(first, second)]
            return total, None if sums is None else sums_first + sums_second

        return (first, second), finish, bound

    listed = lax.dynamic_index_in_dim(
        token_order.reshape(group_count, micro_count, team_size, piece_len),
        member,
        2,
        keepdims=False,
    ).reshape(group_count, share_len)
    seat_listed = lax.dynamic_slice(
        token_order.reshape(group_count, micro_count, team_size, piece_len),
        (target, 0, seat, 0),
        (1, micro_count, 1, piece_len),
    ).reshape(share_len)
    start = (group * team_size + member) * share_len
    token_pieces, back_pieces, send_map, take_map = run_deal(
        jnp.stack([start, group, target]).astype(jnp.int32),
        listed,
        seat_listed,
        tokens,
        cotangent,
        group_len,
    )

    def deal_pieces(pieces):
        return [swap(piece, perm) for piece, perm in zip(pieces, deal_perms)]

    def undeal(pieces, *waits):
        pieces = [
            after(swap(piece, turned(perm)), *waits)
            for piece, perm in zip(pieces, deal_perms)
        ]
        return run_pick(send_map, pieces, True)

    def exchange(v, axis_name):
        return swap(v, team_perms[axis_name])

    def sum_over(v, names):
        for name in names:
            v = v + exchange(v, name)
        return v

    def pack_taps(taps, bias):
        return jnp.concatenate(
            [taps, bias[None, :], jnp.zeros((3, bias.shape[0]), F32)], axis=0
        )

    heads_own = jnp.pad(jnp.stack([step_bias, decay_log, skip_gain]), ((0, 5), (0, 0)))
    lengths_own = jnp.pad(
        seq_lengths.astype(F32),
        ((0, 8 - micro_count), (0, width - seq_lengths.shape[1])),
    )
    local_params = jnp.concatenate(
        [
            pack_taps(conv_value, bias_value),
            jnp.broadcast_to(norm_gate[None, :], (8, width)),
            jnp.pad(heads_own, ((0, 0), (0, width - head_count))),
            jnp.pad(pack_taps(conv_pair, bias_pair), ((0, 0), (0, width - pair_part))),
            lengths_own,
        ],
        axis=0,
    )
    local_params = swap(after(local_params, *token_pieces), cross_perms[0])
    taps_value = local_params[:8]
    norm_gate_row = local_params[8:9]
    heads_got = local_params[16:24, :head_count]
    own_taps = local_params[24:32, :pair_part]
    live_ids = seq_lengths.shape[1] - 1
    bounds = jnp.cumsum(
        local_params[32 : 32 + micro_count, : live_ids + 1].astype(jnp.int32), axis=1
    )
    skip_row = jnp.repeat(heads_got[2:3], head_width, axis=1)
    heads_row = jnp.pad(
        jnp.concatenate([heads_got[0:1], -jnp.exp(heads_got[1:2])], axis=0),
        ((0, 6), (0, LANES - head_count)),
    )
    tap_high = lax.reduce_precision(own_taps, 8, 7)
    tap_mid = lax.reduce_precision(own_taps - tap_high, 8, 7)
    tap_low = own_taps - tap_high - tap_mid
    tap_row = jnp.stack([tap_high, tap_mid, tap_low]).astype(BF16).reshape(1, -1)
    tap_count = tap_row.shape[1]

    small_pad = -(pair_part + head_count) % 16
    small_own = jnp.concatenate(
        [w_pair.T, w_step.T, jnp.zeros((small_pad, w_pair.shape[0]), BF16)], axis=0
    )
    small_w = gather_groups(cross_groups(after(small_own, *token_pieces)), 1)

    pieces = deal_pieces(token_pieces)
    extra = jnp.concatenate(
        [
            small_w[:pair_part],
            jnp.pad(tap_row, ((0, 15), (0, width_full - tap_count))),
        ],
        axis=0,
    )
    dealt_tokens = run_pick(take_map, pieces, False, extra)
    full_rows = seat_view(lax.all_gather(dealt_tokens, TEAM, axis=0))
    value_w = cross_groups(after(w_value, *pieces))
    back_pieces = lax.optimization_barrier((*back_pieces, *value_w))[:group_count]
    pieces = deal_pieces(back_pieces)
    value_w = gather_groups(value_w, 0)
    dealt_back = run_pick(take_map, pieces, False)
    full_back = seat_view(lax.all_gather(dealt_back, TEAM, axis=0))
    later_w = cross_groups(after(jnp.stack([w_gate, w_out.T]), *pieces))
    full_rows, *later_w = lax.optimization_barrier((full_rows, *later_w))
    later_w = gather_groups(later_w, 1)
    gate_w, out_w = later_w[0], later_w[1]

    extra = full_rows[:, :, :, share_len:]
    pair_w = extra[:, :, :, :pair_part].reshape(pair_width, width_full)
    taps_got = extra[:, :, :, pair_part, :tap_count].astype(F32)
    taps_got = taps_got.reshape(team_size, 3, 8, pair_part)
    taps_got = taps_got[:, 0] + (taps_got[:, 1] + taps_got[:, 2])
    taps_pair = jnp.swapaxes(taps_got, 0, 1).reshape(8, pair_width)
    step_w = jnp.pad(
        small_w[pair_part : pair_part + head_count], ((0, LANES - head_count), (0, 0))
    )
    small_w = jnp.concatenate([pair_w, step_w], axis=0)

    consts = head_constants(head_count, head_width)
    weights = (
        norm_in[None, :],
        value_w,
        gate_w,
        small_w,
        taps_value,
        taps_pair,
        heads_row,
        skip_row,
    )
    outs = run_forward(bounds, full_rows, weights, consts, micro_count, piece_len)
    normed, value, conv_v, pair, conv_p, step, scanned, states = outs
    flat = micro_count * block_len
    gate, scaled, grad_normed, stats = run_back(
        bounds, full_back, normed, gate_w, out_w, norm_gate_row, scanned, live_ids, micro_count, piece_len
    )
    partial_out = dot_nt(scaled.reshape(flat, width), out_w).astype(BF16)
    branch = lax.psum_scatter(partial_out, TEAM, scatter_dimension=0, tiled=True)
    stats = sum_over(stats, ("core", "near", "row"))
    low_gate, normed_out, grad_scanned, gate_sums = run_gate(
        bounds, stats, grad_normed, gate, scanned, norm_gate_row, live_ids, inner_full, micro_count, piece_len
    )
    kept = (normed, value, conv_v, pair, conv_p, step, scanned, states)
    g_out = dot_tn(full_back.reshape(flat, width_full), normed_out.reshape(flat, width))
    g_gate = dot_tn(normed, low_gate)
    g_out, g_gate, grad_scanned = lax.optimization_barrier(
        (g_out.astype(BF16), g_gate.astype(BF16), grad_scanned)
    )
    flagged = jnp.concatenate(
        [bounds, jnp.full((1, bounds.shape[1]), my_core, jnp.int32)], axis=0
    )
    live_start = seat * piece_len
    local_stats = lax.dynamic_slice_in_dim(
        stats[0].reshape(micro_count, block_len), live_start, piece_len, 1
    )
    local_places = live_start + jnp.arange(piece_len, dtype=jnp.int32)
    local_seg = jnp.sum(
        (local_places[None, :, None] >= bounds[:, None, :]).astype(jnp.int32), axis=2
    )
    weight = jnp.where(
        local_seg < live_ids, lax.rsqrt(local_stats / inner_full + EPS), 0.0
    ).reshape(share_len, 1)
    bits = jnp.stack([my_near, my_row]).astype(jnp.int32)
    held = []
    all_sums = []
    earlier = None
    crossed = ()
    early = [item.reshape(group_count, -1, width) for item in (g_out, g_gate)]
    for micro in range(micro_count):
        if micro == micro_count - 1 and micro:
            crossed, finish_early, (low_value, low_small, bits, weight, *all_sums[0]) = scatter_groups(
                early, waits=earlier, bound=(*earlier, bits, weight, *all_sums[0])
            )
            earlier = (low_value, low_small)
        low_value, low_small, keep, send, sums, sums_in = run_backward(
            flagged, grad_scanned, low_gate, kept, weights, consts, micro, piece_len, earlier, True
        )
        earlier = (low_value, low_small)
        if crossed:
            send, *crossed = lax.optimization_barrier((send, *crossed))
        held += [keep, exchange(send, "core")]
        all_sums.append([sums, sums_in])
    first_axes = tuple((1 - micro % 2, micro % 2) for micro in range(micro_count))
    next_axes = tuple((0, 1 - micro % 2) for micro in range(micro_count))

    def cross_sides(held, axes):
        names = ("near", "row")
        return [
            item if k % 2 == 0 else exchange(item, names[axes[k // 2][1]])
            for k, item in enumerate(held)
        ]

    held = run_halves(first_axes, bits, *held)
    low_value, low_small, all_sums, *held = lax.optimization_barrier(
        (low_value, low_small, all_sums, *held)
    )
    held = cross_sides(held, first_axes)
    g_value = dot_tn(normed, low_value).astype(BF16)
    opened = open_scatter(g_value.reshape(group_count, -1, width))
    g_small = dot_tn(low_small, normed)
    opened, g_small, held = lax.optimization_barrier((opened, g_small, held))
    held = run_halves(next_axes, bits, *held)
    branch, held = lax.optimization_barrier((branch, held))
    grad_ins = cross_sides(held, next_axes)
    sums = reduce(jnp.add, [item[0] for item in all_sums])
    sums_in = reduce(jnp.add, [item[1] for item in all_sums])[0:1]
    pair_sums = sums[8:13, :pair_width].reshape(1, -1)
    pair_sums = jnp.pad(pair_sums, ((0, 0), (0, -pair_sums.shape[1] % width_full)))
    team_rows = jnp.concatenate(
        [sums_in, pair_sums.reshape(-1, width_full)], axis=0
    )

    def split_rows(v, axis=0):
        high = lax.reduce_precision(v, 8, 7)
        both = jnp.concatenate([high, v - high], axis=0).astype(BF16)
        return jnp.pad(both, ((0, -both.shape[0] % 16), (0, 0)))

    def join_rows(v, count):
        return v[:count].astype(F32) + v[count : 2 * count].astype(F32)

    g_pair = g_small[:pair_width].reshape(sizes[2], sizes[4], 2, pair_part, width_full)

    def pair_stage(g_pair, team_rows, name, bit, axis, *waits):
        keep = lax.dynamic_index_in_dim(g_pair, bit, axis, keepdims=False)
        send = lax.dynamic_index_in_dim(g_pair, 1 - bit, axis, keepdims=False)
        count = send.size // width_full
        packed = jnp.concatenate(
            [send.astype(BF16).reshape(count, width_full), split_rows(team_rows)], axis=0
        )
        packed = after(exchange(packed, name), *waits)
        return (
            keep + packed[:count].reshape(keep.shape).astype(F32),
            team_rows + join_rows(packed[count:], team_rows.shape[0]),
        )

    g_pair, team_rows = pair_stage(g_pair, team_rows, "core", my_core, 2, *held)
    g_pair, team_rows = pair_stage(g_pair, team_rows, "near", my_near, 1)
    g_pair, team_rows, grad_ins, crossed = lax.optimization_barrier(
        (g_pair, team_rows, grad_ins, crossed)
    )
    send_back = run_close(
        partial(close_back_kernel, micro_count),
        group_count,
        take_map,
        dealt_tokens,
        dealt_back,
        norm_in[None, :],
        *grad_ins,
    )
    crossed = lax.optimization_barrier((crossed, send_back))[0]
    (g_out, g_gate), _ = finish_early(*crossed)
    g_out = g_out.T
    branch, send_back = lax.optimization_barrier((branch, send_back))
    send_out = run_close(
        close_out_kernel, group_count, take_map, dealt_tokens, branch, weight
    )
    out_pieces = [swap(piece, turned(perm)) for piece, perm in zip(send_out, deal_perms)]
    g_pair, team_rows = pair_stage(g_pair, team_rows, "row", my_row, 0, *send_back)
    g_small = jnp.concatenate(
        [
            g_pair,
            g_small[pair_width : pair_width + head_count],
            jnp.zeros((small_pad, width_full), F32),
        ],
        axis=0,
    )
    sums = jnp.concatenate(
        [sums[:5], gate_sums[0:1], sums[6:8], team_rows.reshape(-1, width)], axis=0
    )
    small_rows = g_small.shape[0]
    value_rows = width_full // group_count
    late = jnp.swapaxes(g_small.reshape(small_rows, group_count, -1), 0, 1)
    if value_rows != width:
        late = jnp.pad(late, ((0, 0), (0, 0), (0, width - value_rows)))
    crossed, finish, _ = scatter_groups([late], sums, split_rows, join_rows, waits=send_back)
    (late,), sums = finish(*crossed)
    crossed, finish, _ = scatter_groups([g_value], waits=send_back, opened=opened)
    (g_value,), _ = finish(*crossed)
    g_small = late[:, :value_rows]
    g_pair = g_small[:pair_part].T
    g_step = g_small[pair_part : pair_part + head_count].T
    pair_sums = sums[8 + width_full // width :].reshape(-1)[: 5 * pair_width]
    pair_sums = pair_sums.reshape(5, pair_width)
    in_sums = sums[8 : 8 + width_full // width]
    own_place = (my_row * sizes[4] + my_near) * sizes[3] + my_half
    pair_sums = lax.dynamic_slice_in_dim(pair_sums, own_place * pair_part, pair_part, 1)
    g_norm_in = in_sums.reshape(-1) / norm_in.astype(F32)
    g_skip = jnp.sum(sums[6].reshape(head_count, head_width), axis=1)

    block_out = run_pick(send_map, out_pieces, True)
    grad_tokens = undeal(send_back)
    return (
        block_out,
        grad_tokens,
        g_norm_in,
        g_gate,
        g_value,
        g_pair,
        g_step,
        sums[0:4],
        sums[4],
        pair_sums[0:4],
        pair_sums[4],
        sums[7, :head_count],
        sums[7, LANES : LANES + head_count],
        g_skip,
        sums[5],
        g_out,
    )


def solution(mesh):
    shape = mesh.devices.shape
    sizes = (shape[0] // 2, 2, shape[1], 2, shape[2] // 2)
    fine = jax.sharding.Mesh(mesh.devices.reshape(sizes), ALL)
    dp, team = ("pair", "core"), ("row", "half", "near")
    everything = ("pair", "core", "row", "half", "near")
    placed = (
        P(everything, None),
        P(everything, None),
        P(dp, None),
        P(),
        P(),
        P(dp, team),
        P(dp, team),
        P(dp, team),
        P(dp, team),
        P(None, team),
        P(team),
        P(None, team),
        P(team),
        P(team),
        P(team),
        P(team),
        P(team),
        P(team, dp),
    )
    return jax.shard_map(
        partial(per_device, sizes),
        mesh=fine,
        in_specs=placed,
        out_specs=(
            P(everything, None),
            P(everything, None),
            P(),
            P(dp, team),
            P(dp, team),
            P(dp, team),
            P(dp, team),
            P(None, team),
            P(team),
            P(None, team),
            P(team),
            P(team),
            P(team),
            P(team),
            P(team),
            P(team, dp),
        ),
        check_vma=False,
    )
```

```python
from functools import partial
from functools import reduce

import jax
import jax.numpy as jnp
import numpy as np
from jax import lax
from jax.experimental import pallas as pl
from jax.experimental.pallas import tpu as pltpu
from jax.sharding import PartitionSpec as P

EPS = 1e-05
EXACT = lax.Precision.HIGHEST
F32 = jnp.float32
BF16 = jnp.bfloat16
SUB = 128
ROWS = 256
LANES = 128
MIB = 1024 * 1024


def dot_nn(a, b):
    return jnp.dot(a, b, preferred_element_type=F32)


def dot_nt(a, b):
    return lax.dot_general(a, b, (((1,), (1,)), ((), ())), preferred_element_type=F32)


def dot_tn(a, b):
    return lax.dot_general(a, b, (((0,), (0,)), ((), ())), preferred_element_type=F32)


def sigmoid(v):
    return 1.0 / (1.0 + jnp.exp(-v))


def softplus(v):
    return jnp.maximum(v, 0.0) + jnp.log1p(jnp.exp(-jnp.abs(v)))


def split_two(v):
    high = v.astype(BF16)
    return high, (v - high.astype(F32)).astype(BF16)


def read_bounds(bounds_ref, micro):
    return [bounds_ref[micro, k] for k in range(bounds_ref.shape[1])]


def segment_of(places, bounds):
    total = (places >= bounds[0]).astype(jnp.int32)
    for bound in bounds[1:]:
        total = total + (places >= bound).astype(jnp.int32)
    return total


def segment_scalar(place, bounds):
    total = jnp.int32(0)
    for bound in bounds:
        total = total + jnp.where(place >= bound, 1, 0)
    return total


def iota(shape, axis):
    return lax.broadcasted_iota(jnp.int32, shape, axis)


def same_masks(places, bounds, count):
    own = segment_of(places, bounds)
    return [
        (segment_of(places - shift, bounds) == own) & (places >= shift) & (places < count)
        for shift in range(1, 4)
    ]


def expand_heads(parts, spread_ref):
    stacked = jnp.concatenate(parts, axis=0)
    high, low = split_two(stacked)
    lane = iota(stacked.shape, 1)
    joined = jnp.where(lane < 8, high.astype(F32), pltpu.roll(low.astype(F32), 8, 1))
    wide = dot_nn(joined.astype(BF16), spread_ref[...])
    sizes = np.cumsum([0] + [part.shape[0] for part in parts])
    return [wide[sizes[k] : sizes[k + 1]] for k in range(len(parts))]


def reduce_heads(v, gather_ref):
    high, low = split_two(v)
    return dot_nn(high, gather_ref[...]) + dot_nn(low, gather_ref[...])


def scan_frame(base, bounds, steps, rate, lower_ref):
    start_place = base
    col = start_place + iota((SUB, LANES), 0)
    row = start_place + iota((SUB, SUB), 1)
    seg_col = segment_of(col, bounds)
    seg_row = segment_of(row, bounds)
    allowed = (seg_col == seg_row) & (col >= row)
    last_seg = jnp.where(start_place > 0, segment_scalar(start_place - 1, bounds), -1)
    end_seg = segment_scalar(start_place + SUB - 1, bounds)
    log_decay = jnp.dot(
        lower_ref[...], steps * rate, preferred_element_type=F32, precision=EXACT
    )
    reach = jnp.where(seg_col == last_seg, jnp.exp(log_decay), 0.0)
    tail = jnp.where(
        seg_col == end_seg, jnp.exp(log_decay[SUB - 1 : SUB, :] - log_decay), 0.0
    )
    return allowed, log_decay, reach, tail


def decay_grid(log_decay, log_rows, head):
    gap = log_decay[:, head : head + 1] - log_rows[head : head + 1, :]
    return jnp.exp(jnp.minimum(gap, 0.0))


def forward_kernel(
    pair_count,
    bounds_ref,
    x_ref,
    norm_in_ref,
    w_value_ref,
    w_small_ref,
    taps_value_ref,
    taps_pair_ref,
    heads_ref,
    skip_ref,
    spread_ref,
    lower_ref,
    normed_ref,
    value_ref,
    conv_value_ref,
    pair_ref,
    conv_pair_ref,
    step_ref,
    scanned_ref,
    states_ref,
    halo_value,
    halo_pair,
    state,
):
    micro = pl.program_id(0)
    block = pl.program_id(1)
    count = pl.num_programs(1) * ROWS
    bounds = read_bounds(bounds_ref, micro)
    base = block * ROWS

    @pl.when(block == 0)
    def _():
        halo_value[...] = jnp.zeros_like(halo_value)
        halo_pair[...] = jnp.zeros_like(halo_pair)
        state[...] = jnp.zeros_like(state)

    x = x_ref[...].reshape(ROWS, x_ref.shape[-1]).astype(F32)
    rms = lax.rsqrt(jnp.mean(x * x, axis=1, keepdims=True) + EPS)
    normed = (x * rms * norm_in_ref[...].astype(F32)).astype(BF16)
    normed_ref[...] = normed
    value = dot_nn(normed, w_value_ref[...])
    small = dot_nt(normed, w_small_ref[...])
    pair_width = conv_pair_ref.shape[-1]
    pair = small[:, :pair_width]
    step = small[:, pair_width : pair_width + LANES]
    value_ref[...] = value.astype(BF16)
    pair_ref[...] = pair.astype(BF16)
    step_ref[...] = step

    places = base + iota((ROWS, LANES), 0)
    masks = same_masks(places, bounds, count)

    def convolve(v, halo, taps):
        longer = jnp.concatenate([halo, v], axis=0)
        width = v.shape[1]
        out = taps[4:5, :] + taps[3:4, :] * v
        for shift in range(1, 4):
            moved = pltpu.roll(longer, shift, 0)[8:, :]
            mask = jnp.concatenate([masks[shift - 1]] * (width // LANES), axis=1)
            out = out + jnp.where(mask, moved * taps[3 - shift : 4 - shift, :], 0.0)
        return out

    conv_value = convolve(value, halo_value[...], taps_value_ref[...])
    conv_pair = convolve(pair, halo_pair[...], taps_pair_ref[...])
    halo_value[...] = value[ROWS - 8 :, :]
    halo_pair[...] = pair[ROWS - 8 :, :]
    conv_value_ref[...] = conv_value
    conv_pair_ref[...] = conv_pair
    mixed = conv_value * sigmoid(conv_value)
    shared = (conv_pair * sigmoid(conv_pair)).astype(BF16)
    steps = softplus(step + heads_ref[0:1, :])
    rate = heads_ref[1:2, :]
    lane = iota((SUB, LANES), 1)
    left = lane < 64

    scanned_parts = []
    for sub in range(ROWS // SUB):
        rows = slice(sub * SUB, (sub + 1) * SUB)
        sub_steps = steps[rows]
        allowed, log_decay, reach, tail = scan_frame(
            base + sub * SUB, bounds, sub_steps, rate, lower_ref
        )
        steps_wide, reach_wide, tail_wide = expand_heads(
            [sub_steps, reach, tail], spread_ref
        )
        log_rows = log_decay.T
        keys = shared[rows, :LANES]
        reads = shared[rows, LANES:]
        scores = jnp.where(allowed, dot_nt(reads, keys), 0.0)
        stepped = mixed[rows] * steps_wide
        stepped_low = stepped.astype(BF16)
        held = state[...]
        held_low = held.astype(BF16)
        states_ref[sub] = held_low
        outside = dot_nn(reads, held_low) * reach_wide
        inside = []
        for p in range(pair_count):
            cols = slice(p * LANES, (p + 1) * LANES)
            grids = [
                (scores * decay_grid(log_decay, log_rows, 2 * p + k)).astype(BF16)
                for k in range(2)
            ]
            both = stepped_low[:, cols]
            zero = jnp.zeros_like(both)
            inside.append(
                dot_nn(
                    jnp.concatenate(grids, axis=1),
                    jnp.concatenate(
                        [jnp.where(left, both, zero), jnp.where(left, zero, both)], axis=0
                    ),
                )
            )
        scanned_parts.append(
            jnp.concatenate(inside, axis=1) + outside + mixed[rows] * skip_ref[...]
        )
        state[...] = held * reach_wide[SUB - 1 : SUB, :] + dot_tn(
            keys, (stepped * tail_wide).astype(BF16)
        )
    scanned_ref[...] = jnp.concatenate(scanned_parts, axis=0)


def back_kernel(
    live_ids,
    bounds_ref,
    back_ref,
    normed_ref,
    w_gate_ref,
    w_out_ref,
    norm_gate_ref,
    scanned_ref,
    gate_ref,
    scaled_ref,
    grad_normed_ref,
    stats_ref,
):
    micro = pl.program_id(0)
    bounds = read_bounds(bounds_ref, micro)
    base = pl.program_id(1) * ROWS
    places = base + iota((ROWS, LANES), 0)
    live = segment_of(places, bounds) < live_ids
    gate = dot_nn(normed_ref[...], w_gate_ref[...])
    gate_ref[...] = gate
    gated = scanned_ref[...] * (gate * sigmoid(gate))
    normed_gated = gated * norm_gate_ref[...]
    scaled_ref[...] = normed_gated.astype(BF16).reshape(scaled_ref.shape)
    grad = dot_nn(back_ref[...].reshape(ROWS, back_ref.shape[-1]), w_out_ref[...])
    live_wide = jnp.concatenate([live] * (grad.shape[1] // LANES), axis=1)
    grad = jnp.where(live_wide, grad, 0.0)
    grad_normed_ref[...] = grad.astype(BF16)
    ones = jnp.ones((8, gated.shape[1]), BF16)
    high, low = split_two(gated * gated)
    square = dot_nt(ones, high) + dot_nt(ones, low)
    high, low = split_two(grad * normed_gated)
    cross = dot_nt(ones, high) + dot_nt(ones, low)
    stats_ref[...] = jnp.where(iota(cross.shape, 0) == 0, square, cross)


def gate_kernel(
    live_ids,
    inner_full,
    bounds_ref,
    stats_ref,
    grad_normed_ref,
    gate_ref,
    scanned_ref,
    norm_gate_ref,
    low_gate_ref,
    normed_out_ref,
    grad_scanned_ref,
    sums_ref,
):
    micro = pl.program_id(0)
    block = pl.program_id(1)
    bounds = read_bounds(bounds_ref, micro)

    @pl.when((micro == 0) & (block == 0))
    def _():
        sums_ref[...] = jnp.zeros_like(sums_ref)

    tiles = gate_ref.shape[1] // LANES
    live = segment_of(block * ROWS + iota((ROWS, LANES), 0), bounds) < live_ids
    gate = gate_ref[...]
    scanned = scanned_ref[...]
    grad_normed = grad_normed_ref[...].astype(F32)
    norm_gate = norm_gate_ref[...]
    stats = stats_ref[...].T / inner_full
    spread = lax.rsqrt(stats[:, 0:1] + EPS)
    cross = stats[:, 1:2]
    sg = sigmoid(gate)
    act = gate * sg
    gated = scanned * act
    normed_gated = gated * spread
    live_wide = jnp.concatenate([live] * tiles, axis=1)
    normed_out = jnp.where(live_wide, normed_gated * norm_gate, 0.0).astype(BF16)
    normed_out_ref[...] = normed_out.reshape(normed_out_ref.shape)
    grad_gated = spread * (grad_normed * norm_gate - normed_gated * (spread * cross))
    grad_scanned_ref[...] = (grad_gated * act).astype(BF16)
    low_gate_ref[...] = (
        grad_gated * scanned * (sg * (1.0 + gate * (1.0 - sg)))
    ).astype(BF16)
    sums_ref[0:1, :] += jnp.sum(grad_normed * normed_gated, axis=0, keepdims=True)


def backward_kernel(
    pair_count,
    micro,
    first,
    apart,
    bounds_ref,
    grad_scanned_ref,
    low_gate_ref,
    normed_ref,
    value_ref,
    conv_value_ref,
    pair_ref,
    conv_pair_ref,
    step_ref,
    scanned_ref,
    states_ref,
    w_value_ref,
    w_gate_ref,
    w_small_ref,
    taps_value_ref,
    taps_pair_ref,
    heads_ref,
    skip_ref,
    spread_ref,
    gather_ref,
    lower_ref,
    upper_ref,
    *rest,
):
    if not first:
        rest = rest[2:]
    (
        low_value_ref,
        low_small_ref,
        *grad_in_refs,
        sums_ref,
        sums_in_ref,
        halo_value,
        halo_pair,
        state,
    ) = rest
    turn = pl.program_id(0)
    block_count = pl.num_programs(0)
    block = block_count - 1 - turn
    count = block_count * ROWS
    bounds = read_bounds(bounds_ref, micro)
    base = block * ROWS

    @pl.when(turn == 0)
    def _():
        sums_ref[...] = jnp.zeros_like(sums_ref)
        sums_in_ref[...] = jnp.zeros_like(sums_in_ref)
        halo_value[...] = jnp.zeros_like(halo_value)
        halo_pair[...] = jnp.zeros_like(halo_pair)
        state[...] = jnp.zeros_like(state)

    width = value_ref.shape[1]
    scanned = scanned_ref[...]
    grad_low_all = grad_scanned_ref[...]
    grad_scanned = grad_low_all.astype(F32)
    low_gate = low_gate_ref[...]

    conv_value = conv_value_ref[...]
    sig_value = sigmoid(conv_value)
    mixed = conv_value * sig_value
    conv_pair = conv_pair_ref[...]
    sig_pair = sigmoid(conv_pair)
    shared = (conv_pair * sig_pair).astype(BF16)
    step_in = step_ref[...] + heads_ref[0:1, :]
    steps = softplus(step_in)
    rate = heads_ref[1:2, :]
    skip = skip_ref[...]
    lane = iota((SUB, LANES), 1)
    left = lane < 64

    grad_mixed_parts = []
    grad_shared_parts = []
    grad_step_parts = []
    decay_sum = jnp.zeros((1, LANES), F32)
    for sub in reversed(range(ROWS // SUB)):
        rows = slice(sub * SUB, (sub + 1) * SUB)
        sub_steps = steps[rows]
        allowed, log_decay, reach, tail = scan_frame(
            base + sub * SUB, bounds, sub_steps, rate, lower_ref
        )
        steps_wide, reach_wide, tail_wide = expand_heads(
            [sub_steps, reach, tail], spread_ref
        )
        log_rows = log_decay.T
        keys = shared[rows, :LANES]
        reads = shared[rows, LANES:]
        scores = jnp.where(allowed, dot_nt(reads, keys), 0.0)
        sub_mixed = mixed[rows]
        stepped = sub_mixed * steps_wide
        stepped_low = stepped.astype(BF16)
        grad_y = grad_scanned[rows]
        grad_low = grad_low_all[rows]
        held_low = states_ref[sub]
        later = state[...]
        later_low = later.astype(BF16)
        grad_scores = jnp.zeros((SUB, SUB), F32)
        inner = []
        for p in range(pair_count):
            cols = slice(p * LANES, (p + 1) * LANES)
            both_x = stepped_low[:, cols]
            both_y = grad_low[:, cols]
            zero = jnp.zeros_like(both_y)
            halves = [jnp.where(left, both_y, zero), jnp.where(left, zero, both_y)]
            grids = []
            for k in range(2):
                fade = decay_grid(log_decay, log_rows, 2 * p + k)
                grids.append((scores * fade).astype(BF16))
                grad_scores = grad_scores + dot_nt(halves[k], both_x) * fade
            inner.append(
                dot_tn(jnp.concatenate(grids, axis=0), jnp.concatenate(halves, axis=0))
            )
        grad_scores = jnp.where(allowed, grad_scores, 0.0).astype(BF16)
        tail_part = tail_wide * dot_nn(keys, later_low)
        grad_stepped = jnp.concatenate(inner, axis=1) + tail_part
        reached = (grad_y * reach_wide).astype(BF16)
        tailed = (stepped * tail_wide).astype(BF16)
        grad_reads = dot_nn(grad_scores, keys) + dot_nt(reached, held_low)
        grad_keys = dot_tn(grad_scores, reads) + dot_nt(tailed, later_low)
        stepped_back = stepped_low.astype(F32)
        per_log = reduce_heads(
            grad_y * (scanned[rows] - skip * sub_mixed)
            - stepped_back * grad_stepped,
            gather_ref,
        )
        kept_wide = reach_wide[SUB - 1 : SUB, :]
        at_end = jnp.sum(stepped_back * tail_part, axis=0, keepdims=True) + kept_wide * jnp.sum(
            later * held_low.astype(F32), axis=0, keepdims=True
        )
        at_end = reduce_heads(jnp.broadcast_to(at_end, (8, width)), gather_ref)[0:1, :]
        grad_log = (
            jnp.dot(upper_ref[...], per_log, preferred_element_type=F32, precision=EXACT)
            + at_end
        )
        decay_sum = decay_sum + jnp.sum(grad_log * sub_steps, axis=0, keepdims=True) * rate
        grad_steps = reduce_heads(grad_stepped * sub_mixed, gather_ref) + rate * grad_log
        grad_step_parts.insert(0, grad_steps)
        grad_shared_parts.insert(0, jnp.concatenate([grad_keys, grad_reads], axis=1))
        grad_mixed_parts.insert(0, grad_stepped * steps_wide + skip * grad_y)
        state[...] = later * kept_wide + dot_tn(reads, reached)
    grad_mixed = jnp.concatenate(grad_mixed_parts, axis=0)
    grad_shared = jnp.concatenate(grad_shared_parts, axis=0)
    grad_step = jnp.concatenate(grad_step_parts, axis=0) * sigmoid(step_in)

    longer_places = base + iota((ROWS + 8, LANES), 0)
    masks = same_masks(longer_places, bounds, count)

    def convolve_back(q, halo, v, taps):
        longer = jnp.concatenate([q, halo], axis=0)
        grad = taps[3:4, :] * q
        tap_sums = [jnp.sum(v * q, axis=0, keepdims=True)]
        for shift in range(1, 4):
            mask = jnp.concatenate([masks[shift - 1]] * (q.shape[1] // LANES), axis=1)
            kept = jnp.where(mask, longer, 0.0)
            moved = pltpu.roll(kept, ROWS + 8 - shift, 0)[:ROWS, :]
            grad = grad + taps[3 - shift : 4 - shift, :] * moved
            tap_sums.insert(0, jnp.sum(v * moved, axis=0, keepdims=True))
        return grad, tap_sums + [jnp.sum(q, axis=0, keepdims=True)]

    q_value = grad_mixed * (sig_value * (1.0 + conv_value * (1.0 - sig_value)))
    q_pair = grad_shared * (sig_pair * (1.0 + conv_pair * (1.0 - sig_pair)))
    grad_value, value_sums = convolve_back(
        q_value, halo_value[...], value_ref[...].astype(F32), taps_value_ref[...]
    )
    grad_pair, pair_sums = convolve_back(
        q_pair, halo_pair[...], pair_ref[...].astype(F32), taps_pair_ref[...]
    )
    halo_value[...] = q_value[:8, :]
    halo_pair[...] = q_pair[:8, :]
    low_value = grad_value.astype(BF16)
    low_small = jnp.concatenate([grad_pair, grad_step], axis=1).astype(BF16)
    low_value_ref[...] = low_value
    low_small_ref[...] = low_small
    grad_in = (
        dot_nt(low_gate, w_gate_ref[...])
        + dot_nt(low_value, w_value_ref[...])
        + dot_nn(low_small, w_small_ref[...])
    )
    grad_in_low = grad_in.astype(BF16).reshape(grad_in_refs[0].shape)
    if apart:
        mine = block % 2 == bounds_ref[bounds_ref.shape[0] - 1, 0]

        @pl.when(mine)
        def _():
            grad_in_refs[0][...] = grad_in_low

        @pl.when(jnp.logical_not(mine))
        def _():
            grad_in_refs[1][...] = grad_in_low

    else:
        grad_in_refs[0][...] = grad_in_low
    sums_in_ref[0:1, :] += jnp.sum(grad_in * normed_ref[...].astype(F32), axis=0, keepdims=True)
    skip_sum = jnp.sum(grad_scanned * mixed, axis=0, keepdims=True)
    step_sum = jnp.sum(grad_step, axis=0, keepdims=True)
    for k in range(5):
        sums_ref[k : k + 1, :] += value_sums[k]
    sums_ref[6:7, :] += skip_sum
    sums_ref[7:8, :LANES] += step_sum
    sums_ref[7:8, LANES : 2 * LANES] += decay_sum
    for k in range(5):
        sums_ref[8 + k : 9 + k, : pair_sums[k].shape[1]] += pair_sums[k]


def whole_spec(shape):
    return pl.BlockSpec(shape, lambda *_: (0,) * len(shape))


def smem_spec():
    return pl.BlockSpec(memory_space=pltpu.SMEM)


def kernel_params(size):
    return pltpu.CompilerParams(vmem_limit_bytes=size * MIB)


def head_constants(head_count, head_width):
    width = head_count * head_width
    spread = np.zeros((LANES, width), np.float32)
    for h in range(head_count):
        spread[h, h * head_width : (h + 1) * head_width] = 1.0
        spread[h + 8, h * head_width : (h + 1) * head_width] = 1.0
    gather = np.zeros((width, LANES), np.float32)
    for h in range(head_count):
        gather[h * head_width : (h + 1) * head_width, h] = 1.0
    lower = np.tril(np.ones((SUB, SUB), np.float32))
    return (
        jnp.asarray(spread, BF16),
        jnp.asarray(gather, BF16),
        jnp.asarray(lower),
        jnp.asarray(lower.T),
    )


def seat_spec(piece, cols):
    return pl.BlockSpec((None, 2, None, piece, cols), lambda b, i: (i // 2, 0, i % 2, b, 0))


def seat_view(item):
    return item.reshape((item.shape[0] // 4, 2, 2) + item.shape[1:])


def cost(flops, count, moved):
    return pl.CostEstimate(flops=int(flops), transcendentals=int(count), bytes_accessed=int(moved))


def run_forward(bounds, rows, weights, consts, micro_count, piece):
    block_len = 8 * piece
    blocks = block_len // ROWS
    norm_in, w_value, _, w_small, taps_value, taps_pair, heads, skip = weights
    spread, _, lower, _ = consts
    full = rows.shape[4]
    width = w_value.shape[1]
    pair_width = taps_pair.shape[1]
    length = micro_count * block_len
    subs = ROWS // SUB

    def by_rows(cols):
        return pl.BlockSpec((ROWS, cols), lambda b, i: (b * blocks + i, 0))

    wholes = [norm_in, w_value, w_small, taps_value, taps_pair, heads, skip, spread, lower]
    widths = [width, width, pair_width, pair_width, LANES, width]
    types = [BF16, F32, BF16, F32, F32, F32]
    return pl.pallas_call(
        partial(forward_kernel, width // LANES),
        grid=(micro_count, blocks),
        in_specs=[smem_spec(), seat_spec(piece, full)] + [whole_spec(item.shape) for item in wholes],
        out_specs=[by_rows(full)]
        + [by_rows(cols) for cols in widths]
        + [
            pl.BlockSpec((subs, LANES, width), lambda b, i: (b * blocks + i, 0, 0)),
        ],
        out_shape=[jax.ShapeDtypeStruct((length, full), BF16)]
        + [jax.ShapeDtypeStruct((length, cols), kind) for cols, kind in zip(widths, types)]
        + [
            jax.ShapeDtypeStruct((length // SUB, LANES, width), BF16),
        ],
        scratch_shapes=[
            pltpu.VMEM((8, width), F32),
            pltpu.VMEM((8, pair_width), F32),
            pltpu.VMEM((LANES, width), F32),
        ],
        compiler_params=kernel_params(56),
        cost_estimate=cost(length * full * width * 12, length * width * 8, length * width * 40),
        name="forward",
    )(bounds, rows, *wholes)


def run_back(bounds, back, normed, w_gate, w_out, norm_gate, scanned, live_ids, micro_count, piece):
    block_len = 8 * piece
    blocks = block_len // ROWS
    length, width = scanned.shape
    full = normed.shape[1]

    def by_rows(cols):
        return pl.BlockSpec((ROWS, cols), lambda b, i: (b * blocks + i, 0))

    by_cols = pl.BlockSpec((8, ROWS), lambda b, i: (0, b * blocks + i))
    return pl.pallas_call(
        partial(back_kernel, live_ids),
        grid=(micro_count, blocks),
        in_specs=[
            smem_spec(),
            seat_spec(piece, full),
            by_rows(full),
            whole_spec(w_gate.shape),
            whole_spec(w_out.shape),
            whole_spec(norm_gate.shape),
            by_rows(width),
        ],
        out_specs=[by_rows(width), seat_spec(piece, width), by_rows(width), by_cols],
        out_shape=[
            jax.ShapeDtypeStruct((length, width), F32),
            jax.ShapeDtypeStruct(back.shape[:4] + (width,), BF16),
            jax.ShapeDtypeStruct((length, width), BF16),
            jax.ShapeDtypeStruct((8, length), F32),
        ],
        compiler_params=kernel_params(56),
        cost_estimate=cost(length * full * width * 4, length * width, length * width * 30),
        name="back",
    )(bounds, back, normed, w_gate, w_out, norm_gate, scanned)


def run_gate(bounds, stats, grad_normed, gate, scanned, norm_gate, live_ids, inner_full, micro_count, piece):
    block_len = 8 * piece
    blocks = block_len // ROWS
    length, width = gate.shape
    by_rows = pl.BlockSpec((ROWS, width), lambda b, i: (b * blocks + i, 0))
    return pl.pallas_call(
        partial(gate_kernel, live_ids, inner_full),
        grid=(micro_count, blocks),
        in_specs=[
            smem_spec(),
            pl.BlockSpec((8, ROWS), lambda b, i: (0, b * blocks + i)),
            by_rows,
            by_rows,
            by_rows,
            whole_spec(norm_gate.shape),
        ],
        out_specs=[
            by_rows,
            seat_spec(piece, width),
            by_rows,
            whole_spec((8, width)),
        ],
        out_shape=[
            jax.ShapeDtypeStruct((length, width), BF16),
            jax.ShapeDtypeStruct((blocks // 2, 2, 2, micro_count * piece, width), BF16),
            jax.ShapeDtypeStruct((length, width), BF16),
            jax.ShapeDtypeStruct((8, width), F32),
        ],
        compiler_params=kernel_params(32),
        cost_estimate=cost(length * width * 20, length * width, length * width * 20),
        name="gate",
    )(bounds, stats, grad_normed, gate, scanned, norm_gate)


def run_backward(bounds, grad_scanned, low_gate, kept, weights, consts, micro, piece, earlier, apart):
    block_len = 8 * piece
    blocks = block_len // ROWS
    normed, value, conv_value, pair, conv_pair, step, scanned, states = kept
    _, w_value, w_gate, w_small, taps_value, taps_pair, heads, skip = weights
    spread, gather, lower, upper = consts
    full = normed.shape[1]
    length, width = value.shape
    pair_width = pair.shape[1]
    subs = ROWS // SUB

    def place(i):
        return micro * blocks + blocks - 1 - i

    def by_rows(item):
        return pl.BlockSpec((ROWS, item.shape[1]), lambda i: (place(i), 0))

    if apart:
        row_blocks = [
            pl.BlockSpec((None, 2, piece, full), lambda i: ((blocks - 1 - i) // 2, 0, 0, 0))
        ] * 2
        row_shapes = [jax.ShapeDtypeStruct((blocks // 2, 2, piece, full), BF16)] * 2
    else:
        row_blocks = [
            pl.BlockSpec(
                (None, 2, None, piece, full),
                lambda i: ((blocks - 1 - i) // 2, 0, (blocks - 1 - i) % 2, 0, 0),
            )
        ]
        row_shapes = [jax.ShapeDtypeStruct((blocks // 2, 2, 2, piece, full), BF16)]
    rowwise = [grad_scanned, low_gate, normed, value, conv_value, pair, conv_pair, step, scanned]
    wholes = [w_value, w_gate, w_small, taps_value, taps_pair, heads, skip, spread, gather, lower, upper]
    outs = [
        jax.ShapeDtypeStruct((length, width), BF16),
        jax.ShapeDtypeStruct((length, w_small.shape[0]), BF16),
        *row_shapes,
        jax.ShapeDtypeStruct((16, width), F32),
        jax.ShapeDtypeStruct((8, full), F32),
    ]
    ins = [bounds] + rowwise + [states] + wholes
    return pl.pallas_call(
        partial(backward_kernel, width // LANES, micro, earlier is None, apart),
        grid=(blocks,),
        in_specs=[smem_spec()]
        + [by_rows(item) for item in rowwise]
        + [pl.BlockSpec((subs, LANES, width), lambda i: (place(i), 0, 0))]
        + [whole_spec(item.shape) for item in wholes]
        + ([] if earlier is None else [pl.BlockSpec(memory_space=pl.ANY)] * 2),
        out_specs=[by_rows(item) for item in outs[:2]]
        + row_blocks
        + [whole_spec(item.shape) for item in outs[-2:]],
        out_shape=outs,
        input_output_aliases={} if earlier is None else {len(ins): 0, len(ins) + 1: 1},
        scratch_shapes=[
            pltpu.VMEM((8, width), F32),
            pltpu.VMEM((8, pair_width), F32),
            pltpu.VMEM((LANES, width), F32),
        ],
        compiler_params=kernel_params(56),
        cost_estimate=cost(block_len * full * width * 14, block_len * width * 16, block_len * width * 40),
        name="backward",
    )(*ins, *([] if earlier is None else earlier))


def deal_kernel(
    group_shift,
    place_ref,
    listed_ref,
    listed_cols_ref,
    own_ref,
    own_col_ref,
    tokens_ref,
    cotangent_ref,
    send_map_ref,
    take_map_ref,
    *piece_refs,
):
    start, group, target = place_ref[0], place_ref[1], place_ref[2]
    share = tokens_ref.shape[0]
    group_count = listed_cols_ref.shape[1]
    quota = share // group_count
    natural = start + iota((share, share), 1)
    found = []
    for g in range(group_count):
        hits = (listed_cols_ref[:, g : g + 1] == natural).astype(F32)
        found.append(jnp.sum(hits, axis=0, keepdims=True))
    pad = -group_count % 8
    found = jnp.concatenate(found + [jnp.zeros((pad, share), F32)] * (pad > 0), axis=0)
    before = (iota((share, share), 0) < iota((share, share), 1)).astype(BF16)
    rank = dot_nn(found.astype(BF16), before)
    slot = (iota(found.shape, 0) ^ group) * quota
    place = jnp.sum(found * (rank + slot.astype(F32)), axis=0, keepdims=True)
    send_map = (iota((share, share), 0).astype(F32) == place).astype(BF16)
    send_map_ref[...] = send_map
    own_row = jnp.broadcast_to(own_ref[...], (share, share))
    own_col = jnp.broadcast_to(own_col_ref[...], (share, share))
    src_row = lax.shift_right_logical(own_row, group_shift)
    src_col = lax.shift_right_logical(own_col, group_shift)
    ahead = ((src_row == src_col) & (own_row < own_col)).astype(F32)
    order = jnp.sum(ahead, axis=1, keepdims=True)
    wanted = ((src_col ^ target) * quota).astype(F32) + order
    take_map_ref[...] = (iota((share, share), 1).astype(F32) == wanted).astype(BF16)
    write_pieces(piece_refs[:group_count], dot_nn(send_map, tokens_ref[...]))
    write_pieces(piece_refs[group_count:], dot_nn(send_map, cotangent_ref[...]))


def write_pieces(piece_refs, rows):
    size = rows.shape[0] // len(piece_refs)
    for k, piece_ref in enumerate(piece_refs):
        piece_ref[...] = rows[k * size : (k + 1) * size].astype(BF16)


def join_pieces(piece_refs):
    if piece_refs[0].shape[0] % 16 == 0:
        return jnp.concatenate([piece_ref[...] for piece_ref in piece_refs], axis=0)
    wide = [piece_ref[...].astype(F32) for piece_ref in piece_refs]
    return jnp.concatenate(wide, axis=0).astype(BF16)


def run_deal(place, listed, own, tokens, cotangent, group_len):
    share, width = tokens.shape
    group_count = listed.shape[0]
    vmem = pl.BlockSpec(memory_space=pltpu.VMEM)
    piece = jax.ShapeDtypeStruct((share // group_count, width), BF16)
    outs = pl.pallas_call(
        partial(deal_kernel, group_len.bit_length() - 1),
        in_specs=[smem_spec()] + [vmem] * 6,
        out_specs=[vmem] * (2 + 2 * group_count),
        out_shape=[jax.ShapeDtypeStruct((share, share), BF16)] * 2
        + [piece] * (2 * group_count),
        compiler_params=kernel_params(16),
        name="deal",
    )(place, listed, listed.T, own[None, :], own[:, None], tokens, cotangent)
    return outs[2 : 2 + group_count], outs[2 + group_count :], outs[0], outs[1]


def pick_kernel(transposed, extra_rows, map_ref, *refs):
    out_ref = refs[-1]
    pieces = refs[:-1]
    if extra_rows:
        share = out_ref.shape[0] - extra_rows
        out_ref[share:, :] = pieces[-1][...]
        pieces = pieces[:-1]
    dot = dot_tn if transposed else dot_nn
    rows = dot(map_ref[...], join_pieces(pieces)).astype(BF16)
    if extra_rows:
        out_ref[:share, :] = rows
    else:
        out_ref[...] = rows


def run_pick(take_map, pieces, transposed, extra=None):
    vmem = pl.BlockSpec(memory_space=pltpu.VMEM)
    extra_rows = 0 if extra is None else extra.shape[0]
    items = list(pieces) + ([] if extra is None else [extra])
    return pl.pallas_call(
        partial(pick_kernel, transposed, extra_rows),
        in_specs=[vmem] * (1 + len(items)),
        out_specs=vmem,
        out_shape=jax.ShapeDtypeStruct(
            (take_map.shape[0] + extra_rows, pieces[0].shape[1]), BF16
        ),
        compiler_params=kernel_params(16),
        name="pick",
    )(take_map, *items)


def close_out_kernel(map_ref, dealt_ref, branch_ref, weight_ref, *piece_refs):
    shape = dealt_ref.shape
    out = dealt_ref[...].astype(F32) + weight_ref[...] * branch_ref[...].reshape(shape).astype(F32)
    write_pieces(piece_refs, dot_tn(map_ref[...], out.astype(BF16)))


def close_back_kernel(
    grad_count, map_ref, dealt_ref, back_ref, norm_in_ref, *refs
):
    grad_refs, piece_refs = refs[: 2 * grad_count], refs[2 * grad_count :]
    x = dealt_ref[...].astype(F32)
    rms = lax.rsqrt(jnp.mean(x * x, axis=1, keepdims=True) + EPS)
    xhat = x * rms
    grad = jnp.concatenate(
        [
            grad_refs[2 * k][...] + grad_refs[2 * k + 1][...].astype(F32)
            for k in range(grad_count)
        ],
        axis=0,
    )
    win = grad * norm_in_ref[...].astype(F32)
    cross = jnp.mean(win * xhat, axis=1, keepdims=True)
    out = back_ref[...].astype(F32) + rms * (win - xhat * cross)
    write_pieces(piece_refs, dot_tn(map_ref[...], out.astype(BF16)))


def run_close(body, group_count, take_map, dealt, *items):
    share, width = take_map.shape[0], dealt.shape[1]
    whole = [whole_spec(item.shape) for item in items]
    return pl.pallas_call(
        body,
        grid=(1,),
        in_specs=[whole_spec(take_map.shape), whole_spec((share, width))] + whole,
        out_specs=[whole_spec((share // group_count, width))] * group_count,
        out_shape=[jax.ShapeDtypeStruct((share // group_count, width), BF16)] * group_count,
        compiler_params=kernel_params(16),
        name="close",
    )(take_map, dealt, *items)


def halves_kernel(axes, bits_ref, *refs):
    count = len(axes)
    for k, (axis, bit_index) in enumerate(axes):
        held_ref, arrived_ref = refs[2 * k], refs[2 * k + 1]
        keep_ref, send_ref = refs[2 * (count + k)], refs[2 * (count + k) + 1]
        bit = bits_ref[bit_index]

        def total(where):
            return held_ref[where].astype(F32) + arrived_ref[where].astype(F32)

        if len(held_ref.shape) == 3:
            keep_ref[...] = total(bit)
            send_ref[...] = total(1 - bit).astype(BF16)
            continue
        for other in range(2):
            here = (other, bit) if axis == 1 else (bit, other)
            there = (other, 1 - bit) if axis == 1 else (1 - bit, other)
            keep_ref[other] = total(here)
            send_ref[other] = total(there).astype(BF16)


def run_halves(axes, bits, *items):
    vmem = pl.BlockSpec(memory_space=pltpu.VMEM)
    outs = []
    for item in items[::2]:
        outs.append(jax.ShapeDtypeStruct(item.shape[1:], F32))
        outs.append(jax.ShapeDtypeStruct(item.shape[1:], BF16))
    return pl.pallas_call(
        partial(halves_kernel, axes),
        in_specs=[smem_spec()] + [vmem] * len(items),
        out_specs=[vmem] * len(outs),
        out_shape=outs,
        compiler_params=kernel_params(56),
        name="halves",
    )(bits, *items)


ALL = ("pair", "core", "row", "half", "near")
TEAM = ("row", "near", "core")


def make_perm(sizes, move):
    ranks = np.arange(int(np.prod(sizes))).reshape(sizes)
    return [
        (int(ranks[where]), int(ranks[move(*where)])) for where in np.ndindex(*sizes)
    ]


def turned(perm):
    return [(target, source) for source, target in perm]


def swap(v, perm):
    return lax.ppermute(v, ALL, perm)


def choose(bit, first, second, axis):
    return jnp.where(
        bit == 0,
        jnp.concatenate([first, second], axis=axis),
        jnp.concatenate([second, first], axis=axis),
    )


def per_device(
    sizes,
    tokens,
    cotangent,
    seq_lengths,
    token_order,
    norm_in,
    w_gate,
    w_value,
    w_pair,
    w_step,
    conv_value,
    bias_value,
    conv_pair,
    bias_pair,
    step_bias,
    decay_log,
    skip_gain,
    norm_gate,
    w_out,
):
    pair_count = sizes[0]
    group_count = sizes[0] * sizes[1]
    team_size = sizes[2] * sizes[3] * sizes[4]
    my_pair, my_core, my_row, my_half, my_near = [lax.axis_index(name) for name in ALL]
    group = my_pair * 2 + my_core
    target = my_pair * 2 + my_half
    member = my_row * (sizes[3] * sizes[4]) + my_half * sizes[4] + my_near
    seat = my_row * (sizes[3] * sizes[4]) + my_core * sizes[4] + my_near

    share_len, width_full = tokens.shape
    quota_len = share_len // group_count
    micro_count = seq_lengths.shape[0]
    piece_len = share_len // micro_count
    block_len = piece_len * team_size
    group_len = share_len * team_size
    width = w_gate.shape[1]
    inner_full = width * team_size
    head_count = step_bias.shape[0]
    head_width = width // head_count
    pair_part = w_pair.shape[1]
    pair_width = pair_part * team_size
    small_width = pair_width + LANES

    deal_perms = [
        make_perm(
            sizes,
            lambda p, c, r, h, n, e=e: (p ^ (e // 2), h, r, c ^ (e % 2), n),
        )
        for e in range(group_count)
    ]
    cross_perms = [
        make_perm(sizes, lambda p, c, r, h, n, f=f: (p, h, r, c ^ f, n)) for f in range(2)
    ]
    pair_bits = [k for k in range(pair_count.bit_length() - 1)]
    pair_perms = [
        make_perm(sizes, lambda p, c, r, h, n, k=k: (p ^ (1 << k), c, r, h, n))
        for k in pair_bits
    ]

    team_perms = {
        "core": make_perm(sizes, lambda p, c, r, h, n: (p, 1 - c, r, h, n)),
        "near": make_perm(sizes, lambda p, c, r, h, n: (p, c, r, h, 1 - n)),
        "row": make_perm(sizes, lambda p, c, r, h, n: (p, c, 1 - r, h, n)),
    }

    def after(v, *others):
        return lax.optimization_barrier((v,) + others)[0]

    def cross_groups(block):
        return swap(block, cross_perms[0]), swap(block, cross_perms[1])

    def gather_groups(crossed, axis):
        first, second = crossed
        current = choose(my_half, first, second, axis)
        for k in pair_bits:
            other = swap(current, pair_perms[k])
            current = choose((my_pair >> k) & 1, current, other, axis)
        return current

    def open_scatter(part):
        half = part.shape[0] // 2
        bit = (my_pair >> pair_bits[-1]) & 1
        kept = lax.dynamic_slice_in_dim(part, bit * half, half, 0)
        sent = lax.dynamic_slice_in_dim(part, (1 - bit) * half, half, 0)
        return kept, sent.astype(BF16)

    def scatter_groups(
        parts, sums=None, split=None, join=None, waits=(), bound=(), opened=None
    ):
        def pack(items):
            items = [item.astype(BF16) for item in items]
            if sums is not None:
                rows = split(sums)
                items.append(jnp.broadcast_to(rows, items[0].shape[:-2] + rows.shape))
            return jnp.concatenate(items, axis=-2)

        if opened is not None:
            parts = [opened[0]]
        marks = np.cumsum([0] + [part.shape[-2] for part in parts])

        def unpack(v, total):
            items = [
                v[..., int(marks[k]) : int(marks[k + 1]), :].astype(F32)
                for k in range(len(parts))
            ]
            if total is None:
                return items, None
            first = v if v.ndim == 2 else v[0]
            return items, total + join(first[int(marks[-1]) :], total.shape[0])

        for k in reversed(pair_bits):
            if opened is not None:
                arrived = after(swap(opened[1], pair_perms[k]), *waits)
                parts = [opened[0].astype(F32) + arrived.astype(F32)]
                opened = None
                continue
            half = parts[0].shape[0] // 2
            bit = (my_pair >> k) & 1
            kept = [lax.dynamic_slice_in_dim(part, bit * half, half, 0) for part in parts]
            sent = [lax.dynamic_slice_in_dim(part, (1 - bit) * half, half, 0) for part in parts]
            arrived = after(swap(pack(sent), pair_perms[k]), *waits)
            arrived, sums = unpack(arrived, sums)
            parts = [mine.astype(F32) + other for mine, other in zip(kept, arrived)]
        first = [lax.dynamic_index_in_dim(part, my_half, 0, keepdims=False) for part in parts]
        second = [
            lax.dynamic_index_in_dim(part, 1 - my_half, 0, keepdims=False) for part in parts
        ]
        first, second, *bound = lax.optimization_barrier((pack(first), pack(second), *bound))
        first = swap(first, turned(cross_perms[0]))
        second = swap(second, turned(cross_perms[1]))

        def finish(first, second):
            zero = None if sums is None else jnp.zeros_like(sums)
            first, sums_first = unpack(first, zero)
            second, sums_second = unpack(second, zero)
            total = [mine + other for mine, other in zip(first, second)]
            return total, None if sums is None else sums_first + sums_second

        return (first, second), finish, bound

    listed = lax.dynamic_index_in_dim(
        token_order.reshape(group_count, micro_count, team_size, piece_len),
        member,
        2,
        keepdims=False,
    ).reshape(group_count, share_len)
    seat_listed = lax.dynamic_slice(
        token_order.reshape(group_count, micro_count, team_size, piece_len),
        (target, 0, seat, 0),
        (1, micro_count, 1, piece_len),
    ).reshape(share_len)
    start = (group * team_size + member) * share_len
    token_pieces, back_pieces, send_map, take_map = run_deal(
        jnp.stack([start, group, target]).astype(jnp.int32),
        listed,
        seat_listed,
        tokens,
        cotangent,
        group_len,
    )

    def deal_pieces(pieces):
        return [swap(piece, perm) for piece, perm in zip(pieces, deal_perms)]

    def undeal(pieces, *waits):
        pieces = [
            after(swap(piece, turned(perm)), *waits)
            for piece, perm in zip(pieces, deal_perms)
        ]
        return run_pick(send_map, pieces, True)

    def exchange(v, axis_name):
        return swap(v, team_perms[axis_name])

    def sum_over(v, names):
        for name in names:
            v = v + exchange(v, name)
        return v

    def pack_taps(taps, bias):
        return jnp.concatenate(
            [taps, bias[None, :], jnp.zeros((3, bias.shape[0]), F32)], axis=0
        )

    heads_own = jnp.pad(jnp.stack([step_bias, decay_log, skip_gain]), ((0, 5), (0, 0)))
    lengths_own = jnp.pad(
        seq_lengths.astype(F32),
        ((0, 8 - micro_count), (0, width - seq_lengths.shape[1])),
    )
    local_params = jnp.concatenate(
        [
            pack_taps(conv_value, bias_value),
            jnp.broadcast_to(norm_gate[None, :], (8, width)),
            jnp.pad(heads_own, ((0, 0), (0, width - head_count))),
            jnp.pad(pack_taps(conv_pair, bias_pair), ((0, 0), (0, width - pair_part))),
            lengths_own,
        ],
        axis=0,
    )
    local_params = swap(after(local_params, *token_pieces), cross_perms[0])
    taps_value = local_params[:8]
    norm_gate_row = local_params[8:9]
    heads_got = local_params[16:24, :head_count]
    own_taps = local_params[24:32, :pair_part]
    live_ids = seq_lengths.shape[1] - 1
    bounds = jnp.cumsum(
        local_params[32 : 32 + micro_count, : live_ids + 1].astype(jnp.int32), axis=1
    )
    skip_row = jnp.repeat(heads_got[2:3], head_width, axis=1)
    heads_row = jnp.pad(
        jnp.concatenate([heads_got[0:1], -jnp.exp(heads_got[1:2])], axis=0),
        ((0, 6), (0, LANES - head_count)),
    )
    tap_high = lax.reduce_precision(own_taps, 8, 7)
    tap_mid = lax.reduce_precision(own_taps - tap_high, 8, 7)
    tap_low = own_taps - tap_high - tap_mid
    tap_row = jnp.stack([tap_high, tap_mid, tap_low]).astype(BF16).reshape(1, -1)
    tap_count = tap_row.shape[1]

    small_pad = -(pair_part + head_count) % 16
    small_own = jnp.concatenate(
        [w_pair.T, w_step.T, jnp.zeros((small_pad, w_pair.shape[0]), BF16)], axis=0
    )
    small_w = gather_groups(cross_groups(after(small_own, *token_pieces)), 1)

    pieces = deal_pieces(token_pieces)
    extra = jnp.concatenate(
        [
            small_w[:pair_part],
            jnp.pad(tap_row, ((0, 15), (0, width_full - tap_count))),
        ],
        axis=0,
    )
    dealt_tokens = run_pick(take_map, pieces, False, extra)
    full_rows = seat_view(lax.all_gather(dealt_tokens, TEAM, axis=0))
    value_w = cross_groups(after(w_value, *pieces))
    back_pieces = lax.optimization_barrier((*back_pieces, *value_w))[:group_count]
    pieces = deal_pieces(back_pieces)
    value_w = gather_groups(value_w, 0)
    dealt_back = run_pick(take_map, pieces, False)
    full_back = seat_view(lax.all_gather(dealt_back, TEAM, axis=0))
    later_w = cross_groups(after(jnp.stack([w_gate, w_out.T]), *pieces))
    full_rows, *later_w = lax.optimization_barrier((full_rows, *later_w))
    later_w = gather_groups(later_w, 1)
    gate_w, out_w = later_w[0], later_w[1]

    extra = full_rows[:, :, :, share_len:]
    pair_w = extra[:, :, :, :pair_part].reshape(pair_width, width_full)
    taps_got = extra[:, :, :, pair_part, :tap_count].astype(F32)
    taps_got = taps_got.reshape(team_size, 3, 8, pair_part)
    taps_got = taps_got[:, 0] + (taps_got[:, 1] + taps_got[:, 2])
    taps_pair = jnp.swapaxes(taps_got, 0, 1).reshape(8, pair_width)
    step_w = jnp.pad(
        small_w[pair_part : pair_part + head_count], ((0, LANES - head_count), (0, 0))
    )
    small_w = jnp.concatenate([pair_w, step_w], axis=0)

    consts = head_constants(head_count, head_width)
    weights = (
        norm_in[None, :],
        value_w,
        gate_w,
        small_w,
        taps_value,
        taps_pair,
        heads_row,
        skip_row,
    )
    outs = run_forward(bounds, full_rows, weights, consts, micro_count, piece_len)
    normed, value, conv_v, pair, conv_p, step, scanned, states = outs
    flat = micro_count * block_len
    gate, scaled, grad_normed, stats = run_back(
        bounds, full_back, normed, gate_w, out_w, norm_gate_row, scanned, live_ids, micro_count, piece_len
    )
    partial_out = dot_nt(scaled.reshape(flat, width), out_w).astype(BF16)
    branch = lax.psum_scatter(partial_out, TEAM, scatter_dimension=0, tiled=True)
    stats = sum_over(stats, ("core", "near", "row"))
    low_gate, normed_out, grad_scanned, gate_sums = run_gate(
        bounds, stats, grad_normed, gate, scanned, norm_gate_row, live_ids, inner_full, micro_count, piece_len
    )
    kept = (normed, value, conv_v, pair, conv_p, step, scanned, states)
    g_out = dot_tn(full_back.reshape(flat, width_full), normed_out.reshape(flat, width))
    g_gate = dot_tn(normed, low_gate)
    g_out, g_gate, grad_scanned = lax.optimization_barrier(
        (g_out.astype(BF16), g_gate.astype(BF16), grad_scanned)
    )
    flagged = jnp.concatenate(
        [bounds, jnp.full((1, bounds.shape[1]), my_core, jnp.int32)], axis=0
    )
    live_start = seat * piece_len
    local_stats = lax.dynamic_slice_in_dim(
        stats[0].reshape(micro_count, block_len), live_start, piece_len, 1
    )
    local_places = live_start + jnp.arange(piece_len, dtype=jnp.int32)
    local_seg = jnp.sum(
        (local_places[None, :, None] >= bounds[:, None, :]).astype(jnp.int32), axis=2
    )
    weight = jnp.where(
        local_seg < live_ids, lax.rsqrt(local_stats / inner_full + EPS), 0.0
    ).reshape(share_len, 1)
    bits = jnp.stack([my_near, my_row]).astype(jnp.int32)
    held = []
    all_sums = []
    earlier = None
    crossed = ()
    early = [item.reshape(group_count, -1, width) for item in (g_out, g_gate)]
    for micro in range(micro_count):
        if micro == micro_count - 1 and micro:
            crossed, finish_early, (low_value, low_small, bits, weight, *all_sums[0]) = scatter_groups(
                early, waits=earlier, bound=(*earlier, bits, weight, *all_sums[0])
            )
            earlier = (low_value, low_small)
        low_value, low_small, keep, send, sums, sums_in = run_backward(
            flagged, grad_scanned, low_gate, kept, weights, consts, micro, piece_len, earlier, True
        )
        earlier = (low_value, low_small)
        if crossed:
            send, *crossed = lax.optimization_barrier((send, *crossed))
        held += [keep, exchange(send, "core")]
        all_sums.append([sums, sums_in])
    first_axes = tuple((1 - micro % 2, micro % 2) for micro in range(micro_count))
    next_axes = tuple((0, 1 - micro % 2) for micro in range(micro_count))

    def cross_sides(held, axes):
        names = ("near", "row")
        return [
            item if k % 2 == 0 else exchange(item, names[axes[k // 2][1]])
            for k, item in enumerate(held)
        ]

    held = run_halves(first_axes, bits, *held)
    low_value, low_small, all_sums, *held = lax.optimization_barrier(
        (low_value, low_small, all_sums, *held)
    )
    held = cross_sides(held, first_axes)
    g_value = dot_tn(normed, low_value).astype(BF16)
    opened = open_scatter(g_value.reshape(group_count, -1, width))
    g_small = dot_tn(low_small, normed)
    opened, g_small, held = lax.optimization_barrier((opened, g_small, held))
    held = run_halves(next_axes, bits, *held)
    branch, held = lax.optimization_barrier((branch, held))
    grad_ins = cross_sides(held, next_axes)
    sums = reduce(jnp.add, [item[0] for item in all_sums])
    sums_in = reduce(jnp.add, [item[1] for item in all_sums])[0:1]
    pair_sums = sums[8:13, :pair_width].reshape(1, -1)
    pair_sums = jnp.pad(pair_sums, ((0, 0), (0, -pair_sums.shape[1] % width_full)))
    team_rows = jnp.concatenate(
        [sums_in, pair_sums.reshape(-1, width_full)], axis=0
    )

    def split_rows(v, axis=0):
        high = lax.reduce_precision(v, 8, 7)
        both = jnp.concatenate([high, v - high], axis=0).astype(BF16)
        return jnp.pad(both, ((0, -both.shape[0] % 16), (0, 0)))

    def join_rows(v, count):
        return v[:count].astype(F32) + v[count : 2 * count].astype(F32)

    g_pair = g_small[:pair_width].reshape(sizes[2], sizes[4], 2, pair_part, width_full)

    def pair_stage(g_pair, team_rows, name, bit, axis, *waits):
        keep = lax.dynamic_index_in_dim(g_pair, bit, axis, keepdims=False)
        send = lax.dynamic_index_in_dim(g_pair, 1 - bit, axis, keepdims=False)
        count = send.size // width_full
        packed = jnp.concatenate(
            [send.astype(BF16).reshape(count, width_full), split_rows(team_rows)], axis=0
        )
        packed = after(exchange(packed, name), *waits)
        return (
            keep + packed[:count].reshape(keep.shape).astype(F32),
            team_rows + join_rows(packed[count:], team_rows.shape[0]),
        )

    g_pair, team_rows = pair_stage(g_pair, team_rows, "core", my_core, 2, *held)
    g_pair, team_rows = pair_stage(g_pair, team_rows, "near", my_near, 1)
    g_pair, team_rows, grad_ins, crossed = lax.optimization_barrier(
        (g_pair, team_rows, grad_ins, crossed)
    )
    send_back = run_close(
        partial(close_back_kernel, micro_count),
        group_count,
        take_map,
        dealt_tokens,
        dealt_back,
        norm_in[None, :],
        *grad_ins,
    )
    crossed = lax.optimization_barrier((crossed, send_back))[0]
    (g_out, g_gate), _ = finish_early(*crossed)
    g_out = g_out.T
    branch, send_back = lax.optimization_barrier((branch, send_back))
    send_out = run_close(
        close_out_kernel, group_count, take_map, dealt_tokens, branch, weight
    )
    out_pieces = [swap(piece, turned(perm)) for piece, perm in zip(send_out, deal_perms)]
    g_pair, team_rows = pair_stage(g_pair, team_rows, "row", my_row, 0, *send_back)
    g_small = jnp.concatenate(
        [
            g_pair,
            g_small[pair_width : pair_width + head_count],
            jnp.zeros((small_pad, width_full), F32),
        ],
        axis=0,
    )
    sums = jnp.concatenate(
        [sums[:5], gate_sums[0:1], sums[6:8], team_rows.reshape(-1, width)], axis=0
    )
    small_rows = g_small.shape[0]
    value_rows = width_full // group_count
    late = jnp.swapaxes(g_small.reshape(small_rows, group_count, -1), 0, 1)
    if value_rows != width:
        late = jnp.pad(late, ((0, 0), (0, 0), (0, width - value_rows)))
    crossed, finish, _ = scatter_groups([late], sums, split_rows, join_rows, waits=send_back)
    (late,), sums = finish(*crossed)
    crossed, finish, _ = scatter_groups([g_value], waits=send_back, opened=opened)
    (g_value,), _ = finish(*crossed)
    g_small = late[:, :value_rows]
    g_pair = g_small[:pair_part].T
    g_step = g_small[pair_part : pair_part + head_count].T
    pair_sums = sums[8 + width_full // width :].reshape(-1)[: 5 * pair_width]
    pair_sums = pair_sums.reshape(5, pair_width)
    in_sums = sums[8 : 8 + width_full // width]
    own_place = (my_row * sizes[4] + my_near) * sizes[3] + my_half
    pair_sums = lax.dynamic_slice_in_dim(pair_sums, own_place * pair_part, pair_part, 1)
    g_norm_in = in_sums.reshape(-1) / norm_in.astype(F32)
    g_skip = jnp.sum(sums[6].reshape(head_count, head_width), axis=1)

    block_out = run_pick(send_map, out_pieces, True)
    grad_tokens = undeal(send_back)
    return (
        block_out,
        grad_tokens,
        g_norm_in,
        g_gate,
        g_value,
        g_pair,
        g_step,
        sums[0:4],
        sums[4],
        pair_sums[0:4],
        pair_sums[4],
        sums[7, :head_count],
        sums[7, LANES : LANES + head_count],
        g_skip,
        sums[5],
        g_out,
    )


def solution(mesh):
    shape = mesh.devices.shape
    sizes = (shape[0] // 2, 2, shape[1], 2, shape[2] // 2)
    fine = jax.sharding.Mesh(mesh.devices.reshape(sizes), ALL)
    dp, team = ("pair", "core"), ("row", "half", "near")
    everything = ("pair", "core", "row", "half", "near")
    placed = (
        P(everything, None),
        P(everything, None),
        P(dp, None),
        P(),
        P(),
        P(dp, team),
        P(dp, team),
        P(dp, team),
        P(dp, team),
        P(None, team),
        P(team),
        P(None, team),
        P(team),
        P(team),
        P(team),
        P(team),
        P(team),
        P(team, dp),
    )
    return jax.shard_map(
        partial(per_device, sizes),
        mesh=fine,
        in_specs=placed,
        out_specs=(
            P(everything, None),
            P(everything, None),
            P(),
            P(dp, team),
            P(dp, team),
            P(dp, team),
            P(dp, team),
            P(None, team),
            P(team),
            P(None, team),
            P(team),
            P(team),
            P(team),
            P(team),
            P(team),
            P(team, dp),
        ),
        check_vma=False,
    )
```
